32 devices in a mesh: tm: 8 (over y, x, core), dp: 4 (over z).
Axes of the slice: x: 2, y: 2, z: 4, core: 2. Of those that a mesh axis runs over, the one named last changes fastest.
Arguments:
- frames_in: bfloat16 [4, 1024, 1024], P('dp', 'tm'), may hold values from -6 to 6
- valid_frames: int32 [4], P('dp'), may hold values from 512 to 1024, as said below
- kernel: float32 [9, 1024], replicated, may hold values from -2 to 2
- w_qkv: bfloat16 [1024, 3072], replicated, may hold values from -0.1875 to 0.1875
- cotangent: bfloat16 [4, 1024, 1024], P('dp', 'tm'), may hold values from -6 to 6
Outputs:
- attended: bfloat16 [4, 1024, 1024], P('dp', 'tm')
- grad_in: bfloat16 [4, 1024, 1024], P('dp', 'tm')
- qkv_grad: float32 [24, 128, 1024], P('dp', None, 'tm')
The draws below stay inside these ranges and needn't reach their ends.
Inputs may be any that keep to these rules, and one draw needn't show every extreme that they name: `valid_frames`: valid frames of each recording, counted from its start; some recording has all 1024 and some exactly 512.
All inputs are finite; a program needn't handle non-finite values.
Results may differ from the reference program's by a relative error of at most 0.025.
Values may be sent and summed in bfloat16 or wider, within the bound.
No kernel may reach another device: no remote copies, remote signals or barrier semaphores. Data moves between devices by JAX's collectives and lax.ppermute only.
A program may use at most 64 MiB of HBM per device.

```python
import jax
import jax.numpy as jnp
from jax import lax

D = 1024
HEADS = 8
HEAD = 128
KERNEL = 9
LEFT = 70
F_DEV = 128
FRAMES = 1024
RECS = 4


def draw_valid_frames(key, part):
    first, second = jax.random.split(jax.random.fold_in(key, 11))
    counts = jax.random.randint(first, (RECS,), FRAMES // 2, FRAMES + 1)
    order = jax.random.permutation(second, RECS)
    places = jnp.arange(RECS)
    counts = jnp.where(places == order[0], FRAMES, counts)
    counts = jnp.where(places == order[1], FRAMES // 2, counts)
    return counts.astype(jnp.int32)


def strengthened(array, stream_key, source, target, parts, factor):
    owner, partner = [(jnp.arange(array.shape[axis_at]) // (array.shape[axis_at] // parts)).reshape([-1 if axis == axis_at else 1 for axis in range(array.ndim)]) for axis_at in (source, target)]
    chosen = jax.random.permutation(stream_key, parts)[partner]
    strong = (owner == chosen) | (owner == (partner + parts // 2) % parts)
    return jnp.where(strong, factor * array, array)


def steps_of(key, dims, cuts, smallest, high):
    loudness = 1.0
    for dim, shards_of in cuts:
        heights = jax.random.uniform(jax.random.fold_in(jax.random.fold_in(key, 6), dim), (shards_of,), jnp.float32, smallest / len(cuts), high / len(cuts))
        loudness = loudness * jnp.repeat(jnp.exp(heights), dims[dim] // shards_of).reshape((-1,) + (1,) * (len(dims) - 1 - dim))
    return loudness


def noise(key, dims, scale, bound, cuts=(), kind=jnp.bfloat16):
    gain = steps_of(key, dims, cuts, -0.22, 0.18) if cuts else 1.0
    drawn = jax.random.normal(key, dims, jnp.float32) * scale * gain
    return jnp.minimum(jnp.maximum(drawn, -bound), bound).astype(kind)


def heavy_noise(rng, shape, width, bound, pieces, heavy, held_as=jnp.bfloat16):
    array = width * jax.random.normal(rng, shape, jnp.float32)
    if pieces:
        array = array * steps_of(rng, shape, pieces, -0.22, 0.18)
    return jnp.clip(strengthened(array, jax.random.fold_in(rng, 3), *heavy), -bound, bound).astype(held_as)


def setup_inputs(seed: int = 0) -> dict:
    splits = jax.random.split(jax.random.key(seed), 6)
    frames_in = heavy_noise(splits[0], (RECS, FRAMES, D), 1.0, 6.0, ((0, 4), (1, 8)), (1, 2, 8, 2.0))
    valid_frames = draw_valid_frames(jax.random.fold_in(splits[5], 71), 0)
    kernel = noise(splits[2], (KERNEL, D), KERNEL ** -0.5, 2.0, (), jnp.float32)
    w_qkv = noise(splits[3], (D, 3 * D), D ** -0.5, 0.1875)
    cotangent = noise(splits[4], (RECS, FRAMES, D), 1.0, 6.0, ((0, 4), (1, 8)))
    return {"frames_in": frames_in, "valid_frames": valid_frames, "kernel": kernel, "w_qkv": w_qkv, "cotangent": cotangent}


def conv_rows(extended, taps, count):
    total = jnp.zeros((count, extended.shape[1]), jnp.float32)
    for offset in range(KERNEL):
        total = total + taps[offset] * extended[offset:offset + count]
    return total


def band_pass(queries, keys_ext, vals_ext, grad_out, query_pos, key_pos, count):
    factor = HEAD ** -0.5
    offset = query_pos[:, None] - key_pos[None, :]
    allowed = (offset >= 0) & (offset <= LEFT) & (key_pos[None, :] >= 0) & (key_pos[None, :] < count) & (query_pos[:, None] < count)
    q_heads = queries.astype(jnp.float32).reshape(-1, HEADS, HEAD)
    k_heads = keys_ext.astype(jnp.float32).reshape(-1, HEADS, HEAD)
    v_heads = vals_ext.astype(jnp.float32).reshape(-1, HEADS, HEAD)
    g_heads = grad_out.astype(jnp.float32).reshape(-1, HEADS, HEAD)
    scores = jnp.einsum("fhe,ghe->hfg", q_heads, k_heads) * factor
    raised = jnp.where(allowed[None], jnp.exp(scores), 0.0)
    missing = 1.0 - (query_pos < count).astype(jnp.float32)
    prob = raised / (jnp.sum(raised, axis=-1, keepdims=True) + missing[None, :, None])
    prob_low = prob.astype(jnp.bfloat16)
    attended = jnp.einsum("hfg,ghe->fhe", prob_low.astype(jnp.float32), v_heads)
    attended = attended.reshape(queries.shape).astype(jnp.bfloat16)
    grad_prob = jnp.einsum("fhe,ghe->hfg", g_heads, v_heads)
    grad_score = (prob * (grad_prob - jnp.sum(prob * grad_prob, axis=-1, keepdims=True)) * factor).astype(jnp.bfloat16)
    grad_query = jnp.einsum("hfg,ghe->fhe", grad_score.astype(jnp.float32), k_heads).reshape(queries.shape)
    grad_key = jnp.einsum("hfg,fhe->ghe", grad_score.astype(jnp.float32), q_heads).reshape(keys_ext.shape)
    grad_value = jnp.einsum("hfg,fhe->ghe", prob_low.astype(jnp.float32), g_heads).reshape(vals_ext.shape)
    return attended, grad_query, grad_key, grad_value


def reference(frames_in, valid_frames, kernel, w_qkv, cotangent):
    blocks = FRAMES // F_DEV
    factor = float(RECS * FRAMES) ** -0.5

    def one_recording(total, item):
        record, count, cot_rec = item
        positions = jnp.arange(FRAMES, dtype=jnp.int32)
        live = (positions < count)[:, None]
        masked = jnp.where(live, record, jnp.zeros_like(record))
        padded = jnp.concatenate([jnp.zeros((KERNEL - 1, D), jnp.float32), masked.astype(jnp.float32)], axis=0)
        conv = conv_rows(padded, kernel, FRAMES)
        hidden = (masked.astype(jnp.float32) + jax.nn.silu(conv)).astype(jnp.bfloat16)
        qkv = jnp.dot(hidden, w_qkv, preferred_element_type=jnp.float32).astype(jnp.bfloat16)
        grad_out = jnp.where(live, cot_rec, jnp.zeros_like(cot_rec))
        kv_pad = jnp.concatenate([jnp.zeros((LEFT, 2 * D), jnp.bfloat16), qkv[:, D:]], axis=0)

        def one_block(index):
            begin = index * F_DEV
            queries = lax.dynamic_slice_in_dim(qkv[:, :D], begin, F_DEV, 0)
            pairs = lax.dynamic_slice_in_dim(kv_pad, begin, F_DEV + LEFT, 0)
            grads = lax.dynamic_slice_in_dim(grad_out, begin, F_DEV, 0)
            query_pos = begin + jnp.arange(F_DEV, dtype=jnp.int32)
            key_pos = begin - LEFT + jnp.arange(F_DEV + LEFT, dtype=jnp.int32)
            return band_pass(queries, pairs[:, :D], pairs[:, D:], grads, query_pos, key_pos, count)

        attended, grad_query, grad_key, grad_value = lax.map(one_block, jnp.arange(blocks, dtype=jnp.int32))
        zero_rim = jnp.zeros((1, LEFT, D), jnp.float32)
        later_key = jnp.concatenate([grad_key[1:, :LEFT], zero_rim], axis=0)
        later_value = jnp.concatenate([grad_value[1:, :LEFT], zero_rim], axis=0)
        own_key = grad_key[:, LEFT:]
        own_value = grad_value[:, LEFT:]
        own_key = jnp.concatenate([own_key[:, :F_DEV - LEFT], own_key[:, F_DEV - LEFT:] + later_key], axis=1)
        own_value = jnp.concatenate([own_value[:, :F_DEV - LEFT], own_value[:, F_DEV - LEFT:] + later_value], axis=1)
        grad_qkv = jnp.concatenate([grad_query, own_key, own_value], axis=-1).reshape(FRAMES, 3 * D).astype(jnp.bfloat16)
        grad_hidden = lax.dot_general(grad_qkv, w_qkv, (((1,), (1,)), ((), ())), preferred_element_type=jnp.float32)
        logistic = jax.nn.sigmoid(conv)
        grad_conv = grad_hidden * logistic * (1.0 + conv * (1.0 - logistic))
        tail = jnp.concatenate([grad_conv, jnp.zeros((KERNEL - 1, D), jnp.float32)], axis=0)
        spread = conv_rows(tail, kernel[::-1], FRAMES)
        grad_in = jnp.where(live, grad_hidden + spread, 0.0).astype(jnp.bfloat16)
        hidden_blocks = hidden.reshape(blocks, F_DEV, D)
        grad_blocks = grad_qkv.reshape(blocks, F_DEV, 3 * D)

        def add_block(running, pair):
            term = lax.dot_general(pair[0], pair[1], (((0,), (0,)), ((), ())), preferred_element_type=jnp.float32)
            rounded = lax.optimization_barrier(term.astype(jnp.bfloat16))
            return running + rounded.astype(jnp.float32), None

        total, _ = lax.scan(add_block, total, (hidden_blocks, grad_blocks))
        return total, (attended.reshape(FRAMES, D), grad_in)

    start = jnp.zeros((D, 3 * D), jnp.float32)
    total, outputs = lax.scan(one_recording, start, (frames_in, valid_frames, cotangent))
    qkv_grad = (total * factor).reshape(D, 3 * HEADS, HEAD).transpose(1, 2, 0)
    return outputs[0], outputs[1], qkv_grad
```

```python
import functools

import jax
import jax.numpy as jnp
from jax import lax
from jax.experimental import pallas as pl
from jax.experimental.pallas import tpu as pltpu
from jax.sharding import PartitionSpec as P

HEADS = 8
HEAD = 128
KERNEL = 9
LEFT = 70
HALO = 80
EDGE = 16
MIB = 1024 * 1024
F32 = jnp.float32
BF16 = jnp.bfloat16


def params(mib):
    return pltpu.CompilerParams(vmem_limit_bytes=mib * MIB)


def vmem(count):
    return [pl.BlockSpec(memory_space=pltpu.VMEM)] * count


def cost(flops, moved):
    return pl.CostEstimate(flops=flops, bytes_accessed=moved, transcendentals=0)


def dot(a, b, left, right):
    return lax.dot_general(a, b, (((left,), (right,)), ((), ())), preferred_element_type=F32)


def project_kernel(place, prev, own, after, taps, w, hidden_out, conv_out, qkv, ext, hidden):
    frames, width = own.shape
    rows = frames + 2 * HALO
    begin, count = place[0], place[1]
    position = begin - HALO + lax.broadcasted_iota(jnp.int32, (rows, 128), 0)
    live = position < count
    for col in range(0, width, 128):
        cols = pl.ds(col, 128)
        raw = jnp.concatenate([prev[:, cols], own[:, cols], after[:HALO, cols]], axis=0)
        masked = jnp.where(live, raw.astype(F32), 0.0)
        ext[: KERNEL - 1, cols] = jnp.zeros((KERNEL - 1, 128), F32)
        ext[KERNEL - 1 :, cols] = masked
        conv = taps[0:1, cols] * ext[0:rows, cols]
        for tap in range(1, KERNEL):
            conv = conv + taps[tap : tap + 1, cols] * ext[tap : tap + rows, cols]
        conv_out[:, cols] = conv[HALO : HALO + frames + EDGE]
        hidden[:, cols] = (masked + conv / (1.0 + jnp.exp(-conv))).astype(BF16)
    hidden_out[...] = hidden[HALO : HALO + frames]
    for col in range(0, 3 * width, 512):
        cols = pl.ds(col, 512)
        low = HALO if col < width else 0
        qkv[low:rows, cols] = dot(hidden[low:], w[:, cols], 1, 0).astype(BF16)
    qkv[rows:, :] = jnp.zeros((qkv.shape[0] - rows, 3 * width), BF16)


def attend_kernel(place, qkv, cot, after, attended, grads, sends, later):
    frames, width = cot.shape
    span = frames + HALO
    begin, count, chip = place[0], place[1], place[2]

    def mask(shift, wanted):
        key = lax.broadcasted_iota(jnp.int32, (span, frames), 0)
        query = lax.broadcasted_iota(jnp.int32, (span, frames), 1)
        first = begin if shift else begin + frames
        gap = query + (HALO if shift else frames) - key
        seen = first + query - gap
        alive = (first + query < count) & (query < wanted)
        allowed = (gap >= 0) & (gap <= LEFT) & (seen >= 0) & alive
        return allowed, jnp.where(alive[:1], 0.0, 1.0)

    masks = [mask(True, frames), mask(False, HALO)]
    row = lax.broadcasted_iota(jnp.int32, (frames, width), 0)
    later[:HALO] = jnp.where(
        begin + frames + row[:HALO] < count, after[HALO:], jnp.zeros((HALO, width), BF16)
    )
    later[HALO:] = jnp.zeros((frames - HALO, width), BF16)
    factor = HEAD**-0.5

    def band(query, key, value, grad, allowed, missing):
        raised = jnp.where(allowed, jnp.exp(dot(key, query, 1, 1) * factor), 0.0)
        prob = raised * (1.0 / (jnp.sum(raised, axis=0, keepdims=True) + missing))
        grad_prob = dot(value, grad, 1, 1)
        mean = jnp.sum(prob * grad_prob, axis=0, keepdims=True)
        return prob.astype(BF16), (prob * (grad_prob - mean) * factor).astype(BF16)

    own_live = begin + lax.broadcasted_iota(jnp.int32, (frames, HEAD), 0) < count
    for head in range(HEADS):
        q_cols = pl.ds(head * HEAD, HEAD)
        k_cols = pl.ds(width + head * HEAD, HEAD)
        v_cols = pl.ds(2 * width + head * HEAD, HEAD)
        query = qkv[HALO : HALO + frames, q_cols]
        query_b = qkv[HALO + frames : HALO + 2 * frames, q_cols]
        key = qkv[: HALO + span, k_cols]
        value = qkv[: HALO + span, v_cols]
        grad = jnp.where(own_live, cot[:, q_cols], jnp.zeros((frames, HEAD), BF16))
        grad_b = later[:, q_cols]
        prob, score = band(query, key[:span], value[:span], grad, *masks[0])
        prob_b, score_b = band(query_b, key[HALO:], value[HALO:], grad_b, *masks[1])
        attended[:, q_cols] = dot(prob, value[:span], 0, 0).astype(BF16)
        grads[:frames, q_cols] = dot(score, key[:span], 0, 0).astype(BF16)
        grads[frames:, q_cols] = dot(score_b, key[HALO:], 0, 0)[:EDGE].astype(BF16)
        for cols, mine, here, theirs, there in (
            (k_cols, score, query, score_b, query_b),
            (v_cols, prob, grad, prob_b, grad_b),
        ):
            total = dot(theirs[: frames + EDGE], there, 1, 0)
            grads[:frames, cols] = (total[:frames] + dot(mine[HALO:], here, 1, 0)).astype(BF16)
            grads[frames:, cols] = total[frames:].astype(BF16)
    if sends is None:
        return
    for k in range(4):
        slot = chip ^ k
        for i in range(4):
            block = 6 * i + k + (k + 1) // 2
            sends[slot, :, i * HEAD : (i + 1) * HEAD] = grads[:frames, pl.ds(block * HEAD, HEAD)]
        side = (k % 2) * (HEAD // 2)
        for pair in range(2):
            halves = []
            for i in (2 * pair, 2 * pair + 1):
                start = (6 * i + 1 + 3 * (k // 2)) * HEAD + side
                halves.append(grads[:frames, start : start + HEAD // 2])
            at = (4 + pair) * HEAD
            sends[slot, :, at : at + HEAD] = jnp.concatenate(halves, axis=1)


def attend_alone(place, qkv, cot, after, attended, grads, later):
    attend_kernel(place, qkv, cot, after, attended, grads, None, later)


def input_grad_kernel(place, grads, w, conv, taps, grad_in, slopes):
    frames, width = grad_in.shape
    begin, count = place[0], place[1]
    live = begin + lax.broadcasted_iota(jnp.int32, (frames, 256), 0) < count
    for col in range(0, width, 256):
        cols = pl.ds(col, 256)
        grad_hidden = dot(grads[...], w[cols, :], 1, 1)
        value = conv[:, cols]
        logistic = 1.0 / (1.0 + jnp.exp(-value))
        slopes[:, cols] = grad_hidden * (logistic * (1.0 + value * (1.0 - logistic)))
        total = grad_hidden[:frames]
        for tap in range(KERNEL):
            low = KERNEL - 1 - tap
            total = total + taps[tap : tap + 1, cols] * slopes[low : low + frames, cols]
        grad_in[:, cols] = jnp.where(live, total, 0.0).astype(BF16)


def weight_kernel(place, a0, a1, a2, a3, b, b1, b2, b3, send, keep):
    core = place[3]
    left = jnp.concatenate([b[0], b1[...], b2[...], b3[...]], axis=0)
    for k in range(4):
        for out, parity in ((send, 1 - core), (keep, core)):
            cols = pl.ds(pl.multiple_of((2 * k + parity) * HEAD, HEAD), HEAD)
            right = jnp.concatenate([a[:, cols] for a in (a0, a1, a2, a3)], axis=0)
            out[:, k * HEAD : (k + 1) * HEAD] = dot(left, right, 0, 0).astype(out.dtype)


def core_sum_kernel(place, keep, got, own, sends):
    me = place[4]
    whole, half = HEAD, HEAD // 2
    for i in range(4):
        one = keep[i * whole : (i + 1) * whole] + got[i * whole : (i + 1) * whole].astype(F32)
        rows = pl.ds(4 * whole + i * half, half)
        two = keep[rows] + got[rows].astype(F32)
        sends[i ^ me, :whole] = one.astype(BF16)
        sends[i ^ me, whole:] = two.astype(BF16)

        @pl.when(i == me)
        def _():
            own[:whole] = one
            own[whole:] = two


def part_sum_kernel(place, own, g1, g2, g3, sends):
    chip = place[2]
    for k in range(4):
        cols = pl.ds(k * HEAD, HEAD)
        total = own[:, cols] + g1[:, cols].astype(F32)
        total = total + (g2[:, cols].astype(F32) + g3[:, cols].astype(F32))
        sends[k ^ chip] = total.astype(BF16)


def place_kernel(scale, place, own, g1, g2, g3, out):
    chip = place[2]
    for slot, ref in enumerate((own.at[0], g1, g2, g3)):
        k = chip ^ slot
        value = ref[...].astype(F32) * scale
        out[k + (k + 1) // 2] = value[:HEAD]
        start = pl.multiple_of((k % 2) * (HEAD // 2), HEAD // 2)
        out[1 + 3 * (k // 2), pl.ds(start, HEAD // 2)] = value[HEAD:]


def call(kernel, name, outs, place, operands, scratch=(), mib=16, flops=1000000, moved=1000000):
    return pl.pallas_call(
        kernel,
        name=name,
        out_shape=[jax.ShapeDtypeStruct(shape, dtype) for shape, dtype in outs],
        in_specs=[pl.BlockSpec(memory_space=pltpu.SMEM)] + vmem(len(operands)),
        out_specs=vmem(len(outs)),
        scratch_shapes=[pltpu.VMEM(shape, dtype) for shape, dtype in scratch],
        compiler_params=params(mib),
        cost_estimate=cost(flops, moved),
    )(place, *operands)


def shift(value, axis, steps):
    count = lax.axis_size(axis)
    pairs = [(i, i + steps) for i in range(count) if 0 <= i + steps < count]
    return lax.ppermute(value, axis, pairs)


def swap(value, axis, mask):
    return lax.ppermute(value, axis, [(i, i ^ mask) for i in range(lax.axis_size(axis))])


def on_device(frames_in, valid_frames, kernel, w_qkv, cotangent):
    record, cot = frames_in[0], cotangent[0]
    frames, width = record.shape
    span = frames + HALO
    parts, recs = lax.axis_size("tm"), lax.axis_size("dp")
    me = lax.axis_index("tm")
    place = jnp.stack(
        [me * frames, valid_frames[0], me // 2, me % 2, lax.axis_index("dp")]
    ).astype(jnp.int32)
    before = shift(record[frames - HALO :], "tm", 1)
    after = shift(jnp.concatenate([record[:HALO], cot[:HALO]], axis=0), "tm", -1)
    rows = span + HALO
    hidden, conv, qkv = call(
        project_kernel,
        "project",
        [
            ((frames, width), BF16),
            ((frames + EDGE, width), F32),
            ((HALO + 2 * frames, 3 * width), BF16),
        ],
        place,
        [before, record, after, kernel, w_qkv],
        [((rows + KERNEL - 1, width), F32), ((rows, width), BF16)],
        mib=24,
        flops=rows * width * 3 * width * 2,
        moved=9000000,
    )
    split = parts == 8 and recs == 4
    if split:
        peers = [swap(hidden, "tm", mask) for mask in (2, 4, 6)]
    outs = [((frames, width), BF16), ((frames + EDGE, 3 * width), BF16)]
    attended, grads, *sends = call(
        attend_kernel if split else attend_alone,
        "attend",
        outs + [((4, frames, 3 * width // 4), BF16)] * split,
        place,
        [qkv, cot, after],
        [((frames, width), BF16)],
        mib=16,
        flops=8 * 12 * span * 128 * 128 * 2 * 8,
        moved=5000000,
    )
    if split:
        sends = sends[0]
        got = [swap(sends[slot], "tm", 2 * slot) for slot in (1, 2, 3)]
    (grad_in,) = call(
        input_grad_kernel,
        "input_grad",
        [((frames, width), BF16)],
        place,
        [grads, w_qkv, conv, kernel],
        [((frames + EDGE, width), F32)],
        mib=20,
        flops=(frames + EDGE) * width * 3 * width * 2,
        moved=9000000,
    )
    scale = float(recs * parts * frames) ** (-0.5)
    if split:
        cols = 3 * width // 4
        shard = cols // 4
        send, keep = call(
            weight_kernel,
            "weight_grad",
            [((cols, width // 2), BF16), ((cols, width // 2), F32)],
            place,
            [hidden, *peers, sends, *got],
            mib=20,
            flops=cols * width * frames * 8,
            moved=6000000,
        )
        sibling = swap(send, "tm", 1)
        own, shards = call(
            core_sum_kernel,
            "core_sum",
            [((shard, width // 2), F32), ((4, shard, width // 2), BF16)],
            place,
            [keep, sibling],
        )
        others = [swap(shards[mask], "dp", mask) for mask in (1, 2, 3)]
        (blocks,) = call(
            part_sum_kernel,
            "part_sum",
            [((4, shard, HEAD), BF16)],
            place,
            [own, *others],
        )
        last = [swap(blocks[slot], "tm", 2 * slot) for slot in (1, 2, 3)]
        (qkv_grad,) = call(
            functools.partial(place_kernel, scale),
            "place",
            [((3 * HEADS // 4, HEAD, HEAD), F32)],
            place,
            [blocks, *last],
        )
    else:
        partial = dot(hidden, grads[:frames], 0, 0).astype(BF16)
        by_time = lax.psum_scatter(partial, "tm", scatter_dimension=0, tiled=True)
        summed = lax.psum_scatter(by_time, "dp", scatter_dimension=1, tiled=True).astype(F32)
        qkv_grad = summed.reshape(summed.shape[0], -1, HEAD).transpose(1, 2, 0) * scale
    return (attended[None], grad_in[None], qkv_grad)


def solution(mesh):
    return jax.shard_map(
        on_device,
        mesh=mesh,
        in_specs=(P("dp", "tm", None), P("dp"), P(), P(), P("dp", "tm", None)),
        out_specs=(P("dp", "tm", None), P("dp", "tm", None), P("dp", None, "tm")),
        check_vma=False,
    )
```

```python
import functools

import jax
import jax.numpy as jnp
from jax import lax
from jax.experimental import pallas as pl
from jax.experimental.pallas import tpu as pltpu
from jax.sharding import PartitionSpec as P

HEADS = 8
HEAD = 128
KERNEL = 9
LEFT = 70
HALO = 80
EDGE = 16
MIB = 1024 * 1024
F32 = jnp.float32
BF16 = jnp.bfloat16


def params(mib):
    return pltpu.CompilerParams(vmem_limit_bytes=mib * MIB)


def vmem(count):
    return [pl.BlockSpec(memory_space=pltpu.VMEM)] * count


def cost(flops, moved):
    return pl.CostEstimate(flops=flops, bytes_accessed=moved, transcendentals=0)


def dot(a, b, left, right):
    return lax.dot_general(a, b, (((left,), (right,)), ((), ())), preferred_element_type=F32)


def conv_hidden(ext, taps, cols, low, rows, masked):
    conv = taps[0:1, cols] * ext[low : low + rows, cols]
    for tap in range(1, KERNEL):
        conv = conv + taps[tap : tap + 1, cols] * ext[low + tap : low + tap + rows, cols]
    return conv, (masked + conv / (1.0 + jnp.exp(-conv))).astype(BF16)


def live_rows(first, rows, count):
    return first + lax.broadcasted_iota(jnp.int32, (rows, 128), 0) < count


def own_kernel(
    place, far_own, far_taps, w, hidden, conv_out, qkv, own, taps, w_out, ext, sems, small
):
    frames, width = own.shape
    rows = frames - EDGE
    arrivals = [
        pltpu.make_async_copy(source, target, small.at[i])
        for i, (source, target) in enumerate(((far_own, own), (far_taps, taps)))
    ]
    for copy in arrivals:
        copy.start()
    copies = [
        pltpu.make_async_copy(w.at[:, pl.ds(col, 512)], w_out.at[:, pl.ds(col, 512)], sems.at[i])
        for i, col in enumerate(range(0, 3 * width, 512))
    ]
    for copy in copies:
        copy.start()
    for copy in arrivals:
        copy.wait()
    live = live_rows(place[0], frames, place[1])
    for col in range(0, width, 128):
        cols = pl.ds(col, 128)
        masked = jnp.where(live, own[:, cols].astype(F32), 0.0)
        ext[:, cols] = masked
        conv, low = conv_hidden(ext, taps, cols, EDGE - KERNEL + 1, rows, masked[EDGE:])
        conv_out[:, cols] = conv
        hidden[:, cols] = low
    for i, copy in enumerate(copies):
        copy.wait()
        cols = pl.ds(i * 512, 512)
        qkv[:, cols] = dot(hidden[...], w_out[:, cols], 1, 0).astype(BF16)


def rim_kernel(place, prev, own, after, taps, w, first, conv_out, qkv, ext, hidden):
    frames, width = own.shape
    begin, count = place[0], place[1]
    head, back = HALO + EDGE, KERNEL - 1
    live_a = live_rows(begin - HALO, head, count)
    live_b = live_rows(begin + frames - back, HALO + back, count)
    for col in range(0, width, 128):
        cols = pl.ds(col, 128)
        raw = jnp.concatenate([prev[:, cols], own[:EDGE, cols]], axis=0).astype(F32)
        masked = jnp.where(live_a, raw, 0.0)
        ext[:back, cols] = jnp.zeros((back, 128), F32)
        ext[back : back + head, cols] = masked
        conv, low = conv_hidden(ext, taps, cols, 0, head, masked)
        conv_out[:EDGE, cols] = conv[HALO:]
        hidden[:head, cols] = low
        tail = own[frames - EDGE :, cols].astype(F32)[EDGE - back :]
        raw = jnp.concatenate([tail, after[:HALO, cols].astype(F32)], axis=0)
        masked = jnp.where(live_b, raw, 0.0)
        ext[back + head :, cols] = masked
        conv, low = conv_hidden(ext, taps, cols, back + head, HALO, masked[back:])
        conv_out[EDGE:, cols] = conv[:EDGE]
        hidden[head:, cols] = low
    first[...] = hidden[HALO:head]
    rows = head + HALO
    for col in range(0, 3 * width, 512):
        cols = pl.ds(col, 512)
        low = HALO if col < width else 0
        qkv[low:rows, cols] = dot(hidden[low:], w[:, cols], 1, 0).astype(BF16)
    qkv[rows:, :] = jnp.zeros((qkv.shape[0] - rows, 3 * width), BF16)


def ends_kernel(place, f0, f1, f2, f3, _, out):
    for slot, ref in enumerate((f0, f1, f2, f3)):
        out[slot * EDGE : (slot + 1) * EDGE] = ref[ref.shape[0] - EDGE :]


def peers_kernel(place, f1, f2, f3, tails, taps, hidden, ext):
    frames, width = f1.shape
    count, chip, core = place[1], place[2], place[3]
    for slot, ref in ((1, f1), (2, f2), (3, f3)):
        peer = chip ^ slot
        begin = (2 * peer + core) * frames
        source = jnp.where(core == 1, slot, chip ^ jnp.maximum(peer - 1, 0))
        start = pl.multiple_of(source * EDGE, EDGE)
        live = live_rows(begin - EDGE, frames + EDGE, count)
        real = begin - EDGE + lax.broadcasted_iota(jnp.int32, (frames + EDGE, 128), 0) >= 0
        live = live & real
        for col in range(0, width, 128):
            cols = pl.ds(col, 128)
            raw = jnp.concatenate([tails[pl.ds(start, EDGE), cols], ref[:, cols]], axis=0)
            masked = jnp.where(live, raw.astype(F32), 0.0)
            ext[:, cols] = masked
            _, low = conv_hidden(ext, taps, cols, EDGE - KERNEL + 1, frames, masked[EDGE:])
            hidden[(slot - 1) * frames : slot * frames, cols] = low


def attend_kernel(place, rim, mid, cot, after, attended, grads, sends, later):
    frames, width = cot.shape
    span = frames + HALO
    head_rows = HALO + EDGE
    begin, count, chip = place[0], place[1], place[2]

    def mask(shift, wanted):
        key = lax.broadcasted_iota(jnp.int32, (span, frames), 0)
        query = lax.broadcasted_iota(jnp.int32, (span, frames), 1)
        first = begin if shift else begin + frames
        gap = query + (HALO if shift else frames) - key
        seen = first + query - gap
        alive = (first + query < count) & (query < wanted)
        allowed = (gap >= 0) & (gap <= LEFT) & (seen >= 0) & alive
        return allowed, jnp.where(alive[:1], 0.0, 1.0)

    masks = [mask(True, frames), mask(False, HALO)]
    row = lax.broadcasted_iota(jnp.int32, (frames, width), 0)
    later[:HALO] = jnp.where(
        begin + frames + row[:HALO] < count, after[HALO:], jnp.zeros((HALO, width), BF16)
    )
    later[HALO:] = jnp.zeros((frames - HALO, width), BF16)
    factor = HEAD**-0.5

    def band(query, key, value, grad, allowed, missing):
        raised = jnp.where(allowed, jnp.exp(dot(key, query, 1, 1) * factor), 0.0)
        prob = raised * (1.0 / (jnp.sum(raised, axis=0, keepdims=True) + missing))
        grad_prob = dot(value, grad, 1, 1)
        mean = jnp.sum(prob * grad_prob, axis=0, keepdims=True)
        return prob.astype(BF16), (prob * (grad_prob - mean) * factor).astype(BF16)

    own_live = begin + lax.broadcasted_iota(jnp.int32, (frames, HEAD), 0) < count
    for head in range(HEADS):
        q_cols = pl.ds(head * HEAD, HEAD)
        k_cols = pl.ds(width + head * HEAD, HEAD)
        v_cols = pl.ds(2 * width + head * HEAD, HEAD)
        query = jnp.concatenate([rim[HALO:head_rows, q_cols], mid[:, q_cols]], axis=0)
        query_b = rim[head_rows:, q_cols]
        key, value = (
            jnp.concatenate(
                [rim[:head_rows, cols], mid[:, cols], rim[head_rows : head_rows + HALO, cols]],
                axis=0,
            )
            for cols in (k_cols, v_cols)
        )
        grad = jnp.where(own_live, cot[:, q_cols], jnp.zeros((frames, HEAD), BF16))
        grad_b = later[:, q_cols]
        prob, score = band(query, key[:span], value[:span], grad, *masks[0])
        prob_b, score_b = band(query_b, key[HALO:], value[HALO:], grad_b, *masks[1])
        attended[:, q_cols] = dot(prob, value[:span], 0, 0).astype(BF16)
        grads[:frames, q_cols] = dot(score, key[:span], 0, 0).astype(BF16)
        grads[frames:, q_cols] = dot(score_b, key[HALO:], 0, 0)[:EDGE].astype(BF16)
        for cols, mine, here, theirs, there in (
            (k_cols, score, query, score_b, query_b),
            (v_cols, prob, grad, prob_b, grad_b),
        ):
            total = dot(theirs[: frames + EDGE], there, 1, 0)
            grads[:frames, cols] = (total[:frames] + dot(mine[HALO:], here, 1, 0)).astype(BF16)
            grads[frames:, cols] = total[frames:].astype(BF16)
    if sends is None:
        return
    for k in range(4):
        slot = chip ^ k
        for i in range(4):
            block = 6 * i + k + (k + 1) // 2
            sends[slot, :, i * HEAD : (i + 1) * HEAD] = grads[:frames, pl.ds(block * HEAD, HEAD)]
        side = (k % 2) * (HEAD // 2)
        for pair in range(2):
            halves = []
            for i in (2 * pair, 2 * pair + 1):
                start = (6 * i + 1 + 3 * (k // 2)) * HEAD + side
                halves.append(grads[:frames, start : start + HEAD // 2])
            at = (4 + pair) * HEAD
            sends[slot, :, at : at + HEAD] = jnp.concatenate(halves, axis=1)


def attend_alone(place, rim, mid, cot, after, attended, grads, later):
    attend_kernel(place, rim, mid, cot, after, attended, grads, None, later)


def input_grad_kernel(place, grads, w, conv_mid, conv_rim, taps, grad_in, done, slopes):
    frames, width = grad_in.shape
    begin, count = place[0], place[1]
    done[...] = jnp.zeros(done.shape, F32)
    live = begin + lax.broadcasted_iota(jnp.int32, (frames, 256), 0) < count
    for col in range(0, width, 256):
        cols = pl.ds(col, 256)
        grad_hidden = dot(grads[...], w[cols, :], 1, 1)
        rim = conv_rim[:, cols]
        value = jnp.concatenate([rim[:EDGE], conv_mid[:, cols], rim[EDGE:]], axis=0)
        logistic = 1.0 / (1.0 + jnp.exp(-value))
        slopes[:, cols] = grad_hidden * (logistic * (1.0 + value * (1.0 - logistic)))
        total = grad_hidden[:frames]
        for tap in range(KERNEL):
            low = KERNEL - 1 - tap
            total = total + taps[tap : tap + 1, cols] * slopes[low : low + frames, cols]
        grad_in[:, cols] = jnp.where(live, total, 0.0).astype(BF16)


def weight_kernel(keep, place, first, mid, peers, b, b1, b2, b3, _, out):
    parity = place[3] if keep else 1 - place[3]
    left = jnp.concatenate([b[0], b1[...], b2[...], b3[...]], axis=0)
    for k in range(4):
        cols = pl.ds(pl.multiple_of((2 * k + parity) * HEAD, HEAD), HEAD)
        right = jnp.concatenate([a[:, cols] for a in (first, mid, peers)], axis=0)
        out[:, k * HEAD : (k + 1) * HEAD] = dot(left, right, 0, 0).astype(out.dtype)


def core_sum_kernel(place, keep, got, own, near, cross, ahead):
    me = place[4]
    outer, inner = 3 * (1 - me % 2), 2 - me // 2
    for out, i in ((near, outer), (cross, inner), (ahead, 6 - me - outer - inner), (own, me)):
        at = 0
        for size, base in ((HEAD, 0), (HEAD // 2, 4 * HEAD)):
            rows = pl.ds(pl.multiple_of(base + i * size, size), size)
            out[at : at + size] = (keep[rows] + got[rows].astype(F32)).astype(out.dtype)
            at += size


def forward_kernel(place, ahead, got, out):
    inside = (place[4] == 1) | (place[4] == 2)
    out[...] = (ahead[...] + jnp.where(inside, got[...].astype(F32), 0.0)).astype(BF16)


def part_sum_kernel(place, own, g1, g2, g3, g4, sends):
    chip = place[2]
    outside = (place[4] == 0) | (place[4] == 3)
    for k in range(4):
        cols = pl.ds(k * HEAD, HEAD)
        total = own[:, cols] + jnp.where(outside, g1[:, cols].astype(F32), 0.0)
        for got in (g2, g3, g4):
            total = total + got[:, cols].astype(F32)
        sends[k ^ chip] = total.astype(BF16)


def place_kernel(scale, place, own, g1, g2, g3, out):
    chip = place[2]
    for slot, ref in enumerate((own.at[0], g1, g2, g3)):
        k = chip ^ slot
        value = ref[...].astype(F32) * scale
        out[k + (k + 1) // 2] = value[:HEAD]
        start = pl.multiple_of((k % 2) * (HEAD // 2), HEAD // 2)
        out[1 + 3 * (k // 2), pl.ds(start, HEAD // 2)] = value[HEAD:]


def call(
    kernel, name, outs, place, operands, scratch=(), mib=16, flops=1000000, moved=1000000,
    remote=(), after=()
):
    return pl.pallas_call(
        kernel,
        name=name,
        out_shape=[jax.ShapeDtypeStruct(shape, dtype) for shape, dtype in outs],
        in_specs=[pl.BlockSpec(memory_space=pltpu.SMEM)]
        + vmem(len(operands))
        + [pl.BlockSpec(memory_space=pltpu.HBM)] * len(remote)
        + [pl.BlockSpec(memory_space=pl.ANY)] * len(after),
        out_specs=vmem(len(outs)),
        scratch_shapes=[pltpu.VMEM(*x) if isinstance(x, tuple) else x for x in scratch],
        compiler_params=params(mib),
        cost_estimate=cost(flops, moved),
    )(place, *operands, *remote, *after)


def shift(value, axis, steps):
    count = lax.axis_size(axis)
    pairs = [(i, i + steps) for i in range(count) if 0 <= i + steps < count]
    return lax.ppermute(value, axis, pairs)


def swap(value, axis, mask):
    return lax.ppermute(value, axis, [(i, i ^ mask) for i in range(lax.axis_size(axis))])


def on_device(frames_in, valid_frames, kernel, w_qkv, cotangent):
    record, cot = frames_in[0], cotangent[0]
    frames, width = record.shape
    span = frames + HALO
    parts, recs = lax.axis_size("tm"), lax.axis_size("dp")
    me = lax.axis_index("tm")
    place = jnp.stack(
        [me * frames, valid_frames[0], me // 2, me % 2, lax.axis_index("dp")]
    ).astype(jnp.int32)
    split = parts == 8 and recs == 4
    before = shift(record[frames - HALO :], "tm", 1)
    after = shift(jnp.concatenate([record[:HALO], cot[:HALO]], axis=0), "tm", -1)
    rows = frames - EDGE
    mid, conv_mid, qkv_mid, near, taps, w_near = call(
        own_kernel,
        "own_rows",
        [
            ((rows, width), BF16),
            ((rows, width), F32),
            ((rows, 3 * width), BF16),
            ((frames, width), BF16),
            (kernel.shape, F32),
            (w_qkv.shape, BF16),
        ],
        place,
        [],
        [
            ((frames, width), F32),
            pltpu.SemaphoreType.DMA((3 * width // 512,)),
            pltpu.SemaphoreType.DMA((2,)),
        ],
        flops=rows * width * 3 * width * 2,
        moved=9000000,
        remote=[record, kernel, w_qkv],
        mib=42,
    )
    if split:
        peers = [swap(near, "tm", mask) for mask in (2, 4, 6)]
    rows = 2 * HALO + EDGE
    first, conv_rim, qkv_rim = call(
        rim_kernel,
        "rim_rows",
        [
            ((EDGE, width), BF16),
            ((2 * EDGE, width), F32),
            ((HALO + EDGE + frames, 3 * width), BF16),
        ],
        place,
        [before, near, after, taps, w_near],
        [((rows + 2 * (KERNEL - 1), width), F32), ((rows, width), BF16)],
        flops=rows * width * 3 * width * 2,
        moved=9000000,
    )
    outs = [((frames, width), BF16), ((frames + EDGE, 3 * width), BF16)]
    attended, grads, *sends = call(
        attend_kernel if split else attend_alone,
        "attend",
        outs + [((4, frames, 3 * width // 4), BF16)] * split,
        place,
        [qkv_rim, qkv_mid, cot, after],
        [((frames, width), BF16)],
        mib=16,
        flops=8 * 12 * span * 128 * 128 * 2 * 8,
        moved=5000000,
    )
    if split:
        sends = sends[0]
        got = [swap(sends[slot], "tm", 2 * slot) for slot in (1, 2, 3)]
    grad_in, done = call(
        input_grad_kernel,
        "input_grad",
        [((frames, width), BF16), ((8, 128), F32)],
        place,
        [grads, w_near, conv_mid, conv_rim, taps],
        [((frames + EDGE, width), F32)],
        mib=20,
        flops=(frames + EDGE) * width * 3 * width * 2,
        moved=9000000,
    )
    scale = float(recs * parts * frames) ** (-0.5)
    if split:
        cols = 3 * width // 4
        shard = cols // 4
        (ends,) = call(
            ends_kernel, "ends", [((4 * EDGE, width), BF16)], place, [near, *peers], after=[grads]
        )
        (hidden,) = call(
            peers_kernel,
            "peer_hidden",
            [((3 * frames, width), BF16)],
            place,
            [*peers, swap(ends, "tm", 1), taps],
            [((frames + EDGE, width), F32)],
            flops=3 * frames * width * 40,
            moved=2000000,
        )
        send, keep = (
            call(
                functools.partial(weight_kernel, mine),
                "weight_" + ("keep" if mine else "send"),
                [((cols, width // 2), F32 if mine else BF16)],
                place,
                [first, mid, hidden, sends, *got],
                mib=20,
                flops=cols * width * frames * 4,
                moved=6000000,
                after=[done],
            )[0]
            for mine in (False, True)
        )
        sibling = swap(send, "tm", 1)
        own, near, cross, ahead = call(
            core_sum_kernel,
            "core_sum",
            [((shard, width // 2), dtype) for dtype in (F32, BF16, BF16, F32)],
            place,
            [keep, sibling],
        )
        g1 = swap(near, "dp", 1)
        g2 = lax.ppermute(cross, "dp", [(0, 2), (3, 1)])
        g3 = lax.ppermute(cross, "dp", [(1, 2), (2, 1)])
        (ahead,) = call(
            forward_kernel, "forward", [((shard, width // 2), BF16)], place, [ahead, g1]
        )
        g4 = lax.ppermute(ahead, "dp", [(0, 1), (1, 3), (2, 0), (3, 2)])
        (blocks,) = call(
            part_sum_kernel,
            "part_sum",
            [((4, shard, HEAD), BF16)],
            place,
            [own, g1, g2, g3, g4],
        )
        last = [swap(blocks[slot], "tm", 2 * slot) for slot in (1, 2, 3)]
        (qkv_grad,) = call(
            functools.partial(place_kernel, scale),
            "place",
            [((3 * HEADS // 4, HEAD, HEAD), F32)],
            place,
            [blocks, *last],
        )
    else:
        hidden = jnp.concatenate([first, mid], axis=0)
        partial = dot(hidden, grads[:frames], 0, 0).astype(BF16)
        by_time = lax.psum_scatter(partial, "tm", scatter_dimension=0, tiled=True)
        summed = lax.psum_scatter(by_time, "dp", scatter_dimension=1, tiled=True).astype(F32)
        qkv_grad = summed.reshape(summed.shape[0], -1, HEAD).transpose(1, 2, 0) * scale
    return (attended[None], grad_in[None], qkv_grad)


def solution(mesh):
    return jax.shard_map(
        on_device,
        mesh=mesh,
        in_specs=(P("dp", "tm", None), P("dp"), P(), P(), P("dp", "tm", None)),
        out_specs=(P("dp", "tm", None), P("dp", "tm", None), P("dp", None, "tm")),
        check_vma=False,
    )
```

```python
import functools

import jax
import jax.numpy as jnp
from jax import lax
from jax.experimental import pallas as pl
from jax.experimental.pallas import tpu as pltpu
from jax.sharding import PartitionSpec as P

HEADS = 8
HEAD = 128
KERNEL = 9
LEFT = 70
HALO = 80
EDGE = 16
MIB = 1024 * 1024
OWN = 42
F32 = jnp.float32
BF16 = jnp.bfloat16


def params(mib):
    return pltpu.CompilerParams(vmem_limit_bytes=mib * MIB)


def vmem(count):
    return [pl.BlockSpec(memory_space=pltpu.VMEM)] * count


def cost(flops, moved):
    return pl.CostEstimate(flops=flops, bytes_accessed=moved, transcendentals=0)


def dot(a, b, left, right):
    return lax.dot_general(a, b, (((left,), (right,)), ((), ())), preferred_element_type=F32)


def conv_hidden(ext, taps, cols, low, rows, masked):
    conv = taps[0:1, cols] * ext[low : low + rows, cols]
    for tap in range(1, KERNEL):
        conv = conv + taps[tap : tap + 1, cols] * ext[low + tap : low + tap + rows, cols]
    return conv, (masked + conv / (1.0 + jnp.exp(-conv))).astype(BF16)


def live_rows(first, rows, count):
    return first + lax.broadcasted_iota(jnp.int32, (rows, 128), 0) < count


def parts_of(both, frames):
    return both.at[:frames], both.at[frames : 2 * frames], both.at[2 * frames :]


def own_kernel(place, both, w, hidden, conv_out, qkv, w_out, ext, sems):
    frames, width = ext.shape
    own, _, taps = parts_of(both, frames)
    rows = frames - EDGE
    copies = [
        pltpu.make_async_copy(w.at[:, pl.ds(col, 512)], w_out.at[:, pl.ds(col, 512)], sems.at[i])
        for i, col in enumerate(range(0, 3 * width, 512))
    ]
    for copy in copies:
        copy.start()
    live = live_rows(place[0], frames, place[1])
    for col in range(0, width, 128):
        cols = pl.ds(col, 128)
        masked = jnp.where(live, own[:, cols], 0.0)
        ext[:, cols] = masked
        conv, low = conv_hidden(ext, taps, cols, EDGE - KERNEL + 1, rows, masked[EDGE:])
        conv_out[:, cols] = conv
        hidden[:, cols] = low
    for i, copy in enumerate(copies):
        copy.wait()
        cols = pl.ds(i * 512, 512)
        qkv[:, cols] = dot(hidden[...], w_out[:, cols], 1, 0).astype(BF16)


def rim_kernel(place, near, far, both, w, first, conv_out, qkv, ext, hidden):
    frames, width = qkv.shape[0] - HALO - EDGE, w.shape[0]
    own, _, taps = parts_of(both, frames)
    low_core = place[3] == 0
    begin, count = place[0], place[1]
    head, back = HALO + EDGE, KERNEL - 1
    live_a = live_rows(begin - HALO, head, count)
    live_b = live_rows(begin + frames - back, HALO + back, count)
    for col in range(0, width, 128):
        cols = pl.ds(col, 128)
        mate, other = near[:HALO, cols].astype(F32), far[:HALO, cols].astype(F32)
        prev = jnp.where(low_core, other, mate)
        raw = jnp.concatenate([prev, own[:EDGE, cols]], axis=0)
        masked = jnp.where(live_a, raw, 0.0)
        ext[:back, cols] = jnp.zeros((back, 128), F32)
        ext[back : back + head, cols] = masked
        conv, low = conv_hidden(ext, taps, cols, 0, head, masked)
        conv_out[:EDGE, cols] = conv[HALO:]
        hidden[:head, cols] = low
        tail = own[frames - back :, cols]
        raw = jnp.concatenate([tail, jnp.where(low_core, mate, other)], axis=0)
        masked = jnp.where(live_b, raw, 0.0)
        ext[back + head :, cols] = masked
        conv, low = conv_hidden(ext, taps, cols, back + head, HALO, masked[back:])
        conv_out[EDGE:, cols] = conv[:EDGE]
        hidden[head:, cols] = low
    first[...] = hidden[HALO:head]
    rows = head + HALO
    for col in range(0, 3 * width, 512):
        cols = pl.ds(col, 512)
        low = HALO if col < width else 0
        qkv[low:rows, cols] = dot(hidden[low:], w[:, cols], 1, 0).astype(BF16)
    qkv[rows:, :] = jnp.zeros((qkv.shape[0] - rows, 3 * width), BF16)


def ends_kernel(place, both, f1, f2, f3, _, out):
    frames = f1.shape[0]
    out[:EDGE] = both[frames - EDGE : frames].astype(BF16)
    for slot, ref in ((1, f1), (2, f2), (3, f3)):
        out[slot * EDGE : (slot + 1) * EDGE] = ref[frames - EDGE :]


def peers_kernel(place, f1, f2, f3, tails, both, hidden, ext):
    frames, width = f1.shape
    taps = parts_of(both, frames)[2]
    count, chip, core = place[1], place[2], place[3]
    for slot, ref in ((1, f1), (2, f2), (3, f3)):
        peer = chip ^ slot
        begin = (2 * peer + core) * frames
        source = jnp.where(core == 1, slot, chip ^ jnp.maximum(peer - 1, 0))
        start = pl.multiple_of(source * EDGE, EDGE)
        live = live_rows(begin - EDGE, frames + EDGE, count)
        real = begin - EDGE + lax.broadcasted_iota(jnp.int32, (frames + EDGE, 128), 0) >= 0
        live = live & real
        for col in range(0, width, 128):
            cols = pl.ds(col, 128)
            raw = jnp.concatenate([tails[pl.ds(start, EDGE), cols], ref[:, cols]], axis=0)
            masked = jnp.where(live, raw.astype(F32), 0.0)
            ext[:, cols] = masked
            _, low = conv_hidden(ext, taps, cols, EDGE - KERNEL + 1, frames, masked[EDGE:])
            hidden[(slot - 1) * frames : slot * frames, cols] = low


def attend_kernel(place, rim, mid, both, near, far, attended, grads, sends, later):
    frames, width = attended.shape
    cot = parts_of(both, frames)[1]
    span = frames + HALO
    head_rows = HALO + EDGE
    begin, count, chip = place[0], place[1], place[2]

    skip = (frames - LEFT) // EDGE * EDGE

    def mask(start, wanted):
        key = lax.broadcasted_iota(jnp.int32, (start + wanted, frames), 0)
        query = lax.broadcasted_iota(jnp.int32, (start + wanted, frames), 1)
        first = begin if wanted == frames else begin + frames
        gap = query + start - key
        seen = first + query - gap
        alive = (first + query < count) & (query < wanted)
        allowed = (gap >= 0) & (gap <= LEFT) & (seen >= 0) & alive
        return allowed, jnp.where(alive[:1], 0.0, 1.0)

    masks = [mask(HALO, frames), mask(frames - skip, HALO)]
    row = lax.broadcasted_iota(jnp.int32, (frames, width), 0)
    after = jnp.where(place[3] == 0, near[HALO:].astype(F32), far[HALO:].astype(F32))
    later[:HALO] = jnp.where(begin + frames + row[:HALO] < count, after, 0.0).astype(BF16)
    later[HALO:] = jnp.zeros((frames - HALO, width), BF16)
    factor = HEAD**-0.5

    def band(query, key, value, grad, allowed, missing):
        raised = jnp.where(allowed, jnp.exp(dot(key, query, 1, 1) * factor), 0.0)
        prob = raised * (1.0 / (jnp.sum(raised, axis=0, keepdims=True) + missing))
        grad_prob = dot(value, grad, 1, 1)
        mean = jnp.sum(prob * grad_prob, axis=0, keepdims=True)
        return prob.astype(BF16), (prob * (grad_prob - mean) * factor).astype(BF16)

    own_live = begin + lax.broadcasted_iota(jnp.int32, (frames, HEAD), 0) < count
    for head in range(HEADS):
        q_cols = pl.ds(head * HEAD, HEAD)
        k_cols = pl.ds(width + head * HEAD, HEAD)
        v_cols = pl.ds(2 * width + head * HEAD, HEAD)
        query = jnp.concatenate([rim[HALO:head_rows, q_cols], mid[:, q_cols]], axis=0)
        query_b = rim[head_rows:, q_cols]
        key, value = (
            jnp.concatenate(
                [rim[:head_rows, cols], mid[:, cols], rim[head_rows : head_rows + HALO, cols]],
                axis=0,
            )
            for cols in (k_cols, v_cols)
        )
        grad = jnp.where(own_live, cot[:, q_cols], 0.0).astype(BF16)
        grad_b = later[:, q_cols]
        prob, score = band(query, key[:span], value[:span], grad, *masks[0])
        prob_b, score_b = band(query_b, key[HALO + skip :], value[HALO + skip :], grad_b, *masks[1])
        attended[:, q_cols] = dot(prob, value[:span], 0, 0).astype(BF16)
        grads[:frames, q_cols] = dot(score, key[:span], 0, 0).astype(BF16)
        grads[frames:, q_cols] = dot(score_b[:, :EDGE], key[HALO + skip :], 0, 0).astype(BF16)
        for cols, mine, here, theirs, there in (
            (k_cols, score, query, score_b, query_b),
            (v_cols, prob, grad, prob_b, grad_b),
        ):
            late = dot(theirs[: frames - skip + EDGE], there, 1, 0)
            total = dot(mine[HALO:], here, 1, 0)
            grads[:skip, cols] = total[:skip].astype(BF16)
            grads[skip:frames, cols] = (total[skip:] + late[: frames - skip]).astype(BF16)
            grads[frames:, cols] = late[frames - skip :].astype(BF16)
    if sends is None:
        return
    for k in range(4):
        slot = chip ^ k
        for i in range(4):
            block = 6 * i + k + (k + 1) // 2
            sends[slot, :, i * HEAD : (i + 1) * HEAD] = grads[:frames, pl.ds(block * HEAD, HEAD)]
        side = (k % 2) * (HEAD // 2)
        for pair in range(2):
            halves = []
            for i in (2 * pair, 2 * pair + 1):
                start = (6 * i + 1 + 3 * (k // 2)) * HEAD + side
                halves.append(grads[:frames, start : start + HEAD // 2])
            at = (4 + pair) * HEAD
            sends[slot, :, at : at + HEAD] = jnp.concatenate(halves, axis=1)


def attend_alone(place, rim, mid, both, near, far, attended, grads, later):
    attend_kernel(place, rim, mid, both, near, far, attended, grads, None, later)


def input_grad_kernel(place, grads, w, conv_mid, conv_rim, both, *refs):
    grad_in, done, slopes = refs[-3:]
    frames, width = grad_in.shape
    taps = parts_of(both, frames)[2]
    begin, count = place[0], place[1]
    done[...] = jnp.zeros(done.shape, F32)
    live = begin + lax.broadcasted_iota(jnp.int32, (frames, 256), 0) < count
    for col in range(0, width, 256):
        cols = pl.ds(col, 256)
        grad_hidden = dot(grads[...], w[cols, :], 1, 1)
        rim = conv_rim[:, cols]
        value = jnp.concatenate([rim[:EDGE], conv_mid[:, cols], rim[EDGE:]], axis=0)
        logistic = 1.0 / (1.0 + jnp.exp(-value))
        slopes[:, cols] = grad_hidden * (logistic * (1.0 + value * (1.0 - logistic)))
        total = grad_hidden[:frames]
        for tap in range(KERNEL):
            low = KERNEL - 1 - tap
            total = total + taps[tap : tap + 1, cols] * slopes[low : low + frames, cols]
        grad_in[:, cols] = jnp.where(live, total, 0.0).astype(BF16)


def weight_kernel(keep, place, first, mid, peers, b, b1, b2, b3, out):
    parity = place[3] if keep else 1 - place[3]
    left = jnp.concatenate([b[0], b1[...], b2[...], b3[...]], axis=0)
    for k in range(4):
        cols = pl.ds(pl.multiple_of((2 * k + parity) * HEAD, HEAD), HEAD)
        right = jnp.concatenate([a[:, cols] for a in (first, mid, peers)], axis=0)
        out[:, k * HEAD : (k + 1) * HEAD] = dot(left, right, 0, 0).astype(out.dtype)


def core_sum_kernel(place, keep, got, own, near, cross, ahead):
    for mask, out in ((2, near), (3, ahead), (1, cross), (0, own)):
        i = place[4] ^ mask
        at = 0
        for size, base in ((HEAD, 0), (HEAD // 2, 4 * HEAD)):
            rows = pl.ds(pl.multiple_of(base + i * size, size), size)
            out[at : at + size] = (keep[rows] + got[rows].astype(F32)).astype(out.dtype)
            at += size


def forward_kernel(place, ahead, got, out):
    out[...] = (ahead[...] + got[...].astype(F32)).astype(BF16)


def part_sum_kernel(place, own, g1, g2, _, sends):
    chip = place[2]
    for k in range(4):
        cols = pl.ds(k * HEAD, HEAD)
        total = own[:, cols] + g1[:, cols].astype(F32) + g2[:, cols].astype(F32)
        sends[k ^ chip] = total.astype(BF16)


def place_kernel(scale, place, own, g1, g2, g3, out):
    chip = place[2]
    for slot, ref in enumerate((own.at[0], g1, g2, g3)):
        k = chip ^ slot
        value = ref[...].astype(F32) * scale
        out[k + (k + 1) // 2] = value[:HEAD]
        start = pl.multiple_of((k % 2) * (HEAD // 2), HEAD // 2)
        out[1 + 3 * (k // 2), pl.ds(start, HEAD // 2)] = value[HEAD:]


def call(
    kernel, name, outs, place, operands, scratch=(), mib=16, flops=1000000, moved=1000000,
    remote=(), after=()
):
    return pl.pallas_call(
        kernel,
        name=name,
        out_shape=[jax.ShapeDtypeStruct(shape, dtype) for shape, dtype in outs],
        in_specs=[pl.BlockSpec(memory_space=pltpu.SMEM)]
        + vmem(len(operands))
        + [pl.BlockSpec(memory_space=pltpu.HBM)] * len(remote)
        + [pl.BlockSpec(memory_space=pl.ANY)] * len(after),
        out_specs=vmem(len(outs)),
        scratch_shapes=[pltpu.VMEM(*x) if isinstance(x, tuple) else x for x in scratch],
        compiler_params=params(mib),
        cost_estimate=cost(flops, moved),
    )(place, *operands, *remote, *after)


def swap(value, axis, mask):
    return lax.ppermute(value, axis, [(i, i ^ mask) for i in range(lax.axis_size(axis))])


def on_device(frames_in, valid_frames, kernel, w_qkv, cotangent):
    record, cot = frames_in[0], cotangent[0]
    frames, width = record.shape
    span = frames + HALO
    parts, recs = lax.axis_size("tm"), lax.axis_size("dp")
    me = lax.axis_index("tm")
    place = jnp.stack(
        [me * frames, valid_frames[0], me // 2, me % 2, lax.axis_index("dp")]
    ).astype(jnp.int32)
    split = parts == 8 and recs == 4
    both = lax.optimization_barrier(
        jnp.concatenate([record.astype(F32), cot.astype(F32), kernel], axis=0)
    )
    last = jnp.concatenate([both[frames - HALO : frames]] * 2, axis=0)
    first = jnp.concatenate([both[:HALO], both[frames : frames + HALO]], axis=0)
    low_core = me % 2 == 0
    near = swap(jnp.where(low_core, last, first).astype(BF16), "tm", 1)
    far = lax.ppermute(
        jnp.where(low_core, first, last).astype(BF16),
        "tm",
        [(i, i + 1 if i % 2 else i - 1) for i in range(1, parts - 1)],
    )
    if split:
        peers = [swap(record, "tm", mask) for mask in (2, 4, 6)]
    rows = frames - EDGE
    mid, conv_mid, qkv_mid, w_near = call(
        own_kernel,
        "own_rows",
        [
            ((rows, width), BF16),
            ((rows, width), F32),
            ((rows, 3 * width), BF16),
            (w_qkv.shape, BF16),
        ],
        place,
        [both],
        [((frames, width), F32), pltpu.SemaphoreType.DMA((3 * width // 512,))],
        flops=rows * width * 3 * width * 2,
        moved=9000000,
        remote=[w_qkv],
        mib=OWN,
    )
    rows = 2 * HALO + EDGE
    first, conv_rim, qkv_rim = call(
        rim_kernel,
        "rim_rows",
        [
            ((EDGE, width), BF16),
            ((2 * EDGE, width), F32),
            ((HALO + EDGE + frames, 3 * width), BF16),
        ],
        place,
        [near, far, both, w_near],
        [((rows + 2 * (KERNEL - 1), width), F32), ((rows, width), BF16)],
        flops=rows * width * 3 * width * 2,
        moved=9000000,
    )
    outs = [((frames, width), BF16), ((frames + EDGE, 3 * width), BF16)]
    attended, grads, *sends = call(
        attend_kernel if split else attend_alone,
        "attend",
        outs + [((4, frames, 3 * width // 4), BF16)] * split,
        place,
        [qkv_rim, qkv_mid, both, near, far],
        [((frames, width), BF16)],
        mib=16,
        flops=8 * 12 * span * 128 * 128 * 2 * 8,
        moved=5000000,
    )
    if split:
        sends = sends[0]
        got = [swap(sends[slot], "tm", 2 * slot) for slot in (1, 2, 3)]
    scale = float(recs * parts * frames) ** (-0.5)
    if split:
        cols = 3 * width // 4
        shard = cols // 4
        (ends,) = call(
            ends_kernel, "ends", [((4 * EDGE, width), BF16)], place, [both, *peers], after=[grads]
        )
        (hidden,) = call(
            peers_kernel,
            "peer_hidden",
            [((3 * frames, width), BF16)],
            place,
            [*peers, swap(ends, "tm", 1), both],
            [((frames + EDGE, width), F32)],
            flops=3 * frames * width * 40,
            moved=2000000,
        )
        send, keep = (
            call(
                functools.partial(weight_kernel, mine),
                "weight_" + ("keep" if mine else "send"),
                [((cols, width // 2), F32 if mine else BF16)],
                place,
                [first, mid, hidden, sends, *got],
                mib=20,
                flops=cols * width * frames * 4,
                moved=6000000,
            )[0]
            for mine in (False, True)
        )
        sibling = swap(send, "tm", 1)
        own, near, cross, ahead = call(
            core_sum_kernel,
            "core_sum",
            [((shard, width // 2), dtype) for dtype in (F32, BF16, BF16, F32)],
            place,
            [keep, sibling],
        )
        late = [near]
        grad_in, done = call(
            input_grad_kernel,
            "input_grad",
            [((frames, width), BF16), ((8, 128), F32)],
            place,
            [grads, w_near, conv_mid, conv_rim, both],
            [((frames + EDGE, width), F32)],
            mib=20,
            flops=(frames + EDGE) * width * 3 * width * 2,
            moved=9000000,
            after=late,
        )
        got_near, got_cross = swap(near, "dp", 1), swap(cross, "dp", 1)
        (ahead,) = call(
            forward_kernel, "forward", [((shard, width // 2), BF16)], place, [ahead, got_near]
        )
        summed = [swap(ahead, "dp", 3), got_cross]
        (blocks,) = call(
            part_sum_kernel,
            "part_sum",
            [((4, shard, HEAD), BF16)],
            place,
            [own, *summed],
            after=[done],
        )
        last = [swap(blocks[slot], "tm", 2 * slot) for slot in (1, 2, 3)]
        (qkv_grad,) = call(
            functools.partial(place_kernel, scale),
            "place",
            [((3 * HEADS // 4, HEAD, HEAD), F32)],
            place,
            [blocks, *last],
        )
    else:
        late = []
        grad_in, done = call(
            input_grad_kernel,
            "input_grad",
            [((frames, width), BF16), ((8, 128), F32)],
            place,
            [grads, w_near, conv_mid, conv_rim, both],
            [((frames + EDGE, width), F32)],
            mib=20,
            flops=(frames + EDGE) * width * 3 * width * 2,
            moved=9000000,
            after=late,
        )
        hidden = jnp.concatenate([first, mid], axis=0)
        partial = dot(hidden, grads[:frames], 0, 0).astype(BF16)
        by_time = lax.psum_scatter(partial, "tm", scatter_dimension=0, tiled=True)
        summed = lax.psum_scatter(by_time, "dp", scatter_dimension=1, tiled=True).astype(F32)
        qkv_grad = summed.reshape(summed.shape[0], -1, HEAD).transpose(1, 2, 0) * scale
    return (attended[None], grad_in[None], qkv_grad)


def solution(mesh):
    return jax.shard_map(
        on_device,
        mesh=mesh,
        in_specs=(P("dp", "tm", None), P("dp"), P(), P(), P("dp", "tm", None)),
        out_specs=(P("dp", "tm", None), P("dp", "tm", None), P("dp", None, "tm")),
        check_vma=False,
    )
```

```python
import functools

import jax
import jax.numpy as jnp
from jax import lax
from jax.experimental import pallas as pl
from jax.experimental.pallas import tpu as pltpu
from jax.sharding import PartitionSpec as P

HEADS = 8
HEAD = 128
KERNEL = 9
LEFT = 70
HALO = 80
EDGE = 16
MIB = 1024 * 1024
OWN = 42
F32 = jnp.float32
BF16 = jnp.bfloat16


def params(mib):
    return pltpu.CompilerParams(vmem_limit_bytes=mib * MIB)


def vmem(count):
    return [pl.BlockSpec(memory_space=pltpu.VMEM)] * count


def cost(flops, moved):
    return pl.CostEstimate(flops=flops, bytes_accessed=moved, transcendentals=0)


def dot(a, b, left, right):
    return lax.dot_general(a, b, (((left,), (right,)), ((), ())), preferred_element_type=F32)


def conv_hidden(ext, taps, cols, low, rows, masked):
    conv = taps[0:1, cols] * ext[low : low + rows, cols]
    for tap in range(1, KERNEL):
        conv = conv + taps[tap : tap + 1, cols] * ext[low + tap : low + tap + rows, cols]
    return conv, (masked + conv / (1.0 + jnp.exp(-conv))).astype(BF16)


def live_rows(first, rows, count):
    return first + lax.broadcasted_iota(jnp.int32, (rows, 128), 0) < count


def parts_of(both, frames):
    return both.at[:frames], both.at[frames : 2 * frames], both.at[2 * frames :]


def own_kernel(place, both, w, hidden, conv_out, qkv, w_out, ext, sems):
    frames, width = ext.shape
    own, _, taps = parts_of(both, frames)
    rows = frames - EDGE
    copies = [
        pltpu.make_async_copy(w.at[:, pl.ds(col, 512)], w_out.at[:, pl.ds(col, 512)], sems.at[i])
        for i, col in enumerate(range(0, 3 * width, 512))
    ]
    for copy in copies:
        copy.start()
    live = live_rows(place[0], frames, place[1])
    for col in range(0, width, 128):
        cols = pl.ds(col, 128)
        masked = jnp.where(live, own[:, cols], 0.0)
        ext[:, cols] = masked
        conv, low = conv_hidden(ext, taps, cols, EDGE - KERNEL + 1, rows, masked[EDGE:])
        conv_out[:, cols] = conv
        hidden[:, cols] = low
    for i, copy in enumerate(copies):
        copy.wait()
        cols = pl.ds(i * 512, 512)
        qkv[:, cols] = dot(hidden[...], w_out[:, cols], 1, 0).astype(BF16)


def rim_kernel(place, near, far, both, w, first, conv_out, qkv, ext, hidden):
    frames, width = qkv.shape[0] - HALO - EDGE, w.shape[0]
    own, _, taps = parts_of(both, frames)
    low_core = place[3] == 0
    begin, count = place[0], place[1]
    head, back = HALO + EDGE, KERNEL - 1
    live_a = live_rows(begin - HALO, head, count)
    live_b = live_rows(begin + frames - back, HALO + back, count)
    for col in range(0, width, 128):
        cols = pl.ds(col, 128)
        mate, other = near[:HALO, cols].astype(F32), far[:HALO, cols].astype(F32)
        prev = jnp.where(low_core, other, mate)
        raw = jnp.concatenate([prev, own[:EDGE, cols]], axis=0)
        masked = jnp.where(live_a, raw, 0.0)
        ext[:back, cols] = jnp.zeros((back, 128), F32)
        ext[back : back + head, cols] = masked
        conv, low = conv_hidden(ext, taps, cols, 0, head, masked)
        conv_out[:EDGE, cols] = conv[HALO:]
        hidden[:head, cols] = low
        tail = own[frames - back :, cols]
        raw = jnp.concatenate([tail, jnp.where(low_core, mate, other)], axis=0)
        masked = jnp.where(live_b, raw, 0.0)
        ext[back + head :, cols] = masked
        conv, low = conv_hidden(ext, taps, cols, back + head, HALO, masked[back:])
        conv_out[EDGE:, cols] = conv[:EDGE]
        hidden[head:, cols] = low
    first[...] = hidden[HALO:head]
    rows = head + HALO
    for col in range(0, 3 * width, 512):
        cols = pl.ds(col, 512)
        low = HALO if col < width else 0
        qkv[low:rows, cols] = dot(hidden[low:], w[:, cols], 1, 0).astype(BF16)
    qkv[rows:, :] = jnp.zeros((qkv.shape[0] - rows, 3 * width), BF16)


def ends_kernel(place, both, f1, f2, f3, _, out):
    frames = f1.shape[0]
    out[:EDGE] = both[frames - EDGE : frames].astype(BF16)
    for slot, ref in ((1, f1), (2, f2), (3, f3)):
        out[slot * EDGE : (slot + 1) * EDGE] = ref[frames - EDGE :]


def peers_kernel(place, f1, f2, f3, tails, both, hidden, ext):
    frames, width = f1.shape
    taps = parts_of(both, frames)[2]
    count, chip, core = place[1], place[2], place[3]
    for slot, ref in ((1, f1), (2, f2), (3, f3)):
        peer = chip ^ slot
        begin = (2 * peer + core) * frames
        source = jnp.where(core == 1, slot, chip ^ jnp.maximum(peer - 1, 0))
        start = pl.multiple_of(source * EDGE, EDGE)
        live = live_rows(begin - EDGE, frames + EDGE, count)
        real = begin - EDGE + lax.broadcasted_iota(jnp.int32, (frames + EDGE, 128), 0) >= 0
        live = live & real
        for col in range(0, width, 128):
            cols = pl.ds(col, 128)
            raw = jnp.concatenate([tails[pl.ds(start, EDGE), cols], ref[:, cols]], axis=0)
            masked = jnp.where(live, raw.astype(F32), 0.0)
            ext[:, cols] = masked
            _, low = conv_hidden(ext, taps, cols, EDGE - KERNEL + 1, frames, masked[EDGE:])
            hidden[(slot - 1) * frames : slot * frames, cols] = low


def attend_kernel(place, rim, mid, both, near, far, attended, grads, sends, later):
    frames, width = attended.shape
    cot = parts_of(both, frames)[1]
    span = frames + HALO
    head_rows = HALO + EDGE
    begin, count, chip = place[0], place[1], place[2]

    skip = (frames - LEFT) // EDGE * EDGE

    def mask(start, wanted):
        key = lax.broadcasted_iota(jnp.int32, (start + wanted, frames), 0)
        query = lax.broadcasted_iota(jnp.int32, (start + wanted, frames), 1)
        first = begin if wanted == frames else begin + frames
        gap = query + start - key
        seen = first + query - gap
        alive = (first + query < count) & (query < wanted)
        allowed = (gap >= 0) & (gap <= LEFT) & (seen >= 0) & alive
        return allowed, jnp.where(alive[:1], 0.0, 1.0)

    masks = [mask(HALO, frames), mask(frames - skip, HALO)]
    row = lax.broadcasted_iota(jnp.int32, (frames, width), 0)
    after = jnp.where(place[3] == 0, near[HALO:].astype(F32), far[HALO:].astype(F32))
    later[:HALO] = jnp.where(begin + frames + row[:HALO] < count, after, 0.0).astype(BF16)
    later[HALO:] = jnp.zeros((frames - HALO, width), BF16)
    factor = HEAD**-0.5

    def band(query, key, value, grad, allowed, missing):
        raised = jnp.where(allowed, jnp.exp(dot(key, query, 1, 1) * factor), 0.0)
        prob = raised * (1.0 / (jnp.sum(raised, axis=0, keepdims=True) + missing))
        grad_prob = dot(value, grad, 1, 1)
        mean = jnp.sum(prob * grad_prob, axis=0, keepdims=True)
        return prob.astype(BF16), (prob * (grad_prob - mean) * factor).astype(BF16)

    own_live = begin + lax.broadcasted_iota(jnp.int32, (frames, HEAD), 0) < count
    for head in range(HEADS):
        q_cols = pl.ds(head * HEAD, HEAD)
        k_cols = pl.ds(width + head * HEAD, HEAD)
        v_cols = pl.ds(2 * width + head * HEAD, HEAD)
        query = jnp.concatenate([rim[HALO:head_rows, q_cols], mid[:, q_cols]], axis=0)
        query_b = rim[head_rows:, q_cols]
        key, value = (
            jnp.concatenate(
                [rim[:head_rows, cols], mid[:, cols], rim[head_rows : head_rows + HALO, cols]],
                axis=0,
            )
            for cols in (k_cols, v_cols)
        )
        grad = jnp.where(own_live, cot[:, q_cols], 0.0).astype(BF16)
        grad_b = later[:, q_cols]
        prob, score = band(query, key[:span], value[:span], grad, *masks[0])
        prob_b, score_b = band(query_b, key[HALO + skip :], value[HALO + skip :], grad_b, *masks[1])
        attended[:, q_cols] = dot(prob, value[:span], 0, 0).astype(BF16)
        grads[:frames, q_cols] = dot(score, key[:span], 0, 0).astype(BF16)
        grads[frames:, q_cols] = dot(score_b[:, :EDGE], key[HALO + skip :], 0, 0).astype(BF16)
        for cols, mine, here, theirs, there in (
            (k_cols, score, query, score_b, query_b),
            (v_cols, prob, grad, prob_b, grad_b),
        ):
            late = dot(theirs[: frames - skip + EDGE], there, 1, 0)
            total = dot(mine[HALO:], here, 1, 0)
            grads[:skip, cols] = total[:skip].astype(BF16)
            grads[skip:frames, cols] = (total[skip:] + late[: frames - skip]).astype(BF16)
            grads[frames:, cols] = late[frames - skip :].astype(BF16)
    if sends is None:
        return
    for k in range(4):
        slot = chip ^ k
        for i in range(4):
            block = 6 * i + k + (k + 1) // 2
            sends[slot, :, i * HEAD : (i + 1) * HEAD] = grads[:frames, pl.ds(block * HEAD, HEAD)]
        side = (k % 2) * (HEAD // 2)
        for pair in range(2):
            halves = []
            for i in (2 * pair, 2 * pair + 1):
                start = (6 * i + 1 + 3 * (k // 2)) * HEAD + side
                halves.append(grads[:frames, start : start + HEAD // 2])
            at = (4 + pair) * HEAD
            sends[slot, :, at : at + HEAD] = jnp.concatenate(halves, axis=1)


def attend_alone(place, rim, mid, both, near, far, attended, grads, later):
    attend_kernel(place, rim, mid, both, near, far, attended, grads, None, later)


def input_grad_kernel(place, grads, w, conv_mid, conv_rim, both, *refs):
    grad_in, done, slopes = refs[-3:]
    frames, width = grad_in.shape
    taps = parts_of(both, frames)[2]
    begin, count = place[0], place[1]
    done[...] = jnp.zeros(done.shape, F32)
    live = begin + lax.broadcasted_iota(jnp.int32, (frames, 256), 0) < count
    for col in range(0, width, 256):
        cols = pl.ds(col, 256)
        grad_hidden = dot(grads[...], w[cols, :], 1, 1)
        rim = conv_rim[:, cols]
        value = jnp.concatenate([rim[:EDGE], conv_mid[:, cols], rim[EDGE:]], axis=0)
        logistic = 1.0 / (1.0 + jnp.exp(-value))
        slopes[:, cols] = grad_hidden * (logistic * (1.0 + value * (1.0 - logistic)))
        total = grad_hidden[:frames]
        for tap in range(KERNEL):
            low = KERNEL - 1 - tap
            total = total + taps[tap : tap + 1, cols] * slopes[low : low + frames, cols]
        grad_in[:, cols] = jnp.where(live, total, 0.0).astype(BF16)


def weight_kernel(keep, place, first, mid, peers, b, b1, b2, b3, out):
    parity = place[3] if keep else 1 - place[3]
    left = jnp.concatenate([b[0], b1[...], b2[...], b3[...]], axis=0)
    for k in range(4):
        cols = pl.ds(pl.multiple_of((2 * k + parity) * HEAD, HEAD), HEAD)
        right = jnp.concatenate([a[:, cols] for a in (first, mid, peers)], axis=0)
        out[:, k * HEAD : (k + 1) * HEAD] = dot(left, right, 0, 0).astype(out.dtype)


def block(index):
    return pl.ds(pl.multiple_of(index * HEAD, HEAD), HEAD)


def halves(place, value, same, other):
    bit = place[2] % 2
    for out, x in ((other, 1 - bit), (same, bit)):
        for y in range(2):
            out[:, y * HEAD : (y + 1) * HEAD] = value(block(2 * y + x)).astype(out.dtype)


def core_sum_kernel(place, keep, got, near, ahead, *outs):
    parts = ((0, HEAD, 0), (HEAD, HEAD // 2, 4 * HEAD))

    def rows_of(mask, size, base):
        return pl.ds(pl.multiple_of(base + (place[4] ^ mask) * size, size), size)

    for mask, out in ((2, near), (3, ahead)):
        for at, size, base in parts:
            rows = rows_of(mask, size, base)
            out[at : at + size] = (keep[rows] + got[rows].astype(F32)).astype(out.dtype)
    for mask, same, other in ((1, *outs[:2]), (0, *outs[2:])):
        for at, size, base in parts:
            rows = rows_of(mask, size, base)
            halves(
                place,
                lambda cols, rows=rows: keep[rows, cols] + got[rows, cols].astype(F32),
                same.at[at : at + size],
                other.at[at : at + size],
            )


def forward_kernel(place, ahead, got, same, other):
    halves(place, lambda cols: ahead[:, cols] + got[:, cols].astype(F32), same, other)


def mid_sum_kernel(place, s0, s1, s2, o0, o1, o2, _, keep, send):
    bit = place[2] // 2
    for out, y in ((send, 1 - bit), (keep, bit)):
        cols = block(y)
        for i, refs in enumerate(((s0, s1, s2), (o0, o1, o2))):
            a, b, c = (ref[:, cols].astype(F32) for ref in refs)
            out[i] = (a + b + c).astype(out.dtype)


def place_kernel(scale, place, keep, got, out):
    for slot, ref in enumerate((keep, keep, got, got)):
        value = ref[slot % 2].astype(F32) * scale
        k = place[2] ^ slot
        out[k + (k + 1) // 2] = value[:HEAD]
        start = pl.multiple_of((k % 2) * (HEAD // 2), HEAD // 2)
        out[1 + 3 * (k // 2), pl.ds(start, HEAD // 2)] = value[HEAD:]


def call(
    kernel, name, outs, place, operands, scratch=(), mib=16, flops=1000000, moved=1000000,
    remote=(), after=()
):
    return pl.pallas_call(
        kernel,
        name=name,
        out_shape=[jax.ShapeDtypeStruct(shape, dtype) for shape, dtype in outs],
        in_specs=[pl.BlockSpec(memory_space=pltpu.SMEM)]
        + vmem(len(operands))
        + [pl.BlockSpec(memory_space=pltpu.HBM)] * len(remote)
        + [pl.BlockSpec(memory_space=pl.ANY)] * len(after),
        out_specs=vmem(len(outs)),
        scratch_shapes=[pltpu.VMEM(*x) if isinstance(x, tuple) else x for x in scratch],
        compiler_params=params(mib),
        cost_estimate=cost(flops, moved),
    )(place, *operands, *remote, *after)


def swap(value, axis, mask):
    return lax.ppermute(value, axis, [(i, i ^ mask) for i in range(lax.axis_size(axis))])


def swap_both(value, dp_mask, tm_mask):
    recs = lax.axis_size("dp")
    count = lax.axis_size("tm") * recs
    pairs = [(i, (i // recs ^ tm_mask) * recs + (i % recs ^ dp_mask)) for i in range(count)]
    return lax.ppermute(value, ("tm", "dp"), pairs)


def on_device(frames_in, valid_frames, kernel, w_qkv, cotangent):
    record, cot = frames_in[0], cotangent[0]
    frames, width = record.shape
    span = frames + HALO
    parts, recs = lax.axis_size("tm"), lax.axis_size("dp")
    me = lax.axis_index("tm")
    place = jnp.stack(
        [me * frames, valid_frames[0], me // 2, me % 2, lax.axis_index("dp")]
    ).astype(jnp.int32)
    split = parts == 8 and recs == 4
    both = lax.optimization_barrier(
        jnp.concatenate([record.astype(F32), cot.astype(F32), kernel], axis=0)
    )
    last = jnp.concatenate([both[frames - HALO : frames]] * 2, axis=0)
    first = jnp.concatenate([both[:HALO], both[frames : frames + HALO]], axis=0)
    low_core = me % 2 == 0
    near = swap(jnp.where(low_core, last, first).astype(BF16), "tm", 1)
    far = lax.ppermute(
        jnp.where(low_core, first, last).astype(BF16),
        "tm",
        [(i, i + 1 if i % 2 else i - 1) for i in range(1, parts - 1)],
    )
    if split:
        peers = [swap(record, "tm", mask) for mask in (2, 4, 6)]
    rows = frames - EDGE
    mid, conv_mid, qkv_mid, w_near = call(
        own_kernel,
        "own_rows",
        [
            ((rows, width), BF16),
            ((rows, width), F32),
            ((rows, 3 * width), BF16),
            (w_qkv.shape, BF16),
        ],
        place,
        [both],
        [((frames, width), F32), pltpu.SemaphoreType.DMA((3 * width // 512,))],
        flops=rows * width * 3 * width * 2,
        moved=9000000,
        remote=[w_qkv],
        mib=OWN,
    )
    rows = 2 * HALO + EDGE
    first, conv_rim, qkv_rim = call(
        rim_kernel,
        "rim_rows",
        [
            ((EDGE, width), BF16),
            ((2 * EDGE, width), F32),
            ((HALO + EDGE + frames, 3 * width), BF16),
        ],
        place,
        [near, far, both, w_near],
        [((rows + 2 * (KERNEL - 1), width), F32), ((rows, width), BF16)],
        flops=rows * width * 3 * width * 2,
        moved=9000000,
    )
    outs = [((frames, width), BF16), ((frames + EDGE, 3 * width), BF16)]
    attended, grads, *sends = call(
        attend_kernel if split else attend_alone,
        "attend",
        outs + [((4, frames, 3 * width // 4), BF16)] * split,
        place,
        [qkv_rim, qkv_mid, both, near, far],
        [((frames, width), BF16)],
        mib=16,
        flops=8 * 12 * span * 128 * 128 * 2 * 8,
        moved=5000000,
    )
    if split:
        sends = sends[0]
        got = [swap(sends[slot], "tm", 2 * slot) for slot in (1, 2, 3)]
    scale = float(recs * parts * frames) ** (-0.5)
    if split:
        cols = 3 * width // 4
        shard = cols // 4
        (ends,) = call(
            ends_kernel, "ends", [((4 * EDGE, width), BF16)], place, [both, *peers], after=[grads]
        )
        (hidden,) = call(
            peers_kernel,
            "peer_hidden",
            [((3 * frames, width), BF16)],
            place,
            [*peers, swap(ends, "tm", 1), both],
            [((frames + EDGE, width), F32)],
            flops=3 * frames * width * 40,
            moved=2000000,
        )
        send, keep = (
            call(
                functools.partial(weight_kernel, mine),
                "weight_" + ("keep" if mine else "send"),
                [((cols, width // 2), F32 if mine else BF16)],
                place,
                [first, mid, hidden, sends, *got],
                mib=20,
                flops=cols * width * frames * 4,
                moved=6000000,
            )[0]
            for mine in (False, True)
        )
        sibling = swap(send, "tm", 1)
        half = (shard, 2 * HEAD)
        near, ahead, cross_same, cross_other, own_same, own_other = call(
            core_sum_kernel,
            "core_sum",
            [
                ((shard, width // 2), BF16),
                ((shard, width // 2), F32),
                (half, BF16),
                (half, BF16),
                (half, F32),
                (half, BF16),
            ],
            place,
            [keep, sibling],
        )
        late = [near]
        grad_in, done = call(
            input_grad_kernel,
            "input_grad",
            [((frames, width), BF16), ((8, 128), F32)],
            place,
            [grads, w_near, conv_mid, conv_rim, both],
            [((frames + EDGE, width), F32)],
            mib=20,
            flops=(frames + EDGE) * width * 3 * width * 2,
            moved=9000000,
            after=late,
        )
        got_near = swap(near, "dp", 1)
        got_cross = swap(cross_same, "dp", 1), swap_both(cross_other, 1, 2)
        got_own = swap(own_other, "tm", 2)
        same, other = call(
            forward_kernel, "forward", [(half, BF16)] * 2, place, [ahead, got_near]
        )
        got_sums = swap(same, "dp", 3), swap_both(other, 3, 2)
        keep, send = call(
            mid_sum_kernel,
            "mid_sum",
            [((2, shard, HEAD), F32), ((2, shard, HEAD), BF16)],
            place,
            [own_same, got_cross[0], got_sums[0], got_own, got_cross[1], got_sums[1]],
            after=[done],
        )
        (qkv_grad,) = call(
            functools.partial(place_kernel, scale),
            "place",
            [((3 * HEADS // 4, HEAD, HEAD), F32)],
            place,
            [keep, swap(send, "tm", 4)],
        )
    else:
        late = []
        grad_in, done = call(
            input_grad_kernel,
            "input_grad",
            [((frames, width), BF16), ((8, 128), F32)],
            place,
            [grads, w_near, conv_mid, conv_rim, both],
            [((frames + EDGE, width), F32)],
            mib=20,
            flops=(frames + EDGE) * width * 3 * width * 2,
            moved=9000000,
            after=late,
        )
        hidden = jnp.concatenate([first, mid], axis=0)
        partial = dot(hidden, grads[:frames], 0, 0).astype(BF16)
        by_time = lax.psum_scatter(partial, "tm", scatter_dimension=0, tiled=True)
        summed = lax.psum_scatter(by_time, "dp", scatter_dimension=1, tiled=True).astype(F32)
        qkv_grad = summed.reshape(summed.shape[0], -1, HEAD).transpose(1, 2, 0) * scale
    return (attended[None], grad_in[None], qkv_grad)


def solution(mesh):
    return jax.shard_map(
        on_device,
        mesh=mesh,
        in_specs=(P("dp", "tm", None), P("dp"), P(), P(), P("dp", "tm", None)),
        out_specs=(P("dp", "tm", None), P("dp", "tm", None), P("dp", None, "tm")),
        check_vma=False,
    )
```

```python
import functools

import jax
import jax.numpy as jnp
from jax import lax
from jax.experimental import pallas as pl
from jax.experimental.pallas import tpu as pltpu
from jax.sharding import PartitionSpec as P

HEADS = 8
HEAD = 128
KERNEL = 9
LEFT = 70
HALO = 80
EDGE = 16
MIB = 1024 * 1024
OWN = 42
F32 = jnp.float32
BF16 = jnp.bfloat16


def params(mib):
    return pltpu.CompilerParams(vmem_limit_bytes=mib * MIB)


def vmem(count):
    return [pl.BlockSpec(memory_space=pltpu.VMEM)] * count


def cost(flops, moved):
    return pl.CostEstimate(flops=flops, bytes_accessed=moved, transcendentals=0)


def dot(a, b, left, right):
    return lax.dot_general(a, b, (((left,), (right,)), ((), ())), preferred_element_type=F32)


def conv_hidden(ext, taps, cols, low, rows, masked):
    conv = taps[0:1, cols] * ext[low : low + rows, cols]
    for tap in range(1, KERNEL):
        conv = conv + taps[tap : tap + 1, cols] * ext[low + tap : low + tap + rows, cols]
    return conv, (masked + conv / (1.0 + jnp.exp(-conv))).astype(BF16)


def live_rows(first, rows, count):
    return first + lax.broadcasted_iota(jnp.int32, (rows, 128), 0) < count


def parts_of(both, frames):
    return both.at[:frames], both.at[frames : 2 * frames], both.at[2 * frames :]


def project_kernel(place, near, far, both, w, own_hidden, conv_out, qkv, w_out, ext, hidden, sems):
    frames, width = own_hidden.shape
    wide = width
    copies = [
        pltpu.make_async_copy(w.at[:, cols], w_out.at[:, cols], sems.at[i])
        for i, cols in enumerate(pl.ds(i * wide, wide) for i in range(3))
    ]
    for copy in copies:
        copy.start()
    own, _, taps = parts_of(both, frames)
    low_core = place[3] == 0
    rows, back = frames + 2 * HALO, KERNEL - 1
    live = live_rows(place[0] - HALO, rows, place[1])
    for col in range(0, width, 128):
        cols = pl.ds(col, 128)
        mate, other = near[:HALO, cols].astype(F32), far[:, cols].astype(F32)
        before, after = jnp.where(low_core, other, mate), jnp.where(low_core, mate, other)
        raw = jnp.concatenate([before, own[:, cols], after], axis=0)
        masked = jnp.where(live, raw, 0.0)
        ext[:back, cols] = jnp.zeros((back, 128), F32)
        ext[back:, cols] = masked
        conv, low = conv_hidden(ext, taps, cols, 0, rows, masked)
        conv_out[:, cols] = conv[HALO : HALO + frames + EDGE]
        hidden[:, cols] = low
    own_hidden[...] = hidden[HALO : HALO + frames]
    for i, copy in enumerate(copies):
        copy.wait()
        low = HALO if i * wide < width else 0
        for col in range(i * wide, (i + 1) * wide, 512):
            cols = pl.ds(col, 512)
            qkv[low:rows, cols] = dot(hidden[low:], w_out[:, cols], 1, 0).astype(BF16)
    qkv[rows:, :] = jnp.zeros((qkv.shape[0] - rows, 3 * width), BF16)


def ends_kernel(place, both, f1, f2, f3, _, out):
    frames = f1.shape[0]
    out[:EDGE] = both[frames - EDGE : frames].astype(BF16)
    for slot, ref in ((1, f1), (2, f2), (3, f3)):
        out[slot * EDGE : (slot + 1) * EDGE] = ref[frames - EDGE :]


def peers_kernel(place, f1, f2, f3, tails, both, hidden, ext):
    frames, width = f1.shape
    taps = parts_of(both, frames)[2]
    count, chip, core = place[1], place[2], place[3]
    for slot, ref in ((1, f1), (2, f2), (3, f3)):
        peer = chip ^ slot
        begin = (2 * peer + core) * frames
        source = jnp.where(core == 1, slot, chip ^ jnp.maximum(peer - 1, 0))
        start = pl.multiple_of(source * EDGE, EDGE)
        live = live_rows(begin - EDGE, frames + EDGE, count)
        real = begin - EDGE + lax.broadcasted_iota(jnp.int32, (frames + EDGE, 128), 0) >= 0
        live = live & real
        for col in range(0, width, 128):
            cols = pl.ds(col, 128)
            raw = jnp.concatenate([tails[pl.ds(start, EDGE), cols], ref[:, cols]], axis=0)
            masked = jnp.where(live, raw.astype(F32), 0.0)
            ext[:, cols] = masked
            _, low = conv_hidden(ext, taps, cols, EDGE - KERNEL + 1, frames, masked[EDGE:])
            hidden[(slot - 1) * frames : slot * frames, cols] = low


def attend_kernel(place, qkv, both, near, far, attended, grads, sends, later):
    frames, width = attended.shape
    cot = parts_of(both, frames)[1]
    span = frames + HALO
    begin, count, chip = place[0], place[1], place[2]

    skip = (frames - LEFT) // EDGE * EDGE

    def mask(start, wanted):
        key = lax.broadcasted_iota(jnp.int32, (start + wanted, frames), 0)
        query = lax.broadcasted_iota(jnp.int32, (start + wanted, frames), 1)
        first = begin if wanted == frames else begin + frames
        gap = query + start - key
        seen = first + query - gap
        alive = (first + query < count) & (query < wanted)
        allowed = (gap >= 0) & (gap <= LEFT) & (seen >= 0) & alive
        return allowed, jnp.where(alive[:1], 0.0, 1.0)

    masks = [mask(HALO, frames), mask(frames - skip, HALO)]
    row = lax.broadcasted_iota(jnp.int32, (frames, width), 0)
    after = jnp.where(place[3] == 0, near[HALO:].astype(F32), far[...].astype(F32))
    later[:HALO] = jnp.where(begin + frames + row[:HALO] < count, after, 0.0).astype(BF16)
    later[HALO:] = jnp.zeros((frames - HALO, width), BF16)
    factor = HEAD**-0.5

    def band(query, key, value, grad, allowed, missing):
        raised = jnp.where(allowed, jnp.exp(dot(key, query, 1, 1) * factor), 0.0)
        prob = raised * (1.0 / (jnp.sum(raised, axis=0, keepdims=True) + missing))
        grad_prob = dot(value, grad, 1, 1)
        mean = jnp.sum(prob * grad_prob, axis=0, keepdims=True)
        return prob.astype(BF16), (prob * (grad_prob - mean) * factor).astype(BF16)

    own_live = begin + lax.broadcasted_iota(jnp.int32, (frames, HEAD), 0) < count
    for head in range(HEADS):
        q_cols = pl.ds(head * HEAD, HEAD)
        k_cols = pl.ds(width + head * HEAD, HEAD)
        v_cols = pl.ds(2 * width + head * HEAD, HEAD)
        query = qkv[HALO : HALO + frames, q_cols]
        query_b = qkv[HALO + frames : HALO + 2 * frames, q_cols]
        key = qkv[: HALO + span, k_cols]
        value = qkv[: HALO + span, v_cols]
        grad = jnp.where(own_live, cot[:, q_cols], 0.0).astype(BF16)
        grad_b = later[:, q_cols]
        prob, score = band(query, key[:span], value[:span], grad, *masks[0])
        prob_b, score_b = band(query_b, key[HALO + skip :], value[HALO + skip :], grad_b, *masks[1])
        attended[:, q_cols] = dot(prob, value[:span], 0, 0).astype(BF16)
        grads[:frames, q_cols] = dot(score, key[:span], 0, 0).astype(BF16)
        grads[frames:, q_cols] = dot(score_b[:, :EDGE], key[HALO + skip :], 0, 0).astype(BF16)
        for cols, mine, here, theirs, there in (
            (k_cols, score, query, score_b, query_b),
            (v_cols, prob, grad, prob_b, grad_b),
        ):
            late = dot(theirs[: frames - skip + EDGE], there, 1, 0)
            total = dot(mine[HALO:], here, 1, 0)
            grads[:skip, cols] = total[:skip].astype(BF16)
            grads[skip:frames, cols] = (total[skip:] + late[: frames - skip]).astype(BF16)
            grads[frames:, cols] = late[frames - skip :].astype(BF16)
    if sends is None:
        return
    for k in range(4):
        slot = chip ^ k
        for i in range(4):
            block = 6 * i + k + (k + 1) // 2
            sends[slot, :, i * HEAD : (i + 1) * HEAD] = grads[:frames, pl.ds(block * HEAD, HEAD)]
        side = (k % 2) * (HEAD // 2)
        for pair in range(2):
            halves = []
            for i in (2 * pair, 2 * pair + 1):
                start = (6 * i + 1 + 3 * (k // 2)) * HEAD + side
                halves.append(grads[:frames, start : start + HEAD // 2])
            at = (4 + pair) * HEAD
            sends[slot, :, at : at + HEAD] = jnp.concatenate(halves, axis=1)


def attend_alone(place, qkv, both, near, far, attended, grads, later):
    attend_kernel(place, qkv, both, near, far, attended, grads, None, later)


def input_grad_kernel(place, grads, w, conv, both, *refs):
    grad_in, done, slopes = refs[-3:]
    frames, width = grad_in.shape
    taps = parts_of(both, frames)[2]
    begin, count = place[0], place[1]
    done[...] = jnp.zeros(done.shape, F32)
    live = begin + lax.broadcasted_iota(jnp.int32, (frames, 256), 0) < count
    for col in range(0, width, 256):
        cols = pl.ds(col, 256)
        grad_hidden = dot(grads[...], w[cols, :], 1, 1)
        value = conv[:, cols]
        logistic = 1.0 / (1.0 + jnp.exp(-value))
        slopes[:, cols] = grad_hidden * (logistic * (1.0 + value * (1.0 - logistic)))
        total = grad_hidden[:frames]
        for tap in range(KERNEL):
            low = KERNEL - 1 - tap
            total = total + taps[tap : tap + 1, cols] * slopes[low : low + frames, cols]
        grad_in[:, cols] = jnp.where(live, total, 0.0).astype(BF16)


def weight_kernel(mine, place, own, peers, b, b1, b2, b3, out):
    parity = place[3] if mine else 1 - place[3]
    left = jnp.concatenate([b[0], b1[...], b2[...], b3[...]], axis=0)
    right = jnp.concatenate(
        [jnp.concatenate([a[:, block(2 * k + parity)] for k in range(4)], axis=1) for a in (own, peers)],
        axis=0,
    )
    out[...] = dot(left, right, 0, 0).astype(out.dtype)


def block(index):
    return pl.ds(pl.multiple_of(index * HEAD, HEAD), HEAD)


def halves(place, value, same, other):
    bit = place[2] % 2
    for out, x in ((other, 1 - bit), (same, bit)):
        for y in range(2):
            out[:, y * HEAD : (y + 1) * HEAD] = value(block(2 * y + x)).astype(out.dtype)


def shard_rows(place, mask):
    i = place[4] ^ mask
    for at, size, base in ((0, HEAD, 0), (HEAD, HEAD // 2, 4 * HEAD)):
        rows = pl.ds(pl.multiple_of(base + i * size, size), size)
        yield rows, slice(at, at + size)


def core_sum_kernel(place, keep, got, near, ahead, *outs):
    for mask, out in ((2, near), (3, ahead)):
        for rows, at in shard_rows(place, mask):
            out[at] = (keep[rows] + got[rows].astype(F32)).astype(out.dtype)
    for mask, same, other in ((1, *outs[:2]), (0, *outs[2:])):
        for rows, at in shard_rows(place, mask):
            halves(
                place,
                lambda cols, rows=rows: keep[rows, cols] + got[rows, cols].astype(F32),
                same.at[at],
                other.at[at],
            )


def forward_kernel(place, ahead, got, same, other):
    halves(place, lambda cols: ahead[:, cols] + got[:, cols].astype(F32), same, other)


def mid_sum_kernel(place, s0, s1, s2, o0, o1, o2, _, keep, send):
    bit = place[2] // 2
    for out, y in ((send, 1 - bit), (keep, bit)):
        cols = block(y)
        for i, refs in enumerate(((s0, s1, s2), (o0, o1, o2))):
            a, b, c = (ref[:, cols].astype(F32) for ref in refs)
            out[i] = (a + b + c).astype(out.dtype)


def place_kernel(scale, place, keep, got, out):
    for slot, ref in enumerate((keep, keep, got, got)):
        value = ref[slot % 2].astype(F32) * scale
        k = place[2] ^ slot
        out[k + (k + 1) // 2] = value[:HEAD]
        start = pl.multiple_of((k % 2) * (HEAD // 2), HEAD // 2)
        out[1 + 3 * (k // 2), pl.ds(start, HEAD // 2)] = value[HEAD:]


def call(
    kernel, name, outs, place, operands, scratch=(), mib=16, flops=1000000, moved=1000000,
    remote=(), after=()
):
    return pl.pallas_call(
        kernel,
        name=name,
        out_shape=[jax.ShapeDtypeStruct(shape, dtype) for shape, dtype in outs],
        in_specs=[pl.BlockSpec(memory_space=pltpu.SMEM)]
        + vmem(len(operands))
        + [pl.BlockSpec(memory_space=pltpu.HBM)] * len(remote)
        + [pl.BlockSpec(memory_space=pl.ANY)] * len(after),
        out_specs=vmem(len(outs)),
        scratch_shapes=[pltpu.VMEM(*x) if isinstance(x, tuple) else x for x in scratch],
        compiler_params=params(mib),
        cost_estimate=cost(flops, moved),
    )(place, *operands, *remote, *after)


def swap(value, axis, mask):
    return lax.ppermute(value, axis, [(i, i ^ mask) for i in range(lax.axis_size(axis))])


def swap_both(value, dp_mask, tm_mask):
    recs = lax.axis_size("dp")
    count = lax.axis_size("tm") * recs
    pairs = [(i, (i // recs ^ tm_mask) * recs + (i % recs ^ dp_mask)) for i in range(count)]
    return lax.ppermute(value, ("tm", "dp"), pairs)


def on_device(frames_in, valid_frames, kernel, w_qkv, cotangent):
    record, cot = frames_in[0], cotangent[0]
    frames, width = record.shape
    span = frames + HALO
    parts, recs = lax.axis_size("tm"), lax.axis_size("dp")
    me = lax.axis_index("tm")
    place = jnp.stack(
        [me * frames, valid_frames[0], me // 2, me % 2, lax.axis_index("dp")]
    ).astype(jnp.int32)
    split = parts == 8 and recs == 4
    both = lax.optimization_barrier(
        jnp.concatenate([record.astype(F32), cot.astype(F32), kernel], axis=0)
    )
    own = both[:frames].astype(BF16)
    last, first = own[frames - HALO :], own[:HALO]
    first_cot = both[frames : frames + HALO].astype(BF16)
    low_core = me % 2 == 0
    edge = jnp.where(low_core, last, first)
    near = swap(jnp.concatenate([edge, first_cot], axis=0), "tm", 1)
    down = [(i, i - 1) for i in range(2, parts, 2)]
    far = lax.ppermute(
        jnp.where(low_core, first, last), "tm", down + [(i, j) for j, i in down]
    )
    far_cot = lax.ppermute(first_cot, "tm", down)
    if split:
        peers = [swap(own, "tm", mask) for mask in (2, 4, 6)]
    rows = frames + 2 * HALO
    hidden, conv, qkv, w_near = call(
        project_kernel,
        "project",
        [
            ((frames, width), BF16),
            ((frames + EDGE, width), F32),
            ((HALO + 2 * frames, 3 * width), BF16),
            (w_qkv.shape, BF16),
        ],
        place,
        [near, far, both],
        [
            ((rows + KERNEL - 1, width), F32),
            ((rows, width), BF16),
            pltpu.SemaphoreType.DMA((3,)),
        ],
        flops=rows * width * 3 * width * 2,
        moved=9000000,
        remote=[w_qkv],
        mib=OWN,
    )
    outs = [((frames, width), BF16), ((frames + EDGE, 3 * width), BF16)]
    attended, grads, *sends = call(
        attend_kernel if split else attend_alone,
        "attend",
        outs + [((4, frames, 3 * width // 4), BF16)] * split,
        place,
        [qkv, both, near, far_cot],
        [((frames, width), BF16)],
        mib=16,
        flops=8 * 12 * span * 128 * 128 * 2 * 8,
        moved=5000000,
    )
    if split:
        sends = sends[0]
        got = [swap(sends[slot], "tm", 2 * slot) for slot in (1, 2, 3)]
    scale = float(recs * parts * frames) ** (-0.5)
    if split:
        cols = 3 * width // 4
        shard = cols // 4
        (ends,) = call(
            ends_kernel, "ends", [((4 * EDGE, width), BF16)], place, [both, *peers], after=[grads]
        )
        (peers_hidden,) = call(
            peers_kernel,
            "peer_hidden",
            [((3 * frames, width), BF16)],
            place,
            [*peers, swap(ends, "tm", 1), both],
            [((frames + EDGE, width), F32)],
            flops=3 * frames * width * 40,
            moved=2000000,
        )
        operands = [hidden, peers_hidden, sends, *got]
        whole, half = (shard, width // 2), (shard, 2 * HEAD)
        send, keep = (
            call(
                functools.partial(weight_kernel, mine),
                "weight_" + ("keep" if mine else "send"),
                [((cols, width // 2), F32 if mine else BF16)],
                place,
                operands,
                mib=20,
                flops=cols * width * frames * 4,
                moved=6000000,
            )[0]
            for mine in (False, True)
        )
        near, ahead, cross_same, cross_other, own_same, own_other = call(
            core_sum_kernel,
            "core_sum",
            [(whole, BF16), (whole, F32), (half, BF16), (half, BF16), (half, F32), (half, BF16)],
            place,
            [keep, swap(send, "tm", 1)],
        )
        late = [near]
        grad_in, done = call(
            input_grad_kernel,
            "input_grad",
            [((frames, width), BF16), ((8, 128), F32)],
            place,
            [grads, w_near, conv, both],
            [((frames + EDGE, width), F32)],
            mib=20,
            flops=(frames + EDGE) * width * 3 * width * 2,
            moved=9000000,
            after=late,
        )
        got_near = swap(near, "dp", 1)
        got_cross = swap(cross_same, "dp", 1), swap_both(cross_other, 1, 2)
        got_own = swap(own_other, "tm", 2)
        same, other = call(
            forward_kernel, "forward", [(half, BF16)] * 2, place, [ahead, got_near]
        )
        got_sums = swap(same, "dp", 3), swap_both(other, 3, 2)
        keep, send = call(
            mid_sum_kernel,
            "mid_sum",
            [((2, shard, HEAD), F32), ((2, shard, HEAD), BF16)],
            place,
            [own_same, got_cross[0], got_sums[0], got_own, got_cross[1], got_sums[1]],
            after=[done],
        )
        (qkv_grad,) = call(
            functools.partial(place_kernel, scale),
            "place",
            [((3 * HEADS // 4, HEAD, HEAD), F32)],
            place,
            [keep, swap(send, "tm", 4)],
        )
    else:
        late = []
        grad_in, done = call(
            input_grad_kernel,
            "input_grad",
            [((frames, width), BF16), ((8, 128), F32)],
            place,
            [grads, w_near, conv, both],
            [((frames + EDGE, width), F32)],
            mib=20,
            flops=(frames + EDGE) * width * 3 * width * 2,
            moved=9000000,
            after=late,
        )
        partial = dot(hidden, grads[:frames], 0, 0).astype(BF16)
        by_time = lax.psum_scatter(partial, "tm", scatter_dimension=0, tiled=True)
        summed = lax.psum_scatter(by_time, "dp", scatter_dimension=1, tiled=True).astype(F32)
        qkv_grad = summed.reshape(summed.shape[0], -1, HEAD).transpose(1, 2, 0) * scale
    return (attended[None], grad_in[None], qkv_grad)


def solution(mesh):
    return jax.shard_map(
        on_device,
        mesh=mesh,
        in_specs=(P("dp", "tm", None), P("dp"), P(), P(), P("dp", "tm", None)),
        out_specs=(P("dp", "tm", None), P("dp", "tm", None), P("dp", None, "tm")),
        check_vma=False,
    )
```

```python
import functools

import jax
import jax.numpy as jnp
from jax import lax
from jax.experimental import pallas as pl
from jax.experimental.pallas import tpu as pltpu
from jax.sharding import PartitionSpec as P

HEADS = 8
HEAD = 128
KERNEL = 9
LEFT = 70
HALO = 80
EDGE = 16
MIB = 1024 * 1024
OWN = 42
CHUNK = 48
GROUP = 4
F32 = jnp.float32
BF16 = jnp.bfloat16


def params(mib):
    return pltpu.CompilerParams(vmem_limit_bytes=mib * MIB)


def vmem(count):
    return [pl.BlockSpec(memory_space=pltpu.VMEM)] * count


def cost(flops, moved):
    return pl.CostEstimate(flops=flops, bytes_accessed=moved, transcendentals=0)


def dot(a, b, left, right):
    return lax.dot_general(a, b, (((left,), (right,)), ((), ())), preferred_element_type=F32)


def conv_hidden(ext, taps, cols, low, rows, hidden, conv_out=None, keep=(0, 0)):
    weights = [taps[tap : tap + 1, cols] for tap in range(KERNEL)]
    for start in range(0, rows, CHUNK):
        size = min(CHUNK, rows - start)
        at = low + start
        conv = weights[0] * ext[at : at + size, cols]
        for tap in range(1, KERNEL):
            conv = conv + weights[tap] * ext[at + tap : at + tap + size, cols]
        masked = ext[at + KERNEL - 1 : at + KERNEL - 1 + size, cols]
        hidden[start : start + size, cols] = (masked + conv / (1.0 + jnp.exp(-conv))).astype(BF16)
        first, last = max(start, keep[0]), min(start + size, keep[1])
        if first < last:
            conv_out[first - keep[0] : last - keep[0], cols] = conv[first - start : last - start]


def live_rows(first, rows, count):
    return first + lax.broadcasted_iota(jnp.int32, (rows, 128), 0) < count


def parts_of(both, frames):
    return both.at[:frames], both.at[frames : 2 * frames], both.at[2 * frames :]


def project_kernel(place, near, far, both, w, own_hidden, conv_out, qkv, w_out, ext, hidden, sems):
    frames, width = own_hidden.shape
    wide = width
    copies = [
        pltpu.make_async_copy(w.at[:, cols], w_out.at[:, cols], sems.at[i])
        for i, cols in enumerate(pl.ds(i * wide, wide) for i in range(3))
    ]
    for copy in copies:
        copy.start()
    own, _, taps = parts_of(both, frames)
    low_core = place[3] == 0
    rows, back = frames + 2 * HALO, KERNEL - 1
    live = live_rows(place[0] - HALO, rows, place[1])
    for col in range(0, width, 128):
        cols = pl.ds(col, 128)
        mate, other = near[:HALO, cols].astype(F32), far[:, cols].astype(F32)
        before, after = jnp.where(low_core, other, mate), jnp.where(low_core, mate, other)
        raw = jnp.concatenate([before, own[:, cols], after], axis=0)
        masked = jnp.where(live, raw, 0.0)
        ext[:back, cols] = jnp.zeros((back, 128), F32)
        ext[back:, cols] = masked
        conv_hidden(ext, taps, cols, 0, rows, hidden, conv_out, (HALO, HALO + frames + EDGE))
    own_hidden[...] = hidden[HALO : HALO + frames]
    for i, copy in enumerate(copies):
        copy.wait()
        low = HALO if i * wide < width else 0
        for col in range(i * wide, (i + 1) * wide, 512):
            cols = pl.ds(col, 512)
            qkv[low:rows, cols] = dot(hidden[low:], w_out[:, cols], 1, 0).astype(BF16)
    qkv[rows:, :] = jnp.zeros((qkv.shape[0] - rows, 3 * width), BF16)


def ends_kernel(place, both, f1, f2, f3, _, out):
    frames = f1.shape[0]
    out[:EDGE] = both[frames - EDGE : frames].astype(BF16)
    for slot, ref in ((1, f1), (2, f2), (3, f3)):
        out[slot * EDGE : (slot + 1) * EDGE] = ref[frames - EDGE :]


def peers_kernel(place, f1, f2, f3, tails, both, hidden, ext):
    frames, width = f1.shape
    taps = parts_of(both, frames)[2]
    count, chip, core = place[1], place[2], place[3]
    for slot, ref in ((1, f1), (2, f2), (3, f3)):
        peer = chip ^ slot
        begin = (2 * peer + core) * frames
        source = jnp.where(core == 1, slot, chip ^ jnp.maximum(peer - 1, 0))
        start = pl.multiple_of(source * EDGE, EDGE)
        live = live_rows(begin - EDGE, frames + EDGE, count)
        real = begin - EDGE + lax.broadcasted_iota(jnp.int32, (frames + EDGE, 128), 0) >= 0
        live = live & real
        for col in range(0, width, 128):
            cols = pl.ds(col, 128)
            raw = jnp.concatenate([tails[pl.ds(start, EDGE), cols], ref[:, cols]], axis=0)
            masked = jnp.where(live, raw.astype(F32), 0.0)
            ext[:, cols] = masked
            out = hidden.at[(slot - 1) * frames : slot * frames]
            conv_hidden(ext, taps, cols, EDGE - KERNEL + 1, frames, out)


def attend_kernel(place, qkv, both, near, far, attended, grads, sends, later):
    frames, width = attended.shape
    cot = parts_of(both, frames)[1]
    span = frames + HALO
    begin, count, chip = place[0], place[1], place[2]

    skip = (frames - LEFT) // EDGE * EDGE

    def mask(start, wanted):
        key = lax.broadcasted_iota(jnp.int32, (start + wanted, frames), 0)
        query = lax.broadcasted_iota(jnp.int32, (start + wanted, frames), 1)
        first = begin if wanted == frames else begin + frames
        gap = query + start - key
        seen = first + query - gap
        alive = (first + query < count) & (query < wanted)
        allowed = (gap >= 0) & (gap <= LEFT) & (seen >= 0) & alive
        return jnp.where(allowed, 0.0, -jnp.inf), jnp.where(alive[:1], 0.0, 1.0)

    masks = [mask(HALO, frames), mask(frames - skip, HALO)]
    row = lax.broadcasted_iota(jnp.int32, (frames, width), 0)
    after = jnp.where(place[3] == 0, near[HALO:].astype(F32), far[...].astype(F32))
    later[:HALO] = jnp.where(begin + frames + row[:HALO] < count, after, 0.0).astype(BF16)
    later[HALO:] = jnp.zeros((frames - HALO, width), BF16)
    factor = HEAD**-0.5

    def probs(scores, bias, missing):
        raised = jnp.exp(scores * factor + bias)
        return raised * (1.0 / (jnp.sum(raised, axis=0, keepdims=True) + missing))

    def slopes(prob, grad_prob):
        mean = jnp.sum(prob * grad_prob, axis=0, keepdims=True)
        return (prob * (grad_prob - mean) * factor).astype(BF16)

    own_live = begin + lax.broadcasted_iota(jnp.int32, (frames, HEAD), 0) < count
    lead, trail = jnp.zeros((skip, frames), BF16), jnp.zeros((EDGE, frames), BF16)

    def gather(own, late, rhs, rhs_late):
        left = jnp.concatenate([own[HALO:], trail], axis=0)
        right = jnp.concatenate([lead, late[: frames - skip + EDGE]], axis=0)
        left = jnp.concatenate([left, right], axis=1)
        return dot(left, jnp.concatenate([rhs, rhs_late], axis=0), 1, 0).astype(BF16)

    for first in range(0, HEADS, GROUP):
        heads = []
        for head in range(first, first + GROUP):
            q_cols = pl.ds(head * HEAD, HEAD)
            k_cols = pl.ds(width + head * HEAD, HEAD)
            v_cols = pl.ds(2 * width + head * HEAD, HEAD)
            query = qkv[HALO : HALO + frames, q_cols]
            query_b = qkv[HALO + frames : HALO + 2 * frames, q_cols]
            key, key_b = qkv[:span, k_cols], qkv[HALO + skip : HALO + span, k_cols]
            value, value_b = qkv[:span, v_cols], qkv[HALO + skip : HALO + span, v_cols]
            grad = jnp.where(own_live, cot[:, q_cols], 0.0).astype(BF16)
            grad_b = later[:, q_cols]
            heads.append((q_cols, k_cols, v_cols, query, query_b, key, key_b, value, grad, grad_b, value_b))
        scores = [
            (dot(h[5], h[3], 1, 1), dot(h[6], h[4], 1, 1), dot(h[7], h[8], 1, 1), dot(h[10], h[9], 1, 1))
            for h in heads
        ]
        prob = [(probs(s[0], *masks[0]), probs(s[1], *masks[1])) for s in scores]
        low = [(p[0].astype(BF16), p[1].astype(BF16)) for p in prob]
        slope = [(slopes(p[0], s[2]), slopes(p[1], s[3])) for p, s in zip(prob, scores)]
        for h, p, d in zip(heads, low, slope):
            q_cols, k_cols, v_cols, query, query_b, key, key_b, value, grad, grad_b, _ = h
            attended[:, q_cols] = dot(p[0], value, 0, 0).astype(BF16)
            grads[:frames, q_cols] = dot(d[0], key, 0, 0).astype(BF16)
            grads[frames:, q_cols] = dot(d[1][:, :EDGE], key_b, 0, 0).astype(BF16)
            grads[:, k_cols] = gather(d[0], d[1], query, query_b)
            grads[:, v_cols] = gather(p[0], p[1], grad, grad_b)
    if sends is None:
        return
    for k in range(4):
        slot = chip ^ k
        for i in range(4):
            block = 6 * i + k + (k + 1) // 2
            sends[slot, :, i * HEAD : (i + 1) * HEAD] = grads[:frames, pl.ds(block * HEAD, HEAD)]
        side = (k % 2) * (HEAD // 2)
        for pair in range(2):
            halves = []
            for i in (2 * pair, 2 * pair + 1):
                start = (6 * i + 1 + 3 * (k // 2)) * HEAD + side
                halves.append(grads[:frames, start : start + HEAD // 2])
            at = (4 + pair) * HEAD
            sends[slot, :, at : at + HEAD] = jnp.concatenate(halves, axis=1)


def attend_alone(place, qkv, both, near, far, attended, grads, later):
    attend_kernel(place, qkv, both, near, far, attended, grads, None, later)


def input_grad_kernel(place, grads, w, conv, both, *refs):
    grad_in, done, slopes = refs[-3:]
    frames, width = grad_in.shape
    taps = parts_of(both, frames)[2]
    begin, count = place[0], place[1]
    done[...] = jnp.zeros(done.shape, F32)
    live = begin + lax.broadcasted_iota(jnp.int32, (frames, 256), 0) < count
    for col in range(0, width, 256):
        cols = pl.ds(col, 256)
        grad_hidden = dot(grads[...], w[cols, :], 1, 1)
        value = conv[:, cols]
        logistic = 1.0 / (1.0 + jnp.exp(-value))
        slopes[:, cols] = grad_hidden * (logistic * (1.0 + value * (1.0 - logistic)))
        total = grad_hidden[:frames]
        for tap in range(KERNEL):
            low = KERNEL - 1 - tap
            total = total + taps[tap : tap + 1, cols] * slopes[low : low + frames, cols]
        grad_in[:, cols] = jnp.where(live, total, 0.0).astype(BF16)


def weight_kernel(mine, place, own, peers, b, b1, b2, b3, out):
    parity = place[3] if mine else 1 - place[3]
    left = jnp.concatenate([b[0], b1[...], b2[...], b3[...]], axis=0)
    right = jnp.concatenate(
        [jnp.concatenate([a[:, block(2 * k + parity)] for k in range(4)], axis=1) for a in (own, peers)],
        axis=0,
    )
    out[...] = dot(left, right, 0, 0).astype(out.dtype)


def block(index):
    return pl.ds(pl.multiple_of(index * HEAD, HEAD), HEAD)


def halves(place, value, same, other):
    bit = place[2] % 2
    for out, x in ((other, 1 - bit), (same, bit)):
        for y in range(2):
            out[:, y * HEAD : (y + 1) * HEAD] = value(block(2 * y + x)).astype(out.dtype)


def shard_rows(place, mask):
    i = place[4] ^ mask
    for at, size, base in ((0, HEAD, 0), (HEAD, HEAD // 2, 4 * HEAD)):
        rows = pl.ds(pl.multiple_of(base + i * size, size), size)
        yield rows, slice(at, at + size)


def core_sum_kernel(place, keep, got, near, ahead, *outs):
    for mask, out in ((2, near), (3, ahead)):
        for rows, at in shard_rows(place, mask):
            out[at] = (keep[rows] + got[rows].astype(F32)).astype(out.dtype)
    for mask, same, other in ((1, *outs[:2]), (0, *outs[2:])):
        for rows, at in shard_rows(place, mask):
            halves(
                place,
                lambda cols, rows=rows: keep[rows, cols] + got[rows, cols].astype(F32),
                same.at[at],
                other.at[at],
            )


def forward_kernel(place, ahead, got, same, other):
    halves(place, lambda cols: ahead[:, cols] + got[:, cols].astype(F32), same, other)


def mid_sum_kernel(place, s0, s1, s2, o0, o1, o2, _, keep, send):
    bit = place[2] // 2
    for out, y in ((send, 1 - bit), (keep, bit)):
        cols = block(y)
        for i, refs in enumerate(((s0, s1, s2), (o0, o1, o2))):
            a, b, c = (ref[:, cols].astype(F32) for ref in refs)
            out[i] = (a + b + c).astype(out.dtype)


def place_kernel(scale, place, keep, got, out):
    for slot, ref in enumerate((keep, keep, got, got)):
        value = ref[slot % 2].astype(F32) * scale
        k = place[2] ^ slot
        out[k + (k + 1) // 2] = value[:HEAD]
        start = pl.multiple_of((k % 2) * (HEAD // 2), HEAD // 2)
        out[1 + 3 * (k // 2), pl.ds(start, HEAD // 2)] = value[HEAD:]


def call(
    kernel, name, outs, place, operands, scratch=(), mib=16, flops=1000000, moved=1000000,
    remote=(), after=()
):
    return pl.pallas_call(
        kernel,
        name=name,
        out_shape=[jax.ShapeDtypeStruct(shape, dtype) for shape, dtype in outs],
        in_specs=[pl.BlockSpec(memory_space=pltpu.SMEM)]
        + vmem(len(operands))
        + [pl.BlockSpec(memory_space=pltpu.HBM)] * len(remote)
        + [pl.BlockSpec(memory_space=pl.ANY)] * len(after),
        out_specs=vmem(len(outs)),
        scratch_shapes=[pltpu.VMEM(*x) if isinstance(x, tuple) else x for x in scratch],
        compiler_params=params(mib),
        cost_estimate=cost(flops, moved),
    )(place, *operands, *remote, *after)


def swap(value, axis, mask):
    return lax.ppermute(value, axis, [(i, i ^ mask) for i in range(lax.axis_size(axis))])


def swap_both(value, dp_mask, tm_mask):
    recs = lax.axis_size("dp")
    count = lax.axis_size("tm") * recs
    pairs = [(i, (i // recs ^ tm_mask) * recs + (i % recs ^ dp_mask)) for i in range(count)]
    return lax.ppermute(value, ("tm", "dp"), pairs)


def on_device(frames_in, valid_frames, kernel, w_qkv, cotangent):
    record, cot = frames_in[0], cotangent[0]
    frames, width = record.shape
    span = frames + HALO
    parts, recs = lax.axis_size("tm"), lax.axis_size("dp")
    me = lax.axis_index("tm")
    place = jnp.stack(
        [me * frames, valid_frames[0], me // 2, me % 2, lax.axis_index("dp")]
    ).astype(jnp.int32)
    split = parts == 8 and recs == 4
    both = lax.optimization_barrier(
        jnp.concatenate([record.astype(F32), cot.astype(F32), kernel], axis=0)
    )
    own = both[:frames].astype(BF16)
    last, first = own[frames - HALO :], own[:HALO]
    first_cot = both[frames : frames + HALO].astype(BF16)
    low_core = me % 2 == 0
    edge = jnp.where(low_core, last, first)
    near = swap(jnp.concatenate([edge, first_cot], axis=0), "tm", 1)
    down = [(i, i - 1) for i in range(2, parts, 2)]
    far = lax.ppermute(
        jnp.where(low_core, first, last), "tm", down + [(i, j) for j, i in down]
    )
    far_cot = lax.ppermute(first_cot, "tm", down)
    if split:
        peers = [swap(own, "tm", mask) for mask in (2, 4, 6)]
    rows = frames + 2 * HALO
    hidden, conv, qkv, w_near = call(
        project_kernel,
        "project",
        [
            ((frames, width), BF16),
            ((frames + EDGE, width), F32),
            ((HALO + 2 * frames, 3 * width), BF16),
            (w_qkv.shape, BF16),
        ],
        place,
        [near, far, both],
        [
            ((rows + KERNEL - 1, width), F32),
            ((rows, width), BF16),
            pltpu.SemaphoreType.DMA((3,)),
        ],
        flops=rows * width * 3 * width * 2,
        moved=9000000,
        remote=[w_qkv],
        mib=OWN,
    )
    outs = [((frames, width), BF16), ((frames + EDGE, 3 * width), BF16)]
    attended, grads, *sends = call(
        attend_kernel if split else attend_alone,
        "attend",
        outs + [((4, frames, 3 * width // 4), BF16)] * split,
        place,
        [qkv, both, near, far_cot],
        [((frames, width), BF16)],
        mib=16,
        flops=8 * 12 * span * 128 * 128 * 2 * 8,
        moved=5000000,
    )
    if split:
        sends = sends[0]
        got = [swap(sends[slot], "tm", 2 * slot) for slot in (1, 2, 3)]
    scale = float(recs * parts * frames) ** (-0.5)
    if split:
        cols = 3 * width // 4
        shard = cols // 4
        (ends,) = call(
            ends_kernel, "ends", [((4 * EDGE, width), BF16)], place, [both, *peers], after=[grads]
        )
        (peers_hidden,) = call(
            peers_kernel,
            "peer_hidden",
            [((3 * frames, width), BF16)],
            place,
            [*peers, swap(ends, "tm", 1), both],
            [((frames + EDGE, width), F32)],
            flops=3 * frames * width * 40,
            moved=2000000,
        )
        operands = [hidden, peers_hidden, sends, *got]
        whole, half = (shard, width // 2), (shard, 2 * HEAD)
        send, keep = (
            call(
                functools.partial(weight_kernel, mine),
                "weight_" + ("keep" if mine else "send"),
                [((cols, width // 2), F32 if mine else BF16)],
                place,
                operands,
                mib=20,
                flops=cols * width * frames * 4,
                moved=6000000,
            )[0]
            for mine in (False, True)
        )
        near, ahead, cross_same, cross_other, own_same, own_other = call(
            core_sum_kernel,
            "core_sum",
            [(whole, BF16), (whole, F32), (half, BF16), (half, BF16), (half, F32), (half, BF16)],
            place,
            [keep, swap(send, "tm", 1)],
        )
        late = [near]
        grad_in, done = call(
            input_grad_kernel,
            "input_grad",
            [((frames, width), BF16), ((8, 128), F32)],
            place,
            [grads, w_near, conv, both],
            [((frames + EDGE, width), F32)],
            mib=20,
            flops=(frames + EDGE) * width * 3 * width * 2,
            moved=9000000,
            after=late,
        )
        got_near = swap(near, "dp", 1)
        got_cross = swap(cross_same, "dp", 1), swap_both(cross_other, 1, 2)
        got_own = swap(own_other, "tm", 2)
        same, other = call(
            forward_kernel, "forward", [(half, BF16)] * 2, place, [ahead, got_near]
        )
        got_sums = swap(same, "dp", 3), swap_both(other, 3, 2)
        keep, send = call(
            mid_sum_kernel,
            "mid_sum",
            [((2, shard, HEAD), F32), ((2, shard, HEAD), BF16)],
            place,
            [own_same, got_cross[0], got_sums[0], got_own, got_cross[1], got_sums[1]],
            after=[done],
        )
        (qkv_grad,) = call(
            functools.partial(place_kernel, scale),
            "place",
            [((3 * HEADS // 4, HEAD, HEAD), F32)],
            place,
            [keep, swap(send, "tm", 4)],
        )
    else:
        late = []
        grad_in, done = call(
            input_grad_kernel,
            "input_grad",
            [((frames, width), BF16), ((8, 128), F32)],
            place,
            [grads, w_near, conv, both],
            [((frames + EDGE, width), F32)],
            mib=20,
            flops=(frames + EDGE) * width * 3 * width * 2,
            moved=9000000,
            after=late,
        )
        partial = dot(hidden, grads[:frames], 0, 0).astype(BF16)
        by_time = lax.psum_scatter(partial, "tm", scatter_dimension=0, tiled=True)
        summed = lax.psum_scatter(by_time, "dp", scatter_dimension=1, tiled=True).astype(F32)
        qkv_grad = summed.reshape(summed.shape[0], -1, HEAD).transpose(1, 2, 0) * scale
    return (attended[None], grad_in[None], qkv_grad)


def solution(mesh):
    return jax.shard_map(
        on_device,
        mesh=mesh,
        in_specs=(P("dp", "tm", None), P("dp"), P(), P(), P("dp", "tm", None)),
        out_specs=(P("dp", "tm", None), P("dp", "tm", None), P("dp", None, "tm")),
        check_vma=False,
    )
```

```python
import functools

import jax
import jax.numpy as jnp
from jax import lax
from jax.experimental import pallas as pl
from jax.experimental.pallas import tpu as pltpu
from jax.sharding import PartitionSpec as P

HEADS = 8
HEAD = 128
KERNEL = 9
LEFT = 70
HALO = 80
EDGE = 16
MIB = 1024 * 1024
OWN = 42
CHUNK = 48
GROUP = 4
F32 = jnp.float32
BF16 = jnp.bfloat16


def params(mib):
    return pltpu.CompilerParams(vmem_limit_bytes=mib * MIB)


def vmem(count):
    return [pl.BlockSpec(memory_space=pltpu.VMEM)] * count


def cost(flops, moved):
    return pl.CostEstimate(flops=flops, bytes_accessed=moved, transcendentals=0)


def dot(a, b, left, right):
    return lax.dot_general(a, b, (((left,), (right,)), ((), ())), preferred_element_type=F32)


def conv_hidden(ext, taps, cols, low, rows, hidden, conv_out=None, keep=(0, 0)):
    weights = [taps[tap : tap + 1, cols] for tap in range(KERNEL)]
    for start in range(0, rows, CHUNK):
        size = min(CHUNK, rows - start)
        at = low + start
        conv = weights[0] * ext[at : at + size, cols]
        for tap in range(1, KERNEL):
            conv = conv + weights[tap] * ext[at + tap : at + tap + size, cols]
        masked = ext[at + KERNEL - 1 : at + KERNEL - 1 + size, cols]
        hidden[start : start + size, cols] = (masked + conv / (1.0 + jnp.exp(-conv))).astype(BF16)
        first, last = max(start, keep[0]), min(start + size, keep[1])
        if first < last:
            conv_out[first - keep[0] : last - keep[0], cols] = conv[first - start : last - start]


def live_rows(first, rows, count):
    return first + lax.broadcasted_iota(jnp.int32, (rows, 128), 0) < count


def parts_of(both, frames):
    return both.at[:frames], both.at[frames : 2 * frames], both.at[2 * frames :]


def project_kernel(place, near, far, both, w, own_hidden, conv_out, qkv, w_out, ext, hidden, sems):
    frames, width = own_hidden.shape
    wide = width
    copies = [
        pltpu.make_async_copy(w.at[:, cols], w_out.at[:, cols], sems.at[i])
        for i, cols in enumerate(pl.ds(i * wide, wide) for i in range(3))
    ]
    for copy in copies:
        copy.start()
    own, _, taps = parts_of(both, frames)
    low_core = place[3] == 0
    rows, back = frames + 2 * HALO, KERNEL - 1
    live = live_rows(place[0] - HALO, rows, place[1])
    for col in range(0, width, 128):
        cols = pl.ds(col, 128)
        mate, other = near[:HALO, cols].astype(F32), far[:, cols].astype(F32)
        before, after = jnp.where(low_core, other, mate), jnp.where(low_core, mate, other)
        raw = jnp.concatenate([before, own[:, cols], after], axis=0)
        masked = jnp.where(live, raw, 0.0)
        ext[:back, cols] = jnp.zeros((back, 128), F32)
        ext[back:, cols] = masked
        conv_hidden(ext, taps, cols, 0, rows, hidden, conv_out, (HALO, HALO + frames + EDGE))
    own_hidden[...] = hidden[HALO : HALO + frames]
    for i, copy in enumerate(copies):
        copy.wait()
        low = HALO if i * wide < width else 0
        for col in range(i * wide, (i + 1) * wide, 512):
            cols = pl.ds(col, 512)
            qkv[low:rows, cols] = dot(hidden[low:], w_out[:, cols], 1, 0).astype(BF16)
    qkv[rows:, :] = jnp.zeros((qkv.shape[0] - rows, 3 * width), BF16)


def ends_kernel(place, both, f1, f2, f3, _, out):
    frames = f1.shape[0]
    out[:EDGE] = both[frames - EDGE : frames].astype(BF16)
    for slot, ref in ((1, f1), (2, f2), (3, f3)):
        out[slot * EDGE : (slot + 1) * EDGE] = ref[frames - EDGE :]


def peers_kernel(place, f1, f2, f3, tails, both, hidden, ext):
    frames, width = f1.shape
    taps = parts_of(both, frames)[2]
    count, chip, core = place[1], place[2], place[3]
    for slot, ref in ((1, f1), (2, f2), (3, f3)):
        peer = chip ^ slot
        begin = (2 * peer + core) * frames
        source = jnp.where(core == 1, slot, chip ^ jnp.maximum(peer - 1, 0))
        start = pl.multiple_of(source * EDGE, EDGE)
        live = live_rows(begin - EDGE, frames + EDGE, count)
        real = begin - EDGE + lax.broadcasted_iota(jnp.int32, (frames + EDGE, 128), 0) >= 0
        live = live & real
        for col in range(0, width, 128):
            cols = pl.ds(col, 128)
            raw = jnp.concatenate([tails[pl.ds(start, EDGE), cols], ref[:, cols]], axis=0)
            masked = jnp.where(live, raw.astype(F32), 0.0)
            ext[:, cols] = masked
            out = hidden.at[(slot - 1) * frames : slot * frames]
            conv_hidden(ext, taps, cols, EDGE - KERNEL + 1, frames, out)


def attend_kernel(place, qkv, both, near, far, attended, grads, sends, later):
    frames, width = attended.shape
    cot = parts_of(both, frames)[1]
    span = frames + HALO
    begin, count, chip = place[0], place[1], place[2]

    skip = (frames - LEFT) // EDGE * EDGE

    def mask(start, wanted):
        key = lax.broadcasted_iota(jnp.int32, (start + wanted, frames), 0)
        query = lax.broadcasted_iota(jnp.int32, (start + wanted, frames), 1)
        first = begin if wanted == frames else begin + frames
        gap = query + start - key
        seen = first + query - gap
        alive = (first + query < count) & (query < wanted)
        allowed = (gap >= 0) & (gap <= LEFT) & (seen >= 0) & alive
        return jnp.where(allowed, 0.0, -jnp.inf), jnp.where(alive[:1], 0.0, 1.0)

    masks = [mask(HALO, frames), mask(frames - skip, HALO)]
    row = lax.broadcasted_iota(jnp.int32, (frames, width), 0)
    after = jnp.where(place[3] == 0, near[HALO:].astype(F32), far[...].astype(F32))
    later[:HALO] = jnp.where(begin + frames + row[:HALO] < count, after, 0.0).astype(BF16)
    later[HALO:] = jnp.zeros((frames - HALO, width), BF16)
    factor = HEAD**-0.5

    def probs(scores, bias, missing):
        raised = jnp.exp(scores * factor + bias)
        return raised * (1.0 / (jnp.sum(raised, axis=0, keepdims=True) + missing))

    def slopes(prob, grad_prob):
        mean = jnp.sum(prob * grad_prob, axis=0, keepdims=True)
        return (prob * (grad_prob - mean) * factor).astype(BF16)

    own_live = begin + lax.broadcasted_iota(jnp.int32, (frames, HEAD), 0) < count
    lead, trail = jnp.zeros((skip, frames), BF16), jnp.zeros((EDGE, frames), BF16)

    def gather(own, late, rhs, rhs_late):
        left = jnp.concatenate([own[HALO:], trail], axis=0)
        right = jnp.concatenate([lead, late[: frames - skip + EDGE]], axis=0)
        left = jnp.concatenate([left, right], axis=1)
        return dot(left, jnp.concatenate([rhs, rhs_late], axis=0), 1, 0).astype(BF16)

    for first in range(0, HEADS, GROUP):
        heads = []
        for head in range(first, first + GROUP):
            q_cols = pl.ds(head * HEAD, HEAD)
            k_cols = pl.ds(width + head * HEAD, HEAD)
            v_cols = pl.ds(2 * width + head * HEAD, HEAD)
            query = qkv[HALO : HALO + frames, q_cols]
            query_b = qkv[HALO + frames : HALO + 2 * frames, q_cols]
            key, key_b = qkv[:span, k_cols], qkv[HALO + skip : HALO + span, k_cols]
            value, value_b = qkv[:span, v_cols], qkv[HALO + skip : HALO + span, v_cols]
            grad = jnp.where(own_live, cot[:, q_cols], 0.0).astype(BF16)
            grad_b = later[:, q_cols]
            heads.append((q_cols, k_cols, v_cols, query, query_b, key, key_b, value, grad, grad_b, value_b))
        scores = [
            (dot(h[5], h[3], 1, 1), dot(h[6], h[4], 1, 1), dot(h[7], h[8], 1, 1), dot(h[10], h[9], 1, 1))
            for h in heads
        ]
        prob = [(probs(s[0], *masks[0]), probs(s[1], *masks[1])) for s in scores]
        low = [(p[0].astype(BF16), p[1].astype(BF16)) for p in prob]
        slope = [(slopes(p[0], s[2]), slopes(p[1], s[3])) for p, s in zip(prob, scores)]
        for h, p, d in zip(heads, low, slope):
            q_cols, k_cols, v_cols, query, query_b, key, key_b, value, grad, grad_b, _ = h
            attended[:, q_cols] = dot(p[0], value, 0, 0).astype(BF16)
            grads[:frames, q_cols] = dot(d[0], key, 0, 0).astype(BF16)
            grads[frames:, q_cols] = dot(d[1][:, :EDGE], key_b, 0, 0).astype(BF16)
            grads[:, k_cols] = gather(d[0], d[1], query, query_b)
            grads[:, v_cols] = gather(p[0], p[1], grad, grad_b)
    if sends is None:
        return
    for k in range(4):
        slot = chip ^ k
        for i in range(4):
            block = 6 * i + k + (k + 1) // 2
            sends[slot, :, i * HEAD : (i + 1) * HEAD] = grads[:frames, pl.ds(block * HEAD, HEAD)]
        side = (k % 2) * (HEAD // 2)
        for pair in range(2):
            halves = []
            for i in (2 * pair, 2 * pair + 1):
                start = (6 * i + 1 + 3 * (k // 2)) * HEAD + side
                halves.append(grads[:frames, start : start + HEAD // 2])
            at = (4 + pair) * HEAD
            sends[slot, :, at : at + HEAD] = jnp.concatenate(halves, axis=1)


def attend_alone(place, qkv, both, near, far, attended, grads, later):
    attend_kernel(place, qkv, both, near, far, attended, grads, None, later)


def input_grad_kernel(place, grads, w, conv, both, *refs):
    grad_in, done, slopes = refs[-3:]
    frames, width = grad_in.shape
    taps = parts_of(both, frames)[2]
    begin, count = place[0], place[1]
    done[...] = jnp.zeros(done.shape, F32)
    live = begin + lax.broadcasted_iota(jnp.int32, (frames, 256), 0) < count
    for col in range(0, width, 256):
        cols = pl.ds(col, 256)
        grad_hidden = dot(grads[...], w[cols, :], 1, 1)
        value = conv[:, cols]
        logistic = 1.0 / (1.0 + jnp.exp(-value))
        slopes[:, cols] = grad_hidden * (logistic * (1.0 + value * (1.0 - logistic)))
        total = grad_hidden[:frames]
        for tap in range(KERNEL):
            low = KERNEL - 1 - tap
            total = total + taps[tap : tap + 1, cols] * slopes[low : low + frames, cols]
        grad_in[:, cols] = jnp.where(live, total, 0.0).astype(BF16)


def weight_kernel(mine, place, own, peers, b, b1, b2, b3, out):
    parity = place[3] if mine else 1 - place[3]
    left = jnp.concatenate([b[0], b1[...], b2[...], b3[...]], axis=0)
    right = jnp.concatenate(
        [jnp.concatenate([a[:, block(2 * k + parity)] for k in range(4)], axis=1) for a in (own, peers)],
        axis=0,
    )
    out[...] = dot(left, right, 0, 0).astype(out.dtype)


def block(index):
    return pl.ds(pl.multiple_of(index * HEAD, HEAD), HEAD)


def halves(place, value, same, other):
    bit = place[2] % 2
    for out, x in ((other, 1 - bit), (same, bit)):
        for y in range(2):
            out[:, y * HEAD : (y + 1) * HEAD] = value(block(2 * y + x)).astype(out.dtype)


def shard_rows(place, mask):
    i = place[4] ^ mask
    for at, size, base in ((0, HEAD, 0), (HEAD, HEAD // 2, 4 * HEAD)):
        rows = pl.ds(pl.multiple_of(base + i * size, size), size)
        yield rows, slice(at, at + size)


def core_sum_kernel(place, keep, got, near, ahead, *outs):
    for mask, out in ((2, near), (3, ahead)):
        for rows, at in shard_rows(place, mask):
            out[at] = (keep[rows] + got[rows].astype(F32)).astype(out.dtype)
    for mask, same, other in ((1, *outs[:2]), (0, *outs[2:])):
        for rows, at in shard_rows(place, mask):
            halves(
                place,
                lambda cols, rows=rows: keep[rows, cols] + got[rows, cols].astype(F32),
                same.at[at],
                other.at[at],
            )


def forward_kernel(place, ahead, got, same, other):
    halves(place, lambda cols: ahead[:, cols] + got[:, cols].astype(F32), same, other)


def mid_sum_kernel(same, place, moved, kept, cross, sums, *refs):
    keep, send = refs[-2:]
    own = kept if same else moved
    bit = place[2] // 2
    for out, y in ((send, 1 - bit), (keep, bit)):
        cols = block(y)
        a, b, c = (ref[:, cols].astype(F32) for ref in (own, cross, sums))
        out[...] = (a + b + c).astype(out.dtype)


def place_kernel(scale, place, k0, k1, g0, g1, out):
    for slot, ref in enumerate((k0, k1, g0, g1)):
        value = ref[...].astype(F32) * scale
        k = place[2] ^ slot
        out[k + (k + 1) // 2] = value[:HEAD]
        start = pl.multiple_of((k % 2) * (HEAD // 2), HEAD // 2)
        out[1 + 3 * (k // 2), pl.ds(start, HEAD // 2)] = value[HEAD:]


def call(
    kernel, name, outs, place, operands, scratch=(), mib=16, flops=1000000, moved=1000000,
    remote=(), after=()
):
    def placed(*refs):
        begin, left, *rest = (ref[0] for ref in refs[: len(place)])
        kernel((begin, begin + left, *rest), *refs[len(place) :])

    return pl.pallas_call(
        placed,
        name=name,
        out_shape=[jax.ShapeDtypeStruct(shape, dtype) for shape, dtype in outs],
        in_specs=[pl.BlockSpec(memory_space=pltpu.SMEM)] * len(place)
        + vmem(len(operands))
        + [pl.BlockSpec(memory_space=pltpu.HBM)] * len(remote)
        + [pl.BlockSpec(memory_space=pl.ANY)] * len(after),
        out_specs=vmem(len(outs)),
        scratch_shapes=[pltpu.VMEM(*x) if isinstance(x, tuple) else x for x in scratch],
        compiler_params=params(mib),
        cost_estimate=cost(flops, moved),
    )(*place, *operands, *remote, *after)


def swap(value, axis, mask):
    return lax.ppermute(value, axis, [(i, i ^ mask) for i in range(lax.axis_size(axis))])


def swap_both(value, dp_mask, tm_mask):
    recs = lax.axis_size("dp")
    count = lax.axis_size("tm") * recs
    pairs = [(i, (i // recs ^ tm_mask) * recs + (i % recs ^ dp_mask)) for i in range(count)]
    return lax.ppermute(value, ("tm", "dp"), pairs)


def on_device(frames_in, valid_frames, kernel, w_qkv, cotangent):
    record, cot = frames_in[0], cotangent[0]
    frames, width = record.shape
    span = frames + HALO
    parts, recs = lax.axis_size("tm"), lax.axis_size("dp")
    me = lax.axis_index("tm")
    begin = me * frames
    place = [
        jnp.reshape(x, (1,)).astype(jnp.int32)
        for x in (begin, valid_frames[0] - begin, me // 2, me % 2, lax.axis_index("dp"))
    ]
    split = parts == 8 and recs == 4
    both = lax.optimization_barrier(
        jnp.concatenate([record.astype(F32), cot.astype(F32), kernel], axis=0)
    )
    own = both[:frames].astype(BF16)
    last, first = own[frames - HALO :], own[:HALO]
    first_cot = both[frames : frames + HALO].astype(BF16)
    low_core = me % 2 == 0
    edge = jnp.where(low_core, last, first)
    near = swap(jnp.concatenate([edge, first_cot], axis=0), "tm", 1)
    down = [(i, i - 1) for i in range(2, parts, 2)]
    far = lax.ppermute(
        jnp.where(low_core, first, last), "tm", down + [(i, j) for j, i in down]
    )
    far_cot = lax.ppermute(first_cot, "tm", down)
    if split:
        peers = [swap(own, "tm", mask) for mask in (2, 4, 6)]
    rows = frames + 2 * HALO
    hidden, conv, qkv, w_near = call(
        project_kernel,
        "project",
        [
            ((frames, width), BF16),
            ((frames + EDGE, width), F32),
            ((HALO + 2 * frames, 3 * width), BF16),
            (w_qkv.shape, BF16),
        ],
        place,
        [near, far, both],
        [
            ((rows + KERNEL - 1, width), F32),
            ((rows, width), BF16),
            pltpu.SemaphoreType.DMA((3,)),
        ],
        flops=rows * width * 3 * width * 2,
        moved=9000000,
        remote=[w_qkv],
        mib=OWN,
    )
    outs = [((frames, width), BF16), ((frames + EDGE, 3 * width), BF16)]
    attended, grads, *sends = call(
        attend_kernel if split else attend_alone,
        "attend",
        outs + [((4, frames, 3 * width // 4), BF16)] * split,
        place,
        [qkv, both, near, far_cot],
        [((frames, width), BF16)],
        mib=16,
        flops=8 * 12 * span * 128 * 128 * 2 * 8,
        moved=5000000,
    )
    if split:
        sends = sends[0]
        got = [swap(sends[slot], "tm", 2 * slot) for slot in (1, 2, 3)]
    scale = float(recs * parts * frames) ** (-0.5)
    if split:
        cols = 3 * width // 4
        shard = cols // 4
        (ends,) = call(
            ends_kernel, "ends", [((4 * EDGE, width), BF16)], place, [both, *peers], after=[grads]
        )
        (peers_hidden,) = call(
            peers_kernel,
            "peer_hidden",
            [((3 * frames, width), BF16)],
            place,
            [*peers, swap(ends, "tm", 1), both],
            [((frames + EDGE, width), F32)],
            flops=3 * frames * width * 40,
            moved=2000000,
        )
        operands = [hidden, peers_hidden, sends, *got]
        whole, half = (shard, width // 2), (shard, 2 * HEAD)
        send, keep = (
            call(
                functools.partial(weight_kernel, mine),
                "weight_" + ("keep" if mine else "send"),
                [((cols, width // 2), F32 if mine else BF16)],
                place,
                operands,
                mib=20,
                flops=cols * width * frames * 4,
                moved=6000000,
            )[0]
            for mine in (False, True)
        )
        near, ahead, cross_same, cross_other, own_same, own_other = call(
            core_sum_kernel,
            "core_sum",
            [(whole, BF16), (whole, F32), (half, BF16), (half, BF16), (half, F32), (half, BF16)],
            place,
            [keep, swap(send, "tm", 1)],
        )
        late = [near]
        grad_in, done = call(
            input_grad_kernel,
            "input_grad",
            [((frames, width), BF16), ((8, 128), F32)],
            place,
            [grads, w_near, conv, both],
            [((frames + EDGE, width), F32)],
            mib=20,
            flops=(frames + EDGE) * width * 3 * width * 2,
            moved=9000000,
            after=late,
        )
        got_near = swap(near, "dp", 1)
        got_cross = swap(cross_same, "dp", 1), swap_both(cross_other, 1, 2)
        got_own = swap(own_other, "tm", 2)
        same, other = call(
            forward_kernel, "forward", [(half, BF16)] * 2, place, [ahead, got_near]
        )
        got_sums = swap(same, "dp", 3), swap_both(other, 3, 2)
        kept, moved = [], []
        early = [got_cross[1], done]
        for i, name in enumerate(("same", "other")):
            keep, send = call(
                functools.partial(mid_sum_kernel, i == 0),
                "mid_" + name,
                [((shard, HEAD), F32), ((shard, HEAD), BF16)],
                place,
                [got_own, own_same, got_cross[i], got_sums[i]],
                after=early,
            )
            kept.append(keep)
            moved.append(swap(send, "tm", 4))
        (qkv_grad,) = call(
            functools.partial(place_kernel, scale),
            "place",
            [((3 * HEADS // 4, HEAD, HEAD), F32)],
            place,
            [*kept, *moved],
        )
    else:
        late = []
        grad_in, done = call(
            input_grad_kernel,
            "input_grad",
            [((frames, width), BF16), ((8, 128), F32)],
            place,
            [grads, w_near, conv, both],
            [((frames + EDGE, width), F32)],
            mib=20,
            flops=(frames + EDGE) * width * 3 * width * 2,
            moved=9000000,
            after=late,
        )
        partial = dot(hidden, grads[:frames], 0, 0).astype(BF16)
        by_time = lax.psum_scatter(partial, "tm", scatter_dimension=0, tiled=True)
        summed = lax.psum_scatter(by_time, "dp", scatter_dimension=1, tiled=True).astype(F32)
        qkv_grad = summed.reshape(summed.shape[0], -1, HEAD).transpose(1, 2, 0) * scale
    return (attended[None], grad_in[None], qkv_grad)


def solution(mesh):
    return jax.shard_map(
        on_device,
        mesh=mesh,
        in_specs=(P("dp", "tm", None), P("dp"), P(), P(), P("dp", "tm", None)),
        out_specs=(P("dp", "tm", None), P("dp", "tm", None), P("dp", None, "tm")),
        check_vma=False,
    )
```

```python
import functools

import jax
import jax.numpy as jnp
from jax import lax
from jax.experimental import pallas as pl
from jax.experimental.pallas import tpu as pltpu
from jax.sharding import PartitionSpec as P

HEADS = 8
HEAD = 128
KERNEL = 9
LEFT = 70
HALO = 80
EDGE = 16
MIB = 1024 * 1024
OWN = 42
CHUNK = 48
GROUP = 4
F32 = jnp.float32
BF16 = jnp.bfloat16


def params(mib):
    return pltpu.CompilerParams(vmem_limit_bytes=mib * MIB)


def vmem(count):
    return [pl.BlockSpec(memory_space=pltpu.VMEM)] * count


def cost(flops, moved):
    return pl.CostEstimate(flops=flops, bytes_accessed=moved, transcendentals=0)


def dot(a, b, left, right):
    return lax.dot_general(a, b, (((left,), (right,)), ((), ())), preferred_element_type=F32)


def conv_hidden(ext, taps, cols, low, rows, hidden, conv_out=None, keep=(0, 0)):
    weights = [taps[tap : tap + 1, cols] for tap in range(KERNEL)]
    for start in range(0, rows, CHUNK):
        size = min(CHUNK, rows - start)
        at = low + start
        conv = weights[0] * ext[at : at + size, cols]
        for tap in range(1, KERNEL):
            conv = conv + weights[tap] * ext[at + tap : at + tap + size, cols]
        masked = ext[at + KERNEL - 1 : at + KERNEL - 1 + size, cols]
        hidden[start : start + size, cols] = (masked + conv / (1.0 + jnp.exp(-conv))).astype(BF16)
        first, last = max(start, keep[0]), min(start + size, keep[1])
        if first < last:
            conv_out[first - keep[0] : last - keep[0], cols] = conv[first - start : last - start]


def live_rows(first, rows, count):
    return first + lax.broadcasted_iota(jnp.int32, (rows, 128), 0) < count


def parts_of(both, frames):
    return both.at[:frames], both.at[frames : 2 * frames], both.at[2 * frames :]


def project_kernel(place, near, far, both, w, _, own_hidden, conv_out, qkv, w_out, *scratch):
    frames, width = own_hidden.shape
    ext, hidden, sems = scratch
    wide = width
    copies = [
        pltpu.make_async_copy(w.at[:, cols], w_out.at[:, cols], sems.at[i])
        for i, cols in enumerate(pl.ds(i * wide, wide) for i in range(3))
    ]
    for copy in copies:
        copy.start()
    own, _, taps = parts_of(both, frames)
    low_core = place[3] == 0
    rows, back = frames + 2 * HALO, KERNEL - 1
    live = live_rows(place[0] - HALO, rows, place[1]) & ~live_rows(place[0] - HALO, rows, 0)
    for col in range(0, width, 128):
        cols = pl.ds(col, 128)
        mate, other = near[:, cols].astype(F32), far[:, cols].astype(F32)
        before, after = jnp.where(low_core, other, mate), jnp.where(low_core, mate, other)
        raw = jnp.concatenate([before, own[:, cols], after], axis=0)
        masked = jnp.where(live, raw, 0.0)
        ext[:back, cols] = jnp.zeros((back, 128), F32)
        ext[back:, cols] = masked
        conv_hidden(ext, taps, cols, 0, rows, hidden, conv_out, (HALO, HALO + frames + EDGE))
    own_hidden[...] = hidden[HALO : HALO + frames]
    for i, copy in enumerate(copies):
        copy.wait()
        low = HALO if i * wide < width else 0
        for col in range(i * wide, (i + 1) * wide, 512):
            cols = pl.ds(col, 512)
            qkv[low:rows, cols] = dot(hidden[low:], w_out[:, cols], 1, 0).astype(BF16)
    qkv[rows:, :] = jnp.zeros((qkv.shape[0] - rows, 3 * width), BF16)


def ends_kernel(place, both, f1, f2, f3, _, out):
    frames = f1.shape[0]
    out[:EDGE] = both[frames - EDGE : frames].astype(BF16)
    for slot, ref in ((1, f1), (2, f2), (3, f3)):
        out[slot * EDGE : (slot + 1) * EDGE] = ref[frames - EDGE :]


def peers_kernel(place, f1, f2, f3, tails, both, hidden, ext):
    frames, width = f1.shape
    taps = parts_of(both, frames)[2]
    count, chip, core = place[1], place[2], place[3]
    for slot, ref in ((1, f1), (2, f2), (3, f3)):
        peer = chip ^ slot
        begin = (2 * peer + core) * frames
        source = jnp.where(core == 1, slot, chip ^ jnp.maximum(peer - 1, 0))
        start = pl.multiple_of(source * EDGE, EDGE)
        live = live_rows(begin - EDGE, frames + EDGE, count)
        real = begin - EDGE + lax.broadcasted_iota(jnp.int32, (frames + EDGE, 128), 0) >= 0
        live = live & real
        for col in range(0, width, 128):
            cols = pl.ds(col, 128)
            raw = jnp.concatenate([tails[pl.ds(start, EDGE), cols], ref[:, cols]], axis=0)
            masked = jnp.where(live, raw.astype(F32), 0.0)
            ext[:, cols] = masked
            out = hidden.at[(slot - 1) * frames : slot * frames]
            conv_hidden(ext, taps, cols, EDGE - KERNEL + 1, frames, out)


def attend_kernel(place, qkv, both, next_cot, attended, grads, sends, later):
    frames, width = attended.shape
    cot = parts_of(both, frames)[1]
    span = frames + HALO
    begin, count, chip = place[0], place[1], place[2]

    skip = (frames - LEFT) // EDGE * EDGE

    def mask(start, wanted):
        key = lax.broadcasted_iota(jnp.int32, (start + wanted, frames), 0)
        query = lax.broadcasted_iota(jnp.int32, (start + wanted, frames), 1)
        first = begin if wanted == frames else begin + frames
        gap = query + start - key
        seen = first + query - gap
        alive = (first + query < count) & (query < wanted)
        allowed = (gap >= 0) & (gap <= LEFT) & (seen >= 0) & alive
        return jnp.where(allowed, 0.0, -jnp.inf), jnp.where(alive[:1], 0.0, 1.0)

    masks = [mask(HALO, frames), mask(frames - skip, HALO)]
    row = lax.broadcasted_iota(jnp.int32, (frames, width), 0)
    after = next_cot[...].astype(F32)
    later[:HALO] = jnp.where(begin + frames + row[:HALO] < count, after, 0.0).astype(BF16)
    later[HALO:] = jnp.zeros((frames - HALO, width), BF16)
    factor = HEAD**-0.5

    def probs(scores, bias, missing):
        raised = jnp.exp(scores * factor + bias)
        return raised * (1.0 / (jnp.sum(raised, axis=0, keepdims=True) + missing))

    def slopes(prob, grad_prob):
        mean = jnp.sum(prob * grad_prob, axis=0, keepdims=True)
        return (prob * (grad_prob - mean) * factor).astype(BF16)

    own_live = begin + lax.broadcasted_iota(jnp.int32, (frames, HEAD), 0) < count
    lead, trail = jnp.zeros((skip, frames), BF16), jnp.zeros((EDGE, frames), BF16)

    def gather(own, late, rhs, rhs_late):
        left = jnp.concatenate([own[HALO:], trail], axis=0)
        right = jnp.concatenate([lead, late[: frames - skip + EDGE]], axis=0)
        left = jnp.concatenate([left, right], axis=1)
        return dot(left, jnp.concatenate([rhs, rhs_late], axis=0), 1, 0).astype(BF16)

    for first in range(0, HEADS, GROUP):
        heads = []
        for head in range(first, first + GROUP):
            q_cols = pl.ds(head * HEAD, HEAD)
            k_cols = pl.ds(width + head * HEAD, HEAD)
            v_cols = pl.ds(2 * width + head * HEAD, HEAD)
            query = qkv[HALO : HALO + frames, q_cols]
            query_b = qkv[HALO + frames : HALO + 2 * frames, q_cols]
            key, key_b = qkv[:span, k_cols], qkv[HALO + skip : HALO + span, k_cols]
            value, value_b = qkv[:span, v_cols], qkv[HALO + skip : HALO + span, v_cols]
            grad = jnp.where(own_live, cot[:, q_cols], 0.0).astype(BF16)
            grad_b = later[:, q_cols]
            heads.append((q_cols, k_cols, v_cols, query, query_b, key, key_b, value, grad, grad_b, value_b))
        scores = [
            (dot(h[5], h[3], 1, 1), dot(h[6], h[4], 1, 1), dot(h[7], h[8], 1, 1), dot(h[10], h[9], 1, 1))
            for h in heads
        ]
        prob = [(probs(s[0], *masks[0]), probs(s[1], *masks[1])) for s in scores]
        low = [(p[0].astype(BF16), p[1].astype(BF16)) for p in prob]
        slope = [(slopes(p[0], s[2]), slopes(p[1], s[3])) for p, s in zip(prob, scores)]
        for h, p, d in zip(heads, low, slope):
            q_cols, k_cols, v_cols, query, query_b, key, key_b, value, grad, grad_b, _ = h
            attended[:, q_cols] = dot(p[0], value, 0, 0).astype(BF16)
            grads[:frames, q_cols] = dot(d[0], key, 0, 0).astype(BF16)
            grads[frames:, q_cols] = dot(d[1][:, :EDGE], key_b, 0, 0).astype(BF16)
            grads[:, k_cols] = gather(d[0], d[1], query, query_b)
            grads[:, v_cols] = gather(p[0], p[1], grad, grad_b)
    if sends is None:
        return
    for k in range(4):
        slot = chip ^ k
        for i in range(4):
            block = 6 * i + k + (k + 1) // 2
            sends[slot, :, i * HEAD : (i + 1) * HEAD] = grads[:frames, pl.ds(block * HEAD, HEAD)]
        side = (k % 2) * (HEAD // 2)
        for pair in range(2):
            halves = []
            for i in (2 * pair, 2 * pair + 1):
                start = (6 * i + 1 + 3 * (k // 2)) * HEAD + side
                halves.append(grads[:frames, start : start + HEAD // 2])
            at = (4 + pair) * HEAD
            sends[slot, :, at : at + HEAD] = jnp.concatenate(halves, axis=1)


def attend_alone(place, qkv, both, next_cot, attended, grads, later):
    attend_kernel(place, qkv, both, next_cot, attended, grads, None, later)


def input_grad_kernel(place, grads, w, conv, both, *refs):
    grad_in, done, slopes = refs[-3:]
    frames, width = grad_in.shape
    taps = parts_of(both, frames)[2]
    begin, count = place[0], place[1]
    done[...] = jnp.zeros(done.shape, F32)
    live = begin + lax.broadcasted_iota(jnp.int32, (frames, 256), 0) < count
    for col in range(0, width, 256):
        cols = pl.ds(col, 256)
        grad_hidden = dot(grads[...], w[cols, :], 1, 1)
        value = conv[:, cols]
        logistic = 1.0 / (1.0 + jnp.exp(-value))
        slopes[:, cols] = grad_hidden * (logistic * (1.0 + value * (1.0 - logistic)))
        total = grad_hidden[:frames]
        for tap in range(KERNEL):
            low = KERNEL - 1 - tap
            total = total + taps[tap : tap + 1, cols] * slopes[low : low + frames, cols]
        grad_in[:, cols] = jnp.where(live, total, 0.0).astype(BF16)


def weight_kernel(mine, place, own, peers, b, b1, b2, b3, out):
    parity = place[3] if mine else 1 - place[3]
    left = jnp.concatenate([b[0], b1[...], b2[...], b3[...]], axis=0)
    right = jnp.concatenate(
        [jnp.concatenate([a[:, block(2 * k + parity)] for k in range(4)], axis=1) for a in (own, peers)],
        axis=0,
    )
    out[...] = dot(left, right, 0, 0).astype(out.dtype)


def block(index):
    return pl.ds(pl.multiple_of(index * HEAD, HEAD), HEAD)


def halves(place, value, same, other):
    bit = place[2] % 2
    for out, x in ((other, 1 - bit), (same, bit)):
        for y in range(2):
            out[:, y * HEAD : (y + 1) * HEAD] = value(block(2 * y + x)).astype(out.dtype)


def shard_rows(place, mask):
    i = place[4] ^ mask
    for at, size, base in ((0, HEAD, 0), (HEAD, HEAD // 2, 4 * HEAD)):
        rows = pl.ds(pl.multiple_of(base + i * size, size), size)
        yield rows, slice(at, at + size)


def core_sum_kernel(place, keep, got, *outs):
    for i, mask in enumerate((2, 3, 1, 0)):
        for rows, at in shard_rows(place, mask):
            halves(
                place,
                lambda cols, rows=rows: keep[rows, cols] + got[rows, cols].astype(F32),
                outs[2 * i].at[at],
                outs[2 * i + 1].at[at],
            )


def forward_kernel(place, ahead, got, out):
    out[...] = (ahead[...] + got[...].astype(F32)).astype(BF16)


def mid_sum_kernel(same, place, moved, kept, cross, sums, *refs):
    keep, send = refs[-2:]
    own = kept if same else moved
    bit = place[2] // 2
    for out, y in ((send, 1 - bit), (keep, bit)):
        cols = block(y)
        a, b, c = (ref[:, cols].astype(F32) for ref in (own, cross, sums))
        out[...] = (a + b + c).astype(out.dtype)


def place_kernel(scale, place, k0, k1, g0, g1, out):
    for slot, ref in enumerate((k0, k1, g0, g1)):
        value = ref[...].astype(F32) * scale
        k = place[2] ^ slot
        out[k + (k + 1) // 2] = value[:HEAD]
        start = pl.multiple_of((k % 2) * (HEAD // 2), HEAD // 2)
        out[1 + 3 * (k // 2), pl.ds(start, HEAD // 2)] = value[HEAD:]


def call(
    kernel, name, outs, place, operands, scratch=(), mib=16, flops=1000000, moved=1000000,
    remote=(), after=()
):
    def placed(*refs):
        begin, left, *rest = (ref[0] for ref in refs[: len(place)])
        kernel((begin, begin + left, *rest), *refs[len(place) :])

    return pl.pallas_call(
        placed,
        name=name,
        out_shape=[jax.ShapeDtypeStruct(shape, dtype) for shape, dtype in outs],
        in_specs=[pl.BlockSpec(memory_space=pltpu.SMEM)] * len(place)
        + vmem(len(operands))
        + [pl.BlockSpec(memory_space=pltpu.HBM)] * len(remote)
        + [pl.BlockSpec(memory_space=pl.ANY)] * len(after),
        out_specs=vmem(len(outs)),
        scratch_shapes=[pltpu.VMEM(*x) if isinstance(x, tuple) else x for x in scratch],
        compiler_params=params(mib),
        cost_estimate=cost(flops, moved),
    )(*place, *operands, *remote, *after)


def swap(value, axis, mask):
    return lax.ppermute(value, axis, [(i, i ^ mask) for i in range(lax.axis_size(axis))])


def swap_both(value, dp_mask, tm_mask):
    recs = lax.axis_size("dp")
    count = lax.axis_size("tm") * recs
    pairs = [(i, (i // recs ^ tm_mask) * recs + (i % recs ^ dp_mask)) for i in range(count)]
    return lax.ppermute(value, ("tm", "dp"), pairs)


def on_device(frames_in, valid_frames, kernel, w_qkv, cotangent):
    record, cot = frames_in[0], cotangent[0]
    frames, width = record.shape
    span = frames + HALO
    parts, recs = lax.axis_size("tm"), lax.axis_size("dp")
    me = lax.axis_index("tm")
    begin = me * frames
    place = [
        jnp.reshape(x, (1,)).astype(jnp.int32)
        for x in (begin, valid_frames[0] - begin, me // 2, me % 2, lax.axis_index("dp"))
    ]
    split = parts == 8 and recs == 4
    both = lax.optimization_barrier(
        jnp.concatenate([record.astype(F32), cot.astype(F32), kernel], axis=0)
    )
    own = both[:frames].astype(BF16)
    last, first = own[frames - HALO :], own[:HALO]
    first_cot = both[frames : frames + HALO].astype(BF16)
    low_core = me % 2 == 0
    edge = jnp.where(low_core, last, first)
    near = swap(edge, "tm", 1)
    far = lax.ppermute(
        jnp.where(low_core, first, last),
        "tm",
        [(i, (i + 1 if i % 2 else i - 1) % parts) for i in range(parts)],
    )
    next_cot = lax.ppermute(first_cot, "tm", [(i, (i - 1) % parts) for i in range(parts)])
    if split:
        peers = [swap(own, "tm", mask) for mask in (2, 4, 6)]
    rows = frames + 2 * HALO
    hidden, conv, qkv, w_near = call(
        project_kernel,
        "project",
        [
            ((frames, width), BF16),
            ((frames + EDGE, width), F32),
            ((HALO + 2 * frames, 3 * width), BF16),
            (w_qkv.shape, BF16),
        ],
        place,
        [near, far, both],
        [
            ((rows + KERNEL - 1, width), F32),
            ((rows, width), BF16),
            pltpu.SemaphoreType.DMA((3,)),
        ],
        flops=rows * width * 3 * width * 2,
        moved=9000000,
        remote=[w_qkv],
        after=[next_cot],
        mib=OWN,
    )
    outs = [((frames, width), BF16), ((frames + EDGE, 3 * width), BF16)]
    attended, grads, *sends = call(
        attend_kernel if split else attend_alone,
        "attend",
        outs + [((4, frames, 3 * width // 4), BF16)] * split,
        place,
        [qkv, both, next_cot],
        [((frames, width), BF16)],
        mib=16,
        flops=8 * 12 * span * 128 * 128 * 2 * 8,
        moved=5000000,
    )
    if split:
        sends = sends[0]
        got = [swap(sends[slot], "tm", 2 * slot) for slot in (1, 2, 3)]
    scale = float(recs * parts * frames) ** (-0.5)
    if split:
        cols = 3 * width // 4
        shard = cols // 4
        (ends,) = call(
            ends_kernel, "ends", [((4 * EDGE, width), BF16)], place, [both, *peers], after=[grads]
        )
        (peers_hidden,) = call(
            peers_kernel,
            "peer_hidden",
            [((3 * frames, width), BF16)],
            place,
            [*peers, swap(ends, "tm", 1), both],
            [((frames + EDGE, width), F32)],
            flops=3 * frames * width * 40,
            moved=2000000,
        )
        operands = [hidden, peers_hidden, sends, *got]
        whole, half = (shard, width // 2), (shard, 2 * HEAD)
        send, keep = (
            call(
                functools.partial(weight_kernel, mine),
                "weight_" + ("keep" if mine else "send"),
                [((cols, width // 2), F32 if mine else BF16)],
                place,
                operands,
                mib=20,
                flops=cols * width * frames * 4,
                moved=6000000,
            )[0]
            for mine in (False, True)
        )
        low, high = (half, BF16), (half, F32)
        near_same, near_other, *ahead, cross_same, cross_other, own_same, own_other = call(
            core_sum_kernel,
            "core_sum",
            [low, low, high, high, low, low, high, low],
            place,
            [keep, swap(send, "tm", 1)],
        )
        late = [near_same]
        grad_in, done = call(
            input_grad_kernel,
            "input_grad",
            [((frames, width), BF16), ((8, 128), F32)],
            place,
            [grads, w_near, conv, both],
            [((frames + EDGE, width), F32)],
            mib=20,
            flops=(frames + EDGE) * width * 3 * width * 2,
            moved=9000000,
            after=late,
        )
        got_near = swap(near_same, "dp", 1), swap(near_other, "dp", 1)
        got_cross = swap(cross_same, "dp", 1), swap_both(cross_other, 1, 2)
        got_own = swap(own_other, "tm", 2)
        same, other = (
            call(forward_kernel, "forward_" + name, [low], place, [part, got])[0]
            for name, part, got in zip(("same", "other"), ahead, got_near)
        )
        got_sums = swap(same, "dp", 3), swap_both(other, 3, 2)
        kept, moved = [], []
        early = [got_cross[1], done]
        for i, name in enumerate(("same", "other")):
            keep, send = call(
                functools.partial(mid_sum_kernel, i == 0),
                "mid_" + name,
                [((shard, HEAD), F32), ((shard, HEAD), BF16)],
                place,
                [got_own, own_same, got_cross[i], got_sums[i]],
                after=early,
            )
            kept.append(keep)
            moved.append(swap(send, "tm", 4))
        (qkv_grad,) = call(
            functools.partial(place_kernel, scale),
            "place",
            [((3 * HEADS // 4, HEAD, HEAD), F32)],
            place,
            [*kept, *moved],
        )
    else:
        late = []
        grad_in, done = call(
            input_grad_kernel,
            "input_grad",
            [((frames, width), BF16), ((8, 128), F32)],
            place,
            [grads, w_near, conv, both],
            [((frames + EDGE, width), F32)],
            mib=20,
            flops=(frames + EDGE) * width * 3 * width * 2,
            moved=9000000,
            after=late,
        )
        partial = dot(hidden, grads[:frames], 0, 0).astype(BF16)
        by_time = lax.psum_scatter(partial, "tm", scatter_dimension=0, tiled=True)
        summed = lax.psum_scatter(by_time, "dp", scatter_dimension=1, tiled=True).astype(F32)
        qkv_grad = summed.reshape(summed.shape[0], -1, HEAD).transpose(1, 2, 0) * scale
    return (attended[None], grad_in[None], qkv_grad)


def solution(mesh):
    return jax.shard_map(
        on_device,
        mesh=mesh,
        in_specs=(P("dp", "tm", None), P("dp"), P(), P(), P("dp", "tm", None)),
        out_specs=(P("dp", "tm", None), P("dp", "tm", None), P("dp", None, "tm")),
        check_vma=False,
    )
```

```python
import functools

import jax
import jax.numpy as jnp
from jax import lax
from jax.experimental import pallas as pl
from jax.experimental.pallas import tpu as pltpu
from jax.sharding import PartitionSpec as P

HEADS = 8
HEAD = 128
KERNEL = 9
LEFT = 70
HALO = 80
EDGE = 16
MIB = 1024 * 1024
OWN = 42
CHUNK = 48
GROUP = 4
F32 = jnp.float32
BF16 = jnp.bfloat16


def params(mib):
    return pltpu.CompilerParams(vmem_limit_bytes=mib * MIB)


def vmem(count):
    return [pl.BlockSpec(memory_space=pltpu.VMEM)] * count


def cost(flops, moved):
    return pl.CostEstimate(flops=flops, bytes_accessed=moved, transcendentals=0)


def dot(a, b, left, right):
    return lax.dot_general(a, b, (((left,), (right,)), ((), ())), preferred_element_type=F32)


def conv_hidden(ext, taps, cols, low, rows, hidden, conv_out=None, keep=(0, 0)):
    weights = [taps[tap : tap + 1, cols] for tap in range(KERNEL)]
    for start in range(0, rows, CHUNK):
        size = min(CHUNK, rows - start)
        at = low + start
        conv = weights[0] * ext[at : at + size, cols]
        for tap in range(1, KERNEL):
            conv = conv + weights[tap] * ext[at + tap : at + tap + size, cols]
        masked = ext[at + KERNEL - 1 : at + KERNEL - 1 + size, cols]
        hidden[start : start + size, cols] = (masked + conv / (1.0 + jnp.exp(-conv))).astype(BF16)
        first, last = max(start, keep[0]), min(start + size, keep[1])
        if first < last:
            conv_out[first - keep[0] : last - keep[0], cols] = conv[first - start : last - start]


def live_rows(first, rows, count):
    return first + lax.broadcasted_iota(jnp.int32, (rows, 128), 0) < count


def parts_of(both, frames):
    return both.at[:frames], both.at[frames : 2 * frames], both.at[2 * frames :]


def own_kernel(place, both, w, _, hidden, conv_out, qkv, w_out, ext, sems):
    frames, width = ext.shape
    rows, wide = frames - EDGE, width
    copies = [
        pltpu.make_async_copy(w.at[:, cols], w_out.at[:, cols], sems.at[i])
        for i, cols in enumerate(pl.ds(i * wide, wide) for i in range(3))
    ]
    for copy in copies:
        copy.start()
    own, _, taps = parts_of(both, frames)
    live = live_rows(place[0], frames, place[1])
    for col in range(0, width, 128):
        cols = pl.ds(col, 128)
        ext[:, cols] = jnp.where(live, own[:, cols], 0.0)
        conv_hidden(ext, taps, cols, EDGE - KERNEL + 1, rows, hidden, conv_out, (0, rows))
    for i, copy in enumerate(copies):
        copy.wait()
        for col in range(i * wide, (i + 1) * wide, 512):
            cols = pl.ds(col, 512)
            qkv[:, cols] = dot(hidden[...], w_out[:, cols], 1, 0).astype(BF16)


def rim_kernel(place, near, far, both, w, _, first, conv_out, qkv, ext, hidden):
    width = w.shape[0]
    frames = qkv.shape[0] - HALO - EDGE
    own, _, taps = parts_of(both, frames)
    low_core = place[3] == 0
    head, back = HALO + EDGE, KERNEL - 1
    rows = head + HALO
    begin, count = place[0], place[1]
    live_a = live_rows(begin - HALO, head, count) & ~live_rows(begin - HALO, head, 0)
    live_b = live_rows(begin + frames - back, HALO + back, count)
    for col in range(0, width, 128):
        cols = pl.ds(col, 128)
        mate, other = near[:, cols].astype(F32), far[:, cols].astype(F32)
        raw = jnp.concatenate([jnp.where(low_core, other, mate), own[:EDGE, cols]], axis=0)
        ext[:back, cols] = jnp.zeros((back, 128), F32)
        ext[back : back + head, cols] = jnp.where(live_a, raw, 0.0)
        conv_hidden(
            ext, taps, cols, 0, head, hidden.at[:head], conv_out.at[:EDGE], (HALO, head)
        )
        after = jnp.where(low_core, mate, other)
        raw = jnp.concatenate([own[frames - back :, cols], after], axis=0)
        ext[back + head :, cols] = jnp.where(live_b, raw, 0.0)
        conv_hidden(
            ext, taps, cols, back + head, HALO, hidden.at[head:], conv_out.at[EDGE:], (0, EDGE)
        )
    first[...] = hidden[HALO:head]
    for col in range(0, 3 * width, 512):
        cols = pl.ds(col, 512)
        low = HALO if col < width else 0
        qkv[low:rows, cols] = dot(hidden[low:], w[:, cols], 1, 0).astype(BF16)
    qkv[rows:, :] = jnp.zeros((qkv.shape[0] - rows, 3 * width), BF16)


def ends_kernel(place, both, f1, f2, f3, _, out):
    frames = f1.shape[0]
    out[:EDGE] = both[frames - EDGE : frames].astype(BF16)
    for slot, ref in ((1, f1), (2, f2), (3, f3)):
        out[slot * EDGE : (slot + 1) * EDGE] = ref[frames - EDGE :]


def peers_kernel(place, f1, f2, f3, tails, both, hidden, ext):
    frames, width = f1.shape
    taps = parts_of(both, frames)[2]
    count, chip, core = place[1], place[2], place[3]
    for slot, ref in ((1, f1), (2, f2), (3, f3)):
        peer = chip ^ slot
        begin = (2 * peer + core) * frames
        source = jnp.where(core == 1, slot, chip ^ jnp.maximum(peer - 1, 0))
        start = pl.multiple_of(source * EDGE, EDGE)
        live = live_rows(begin - EDGE, frames + EDGE, count)
        real = begin - EDGE + lax.broadcasted_iota(jnp.int32, (frames + EDGE, 128), 0) >= 0
        live = live & real
        for col in range(0, width, 128):
            cols = pl.ds(col, 128)
            raw = jnp.concatenate([tails[pl.ds(start, EDGE), cols], ref[:, cols]], axis=0)
            masked = jnp.where(live, raw.astype(F32), 0.0)
            ext[:, cols] = masked
            out = hidden.at[(slot - 1) * frames : slot * frames]
            conv_hidden(ext, taps, cols, EDGE - KERNEL + 1, frames, out)


def attend_kernel(place, rim, mid, both, next_cot, attended, grads, sends, later):
    frames, width = attended.shape
    cot = parts_of(both, frames)[1]
    span = frames + HALO
    begin, count, chip = place[0], place[1], place[2]

    head = HALO + EDGE
    skip = (frames - LEFT) // EDGE * EDGE

    def mask(start, wanted):
        key = lax.broadcasted_iota(jnp.int32, (start + wanted, frames), 0)
        query = lax.broadcasted_iota(jnp.int32, (start + wanted, frames), 1)
        first = begin if wanted == frames else begin + frames
        gap = query + start - key
        seen = first + query - gap
        alive = (first + query < count) & (query < wanted)
        allowed = (gap >= 0) & (gap <= LEFT) & (seen >= 0) & alive
        return jnp.where(allowed, 0.0, -jnp.inf), jnp.where(alive[:1], 0.0, 1.0)

    masks = [mask(HALO, frames), mask(frames - skip, HALO)]
    row = lax.broadcasted_iota(jnp.int32, (frames, width), 0)
    after = next_cot[...].astype(F32)
    later[:HALO] = jnp.where(begin + frames + row[:HALO] < count, after, 0.0).astype(BF16)
    later[HALO:] = jnp.zeros((frames - HALO, width), BF16)
    factor = HEAD**-0.5

    def probs(scores, bias, missing):
        raised = jnp.exp(scores * factor + bias)
        return raised * (1.0 / (jnp.sum(raised, axis=0, keepdims=True) + missing))

    def slopes(prob, grad_prob):
        mean = jnp.sum(prob * grad_prob, axis=0, keepdims=True)
        return (prob * (grad_prob - mean) * factor).astype(BF16)

    own_live = begin + lax.broadcasted_iota(jnp.int32, (frames, HEAD), 0) < count
    lead, trail = jnp.zeros((skip, frames), BF16), jnp.zeros((EDGE, frames), BF16)

    def gather(own, late, rhs, rhs_late):
        left = jnp.concatenate([own[HALO:], trail], axis=0)
        right = jnp.concatenate([lead, late[: frames - skip + EDGE]], axis=0)
        left = jnp.concatenate([left, right], axis=1)
        return dot(left, jnp.concatenate([rhs, rhs_late], axis=0), 1, 0).astype(BF16)

    for first in range(0, HEADS, GROUP):
        heads = []
        for index in range(first, first + GROUP):
            q_cols = pl.ds(index * HEAD, HEAD)
            k_cols = pl.ds(width + index * HEAD, HEAD)
            v_cols = pl.ds(2 * width + index * HEAD, HEAD)
            query = jnp.concatenate([rim[HALO:head, q_cols], mid[:, q_cols]], axis=0)
            query_b = rim[head:, q_cols]
            key, value = (
                jnp.concatenate([rim[:head, cols], mid[:, cols]], axis=0) for cols in (k_cols, v_cols)
            )
            key_b, value_b = (
                jnp.concatenate([mid[skip - EDGE :, cols], rim[head : head + HALO, cols]], axis=0)
                for cols in (k_cols, v_cols)
            )
            grad = jnp.where(own_live, cot[:, q_cols], 0.0).astype(BF16)
            grad_b = later[:, q_cols]
            heads.append((q_cols, k_cols, v_cols, query, query_b, key, key_b, value, grad, grad_b, value_b))
        scores = [
            (dot(h[5], h[3], 1, 1), dot(h[6], h[4], 1, 1), dot(h[7], h[8], 1, 1), dot(h[10], h[9], 1, 1))
            for h in heads
        ]
        prob = [(probs(s[0], *masks[0]), probs(s[1], *masks[1])) for s in scores]
        low = [(p[0].astype(BF16), p[1].astype(BF16)) for p in prob]
        slope = [(slopes(p[0], s[2]), slopes(p[1], s[3])) for p, s in zip(prob, scores)]
        for h, p, d in zip(heads, low, slope):
            q_cols, k_cols, v_cols, query, query_b, key, key_b, value, grad, grad_b, _ = h
            attended[:, q_cols] = dot(p[0], value, 0, 0).astype(BF16)
            grads[:frames, q_cols] = dot(d[0], key, 0, 0).astype(BF16)
            grads[frames:, q_cols] = dot(d[1][:, :EDGE], key_b, 0, 0).astype(BF16)
            grads[:, k_cols] = gather(d[0], d[1], query, query_b)
            grads[:, v_cols] = gather(p[0], p[1], grad, grad_b)
    if sends is None:
        return
    for k in range(4):
        slot = chip ^ k
        for i in range(4):
            block = 6 * i + k + (k + 1) // 2
            sends[slot, :, i * HEAD : (i + 1) * HEAD] = grads[:frames, pl.ds(block * HEAD, HEAD)]
        side = (k % 2) * (HEAD // 2)
        for pair in range(2):
            halves = []
            for i in (2 * pair, 2 * pair + 1):
                start = (6 * i + 1 + 3 * (k // 2)) * HEAD + side
                halves.append(grads[:frames, start : start + HEAD // 2])
            at = (4 + pair) * HEAD
            sends[slot, :, at : at + HEAD] = jnp.concatenate(halves, axis=1)


def attend_alone(place, rim, mid, both, next_cot, attended, grads, later):
    attend_kernel(place, rim, mid, both, next_cot, attended, grads, None, later)


def input_grad_kernel(place, grads, w, conv_mid, conv_rim, both, *refs):
    grad_in, done, slopes = refs[-3:]
    frames, width = grad_in.shape
    taps = parts_of(both, frames)[2]
    begin, count = place[0], place[1]
    done[...] = jnp.zeros(done.shape, F32)
    live = begin + lax.broadcasted_iota(jnp.int32, (frames, 256), 0) < count
    for col in range(0, width, 256):
        cols = pl.ds(col, 256)
        grad_hidden = dot(grads[...], w[cols, :], 1, 1)
        rim = conv_rim[:, cols]
        value = jnp.concatenate([rim[:EDGE], conv_mid[:, cols], rim[EDGE:]], axis=0)
        logistic = 1.0 / (1.0 + jnp.exp(-value))
        slopes[:, cols] = grad_hidden * (logistic * (1.0 + value * (1.0 - logistic)))
        total = grad_hidden[:frames]
        for tap in range(KERNEL):
            low = KERNEL - 1 - tap
            total = total + taps[tap : tap + 1, cols] * slopes[low : low + frames, cols]
        grad_in[:, cols] = jnp.where(live, total, 0.0).astype(BF16)


def weight_kernel(mine, ys, place, first, mid, peers, b, b1, b2, b3, out):
    parity = place[3] if mine else 1 - place[3]
    left = jnp.concatenate([b[0], b1[...], b2[...], b3[...]], axis=0)
    chips = [2 * y + x for y in ys for x in range(2)]
    right = jnp.concatenate(
        [jnp.concatenate([a[:, block(2 * k + parity)] for k in chips], axis=1) for a in (first, mid, peers)],
        axis=0,
    )
    out[...] = dot(left, right, 0, 0).astype(out.dtype)


def block(index):
    return pl.ds(pl.multiple_of(index * HEAD, HEAD), HEAD)


def halves(place, value, same, other):
    bit = place[2] % 2
    for out, x in ((other, 1 - bit), (same, bit)):
        for y in range(2):
            out[:, y * HEAD : (y + 1) * HEAD] = value(y, x).astype(out.dtype)


def shard_rows(place, mask):
    i = place[4] ^ mask
    for at, size, base in ((0, HEAD, 0), (HEAD, HEAD // 2, 4 * HEAD)):
        rows = pl.ds(pl.multiple_of(base + i * size, size), size)
        yield rows, slice(at, at + size)


def core_sum_kernel(place, keep, got0, got1, *outs):
    for i, mask in enumerate((2, 3, 1, 0)):
        for rows, at in shard_rows(place, mask):

            def value(y, x, rows=rows):
                return keep[rows, block(2 * y + x)] + (got0, got1)[y][rows, block(x)].astype(F32)

            halves(place, value, outs[2 * i].at[at], outs[2 * i + 1].at[at])


def forward_kernel(place, ahead, got, out):
    out[...] = (ahead[...] + got[...].astype(F32)).astype(BF16)


def mid_sum_kernel(same, place, moved, kept, cross, sums, *refs):
    keep, send = refs[-2:]
    own = kept if same else moved
    bit = place[2] // 2
    for out, y in ((send, 1 - bit), (keep, bit)):
        cols = block(y)
        a, b, c = (ref[:, cols].astype(F32) for ref in (own, cross, sums))
        out[...] = (a + b + c).astype(out.dtype)


def place_kernel(scale, place, k0, k1, g0, g1, out):
    for slot, ref in enumerate((k0, k1, g0, g1)):
        value = ref[...].astype(F32) * scale
        k = place[2] ^ slot
        out[k + (k + 1) // 2] = value[:HEAD]
        start = pl.multiple_of((k % 2) * (HEAD // 2), HEAD // 2)
        out[1 + 3 * (k // 2), pl.ds(start, HEAD // 2)] = value[HEAD:]


def call(
    kernel, name, outs, place, operands, scratch=(), mib=16, flops=1000000, moved=1000000,
    remote=(), after=()
):
    def placed(*refs):
        begin, left, *rest = (ref[0] for ref in refs[: len(place)])
        kernel((begin, begin + left, *rest), *refs[len(place) :])

    return pl.pallas_call(
        placed,
        name=name,
        out_shape=[jax.ShapeDtypeStruct(shape, dtype) for shape, dtype in outs],
        in_specs=[pl.BlockSpec(memory_space=pltpu.SMEM)] * len(place)
        + vmem(len(operands))
        + [pl.BlockSpec(memory_space=pltpu.HBM)] * len(remote)
        + [pl.BlockSpec(memory_space=pl.ANY)] * len(after),
        out_specs=vmem(len(outs)),
        scratch_shapes=[pltpu.VMEM(*x) if isinstance(x, tuple) else x for x in scratch],
        compiler_params=params(mib),
        cost_estimate=cost(flops, moved),
    )(*place, *operands, *remote, *after)


def swap(value, axis, mask):
    return lax.ppermute(value, axis, [(i, i ^ mask) for i in range(lax.axis_size(axis))])


def swap_both(value, dp_mask, tm_mask):
    recs = lax.axis_size("dp")
    count = lax.axis_size("tm") * recs
    pairs = [(i, (i // recs ^ tm_mask) * recs + (i % recs ^ dp_mask)) for i in range(count)]
    return lax.ppermute(value, ("tm", "dp"), pairs)


def on_device(frames_in, valid_frames, kernel, w_qkv, cotangent):
    record, cot = frames_in[0], cotangent[0]
    frames, width = record.shape
    span = frames + HALO
    parts, recs = lax.axis_size("tm"), lax.axis_size("dp")
    me = lax.axis_index("tm")
    begin = me * frames
    place = [
        jnp.reshape(x, (1,)).astype(jnp.int32)
        for x in (begin, valid_frames[0] - begin, me // 2, me % 2, lax.axis_index("dp"))
    ]
    split = parts == 8 and recs == 4
    both = lax.optimization_barrier(
        jnp.concatenate([record.astype(F32), cot.astype(F32), kernel], axis=0)
    )
    own = both[:frames].astype(BF16)
    last, start = own[frames - HALO :], own[:HALO]
    first_cot = both[frames : frames + HALO].astype(BF16)
    low_core = me % 2 == 0
    edge = jnp.where(low_core, last, start)
    near = swap(edge, "tm", 1)
    far = lax.ppermute(
        jnp.where(low_core, start, last),
        "tm",
        [(i, (i + 1 if i % 2 else i - 1) % parts) for i in range(parts)],
    )
    next_cot = lax.ppermute(first_cot, "tm", [(i, (i - 1) % parts) for i in range(parts)])
    if split:
        peers = [swap(own, "tm", mask) for mask in (2, 4, 6)]
    rows = frames - EDGE
    mid, conv_mid, qkv_mid, w_near = call(
        own_kernel,
        "own_rows",
        [((rows, width), BF16), ((rows, width), F32), ((rows, 3 * width), BF16), (w_qkv.shape, BF16)],
        place,
        [both],
        [((frames, width), F32), pltpu.SemaphoreType.DMA((3,))],
        flops=rows * width * 3 * width * 2,
        moved=9000000,
        remote=[w_qkv],
        after=[near],
        mib=OWN,
    )
    rows = 2 * HALO + EDGE
    first, conv_rim, qkv_rim = call(
        rim_kernel,
        "rim_rows",
        [((EDGE, width), BF16), ((2 * EDGE, width), F32), ((HALO + EDGE + frames, 3 * width), BF16)],
        place,
        [near, far, both, w_near],
        [((rows + 2 * (KERNEL - 1), width), F32), ((rows, width), BF16)],
        flops=rows * width * 3 * width * 2,
        moved=9000000,
        after=[next_cot],
    )
    outs = [((frames, width), BF16), ((frames + EDGE, 3 * width), BF16)]
    attended, grads, *sends = call(
        attend_kernel if split else attend_alone,
        "attend",
        outs + [((4, frames, 3 * width // 4), BF16)] * split,
        place,
        [qkv_rim, qkv_mid, both, next_cot],
        [((frames, width), BF16)],
        mib=16,
        flops=8 * 12 * span * 128 * 128 * 2 * 8,
        moved=5000000,
    )
    if split:
        sends = sends[0]
        got = [swap(sends[slot], "tm", 2 * slot) for slot in (1, 2, 3)]
    scale = float(recs * parts * frames) ** (-0.5)
    if split:
        cols = 3 * width // 4
        shard = cols // 4
        (ends,) = call(
            ends_kernel, "ends", [((4 * EDGE, width), BF16)], place, [both, *peers], after=[grads]
        )
        (peers_hidden,) = call(
            peers_kernel,
            "peer_hidden",
            [((3 * frames, width), BF16)],
            place,
            [*peers, swap(ends, "tm", 1), both],
            [((frames + EDGE, width), F32)],
            flops=3 * frames * width * 40,
            moved=2000000,
        )
        operands = [first, mid, peers_hidden, sends, *got]
        whole, half = (shard, width // 2), (shard, 2 * HEAD)
        send0, send1, keep = (
            call(
                functools.partial(weight_kernel, mine, ys),
                "weight_" + name,
                [((cols, len(ys) * 2 * HEAD), F32 if mine else BF16)],
                place,
                operands,
                mib=20,
                flops=cols * width * frames * 4,
                moved=6000000,
            )[0]
            for name, mine, ys in (("send0", False, (0,)), ("send1", False, (1,)), ("keep", True, (0, 1)))
        )
        low, high = (half, BF16), (half, F32)
        near_same, near_other, *ahead, cross_same, cross_other, own_same, own_other = call(
            core_sum_kernel,
            "core_sum",
            [low, low, high, high, low, low, high, low],
            place,
            [keep, swap(send0, "tm", 1), swap(send1, "tm", 1)],
        )
        late = [near_same]
        grad_in, done = call(
            input_grad_kernel,
            "input_grad",
            [((frames, width), BF16), ((8, 128), F32)],
            place,
            [grads, w_near, conv_mid, conv_rim, both],
            [((frames + EDGE, width), F32)],
            mib=20,
            flops=(frames + EDGE) * width * 3 * width * 2,
            moved=9000000,
            after=late,
        )
        got_near = swap(near_same, "dp", 1), swap(near_other, "dp", 1)
        got_cross = swap(cross_same, "dp", 1), swap_both(cross_other, 1, 2)
        got_own = swap(own_other, "tm", 2)
        same, other = (
            call(forward_kernel, "forward_" + name, [low], place, [part, got])[0]
            for name, part, got in zip(("same", "other"), ahead, got_near)
        )
        got_sums = swap(same, "dp", 3), swap_both(other, 3, 2)
        kept, moved = [], []
        early = [got_cross[1], done]
        for i, name in enumerate(("same", "other")):
            keep, send = call(
                functools.partial(mid_sum_kernel, i == 0),
                "mid_" + name,
                [((shard, HEAD), F32), ((shard, HEAD), BF16)],
                place,
                [got_own, own_same, got_cross[i], got_sums[i]],
                after=early,
            )
            kept.append(keep)
            moved.append(swap(send, "tm", 4))
        (qkv_grad,) = call(
            functools.partial(place_kernel, scale),
            "place",
            [((3 * HEADS // 4, HEAD, HEAD), F32)],
            place,
            [*kept, *moved],
        )
    else:
        late = []
        grad_in, done = call(
            input_grad_kernel,
            "input_grad",
            [((frames, width), BF16), ((8, 128), F32)],
            place,
            [grads, w_near, conv_mid, conv_rim, both],
            [((frames + EDGE, width), F32)],
            mib=20,
            flops=(frames + EDGE) * width * 3 * width * 2,
            moved=9000000,
            after=late,
        )
        hidden = jnp.concatenate([first, mid], axis=0)
        partial = dot(hidden, grads[:frames], 0, 0).astype(BF16)
        by_time = lax.psum_scatter(partial, "tm", scatter_dimension=0, tiled=True)
        summed = lax.psum_scatter(by_time, "dp", scatter_dimension=1, tiled=True).astype(F32)
        qkv_grad = summed.reshape(summed.shape[0], -1, HEAD).transpose(1, 2, 0) * scale
    return (attended[None], grad_in[None], qkv_grad)


def solution(mesh):
    return jax.shard_map(
        on_device,
        mesh=mesh,
        in_specs=(P("dp", "tm", None), P("dp"), P(), P(), P("dp", "tm", None)),
        out_specs=(P("dp", "tm", None), P("dp", "tm", None), P("dp", None, "tm")),
        check_vma=False,
    )
```

```python
import functools

import jax
import jax.numpy as jnp
from jax import lax
from jax.experimental import pallas as pl
from jax.experimental.pallas import tpu as pltpu
from jax.sharding import PartitionSpec as P

HEADS = 8
HEAD = 128
KERNEL = 9
LEFT = 70
HALO = 80
EDGE = 16
MIB = 1024 * 1024
OWN = 42
CHUNK = 48
GROUP = 4
F32 = jnp.float32
BF16 = jnp.bfloat16


def params(mib):
    return pltpu.CompilerParams(vmem_limit_bytes=mib * MIB)


def vmem(count):
    return [pl.BlockSpec(memory_space=pltpu.VMEM)] * count


def cost(flops, moved):
    return pl.CostEstimate(flops=flops, bytes_accessed=moved, transcendentals=0)


def dot(a, b, left, right):
    return lax.dot_general(a, b, (((left,), (right,)), ((), ())), preferred_element_type=F32)


def conv_hidden(ext, taps, cols, low, rows, hidden, conv_out=None, keep=(0, 0)):
    weights = [taps[tap : tap + 1, cols] for tap in range(KERNEL)]
    for start in range(0, rows, CHUNK):
        size = min(CHUNK, rows - start)
        at = low + start
        conv = weights[0] * ext[at : at + size, cols]
        for tap in range(1, KERNEL):
            conv = conv + weights[tap] * ext[at + tap : at + tap + size, cols]
        masked = ext[at + KERNEL - 1 : at + KERNEL - 1 + size, cols]
        hidden[start : start + size, cols] = (masked + conv / (1.0 + jnp.exp(-conv))).astype(BF16)
        first, last = max(start, keep[0]), min(start + size, keep[1])
        if first < last:
            conv_out[first - keep[0] : last - keep[0], cols] = conv[first - start : last - start]


def live_rows(first, rows, count):
    return first + lax.broadcasted_iota(jnp.int32, (rows, 128), 0) < count


def parts_of(both, frames):
    return both.at[:frames], both.at[frames : 2 * frames], both.at[2 * frames :]


def project_kernel(place, near, far, both, w, _, own_hidden, conv_out, qkv, w_out, *scratch):
    frames, width = own_hidden.shape
    ext, hidden, sems = scratch
    wide = width
    copies = [
        pltpu.make_async_copy(w.at[:, cols], w_out.at[:, cols], sems.at[i])
        for i, cols in enumerate(pl.ds(i * wide, wide) for i in range(3))
    ]
    for copy in copies:
        copy.start()
    own, _, taps = parts_of(both, frames)
    low_core = place[3] == 0
    rows, back = frames + 2 * HALO, KERNEL - 1
    live = live_rows(place[0] - HALO, rows, place[1]) & ~live_rows(place[0] - HALO, rows, 0)
    for col in range(0, width, 128):
        cols = pl.ds(col, 128)
        mate, other = near[:, cols].astype(F32), far[:, cols].astype(F32)
        before, after = jnp.where(low_core, other, mate), jnp.where(low_core, mate, other)
        raw = jnp.concatenate([before, own[:, cols], after], axis=0)
        masked = jnp.where(live, raw, 0.0)
        ext[:back, cols] = jnp.zeros((back, 128), F32)
        ext[back:, cols] = masked
        conv_hidden(ext, taps, cols, 0, rows, hidden, conv_out, (HALO, HALO + frames + EDGE))
    own_hidden[...] = hidden[HALO : HALO + frames]
    for i, copy in enumerate(copies):
        copy.wait()
        low = HALO if i * wide < width else 0
        for col in range(i * wide, (i + 1) * wide, 512):
            cols = pl.ds(col, 512)
            qkv[low:rows, cols] = dot(hidden[low:], w_out[:, cols], 1, 0).astype(BF16)
    qkv[rows:, :] = jnp.zeros((qkv.shape[0] - rows, 3 * width), BF16)


def ends_kernel(place, both, f1, f2, f3, _, out):
    frames = f1.shape[0]
    out[:EDGE] = both[frames - EDGE : frames].astype(BF16)
    for slot, ref in ((1, f1), (2, f2), (3, f3)):
        out[slot * EDGE : (slot + 1) * EDGE] = ref[frames - EDGE :]


def peers_kernel(place, f1, f2, f3, tails, both, hidden, ext):
    frames, width = f1.shape
    taps = parts_of(both, frames)[2]
    count, chip, core = place[1], place[2], place[3]
    for slot, ref in ((1, f1), (2, f2), (3, f3)):
        peer = chip ^ slot
        begin = (2 * peer + core) * frames
        source = jnp.where(core == 1, slot, chip ^ jnp.maximum(peer - 1, 0))
        start = pl.multiple_of(source * EDGE, EDGE)
        live = live_rows(begin - EDGE, frames + EDGE, count)
        real = begin - EDGE + lax.broadcasted_iota(jnp.int32, (frames + EDGE, 128), 0) >= 0
        live = live & real
        for col in range(0, width, 128):
            cols = pl.ds(col, 128)
            raw = jnp.concatenate([tails[pl.ds(start, EDGE), cols], ref[:, cols]], axis=0)
            masked = jnp.where(live, raw.astype(F32), 0.0)
            ext[:, cols] = masked
            out = hidden.at[(slot - 1) * frames : slot * frames]
            conv_hidden(ext, taps, cols, EDGE - KERNEL + 1, frames, out)


def attend_kernel(place, qkv, both, next_cot, attended, grads, sends, later):
    frames, width = attended.shape
    cot = parts_of(both, frames)[1]
    span = frames + HALO
    begin, count, chip = place[0], place[1], place[2]

    skip = (frames - LEFT) // EDGE * EDGE

    def mask(start, wanted):
        key = lax.broadcasted_iota(jnp.int32, (start + wanted, frames), 0)
        query = lax.broadcasted_iota(jnp.int32, (start + wanted, frames), 1)
        first = begin if wanted == frames else begin + frames
        gap = query + start - key
        seen = first + query - gap
        alive = (first + query < count) & (query < wanted)
        allowed = (gap >= 0) & (gap <= LEFT) & (seen >= 0) & alive
        return jnp.where(allowed, 0.0, -jnp.inf), jnp.where(alive[:1], 0.0, 1.0)

    masks = [mask(HALO, frames), mask(frames - skip, HALO)]
    row = lax.broadcasted_iota(jnp.int32, (frames, width), 0)
    after = next_cot[...].astype(F32)
    later[:HALO] = jnp.where(begin + frames + row[:HALO] < count, after, 0.0).astype(BF16)
    later[HALO:] = jnp.zeros((frames - HALO, width), BF16)
    factor = HEAD**-0.5

    def probs(scores, bias, missing):
        raised = jnp.exp(scores * factor + bias)
        return raised * (1.0 / (jnp.sum(raised, axis=0, keepdims=True) + missing))

    def slopes(prob, grad_prob):
        mean = jnp.sum(prob * grad_prob, axis=0, keepdims=True)
        return (prob * (grad_prob - mean) * factor).astype(BF16)

    own_live = begin + lax.broadcasted_iota(jnp.int32, (frames, HEAD), 0) < count
    lead, trail = jnp.zeros((skip, frames), BF16), jnp.zeros((EDGE, frames), BF16)

    def gather(own, late, rhs, rhs_late):
        left = jnp.concatenate([own[HALO:], trail], axis=0)
        right = jnp.concatenate([lead, late[: frames - skip + EDGE]], axis=0)
        left = jnp.concatenate([left, right], axis=1)
        return dot(left, jnp.concatenate([rhs, rhs_late], axis=0), 1, 0).astype(BF16)

    for first in range(0, HEADS, GROUP):
        heads = []
        for head in range(first, first + GROUP):
            q_cols = pl.ds(head * HEAD, HEAD)
            k_cols = pl.ds(width + head * HEAD, HEAD)
            v_cols = pl.ds(2 * width + head * HEAD, HEAD)
            query = qkv[HALO : HALO + frames, q_cols]
            query_b = qkv[HALO + frames : HALO + 2 * frames, q_cols]
            key, key_b = qkv[:span, k_cols], qkv[HALO + skip : HALO + span, k_cols]
            value, value_b = qkv[:span, v_cols], qkv[HALO + skip : HALO + span, v_cols]
            grad = jnp.where(own_live, cot[:, q_cols], 0.0).astype(BF16)
            grad_b = later[:, q_cols]
            heads.append((q_cols, k_cols, v_cols, query, query_b, key, key_b, value, grad, grad_b, value_b))
        scores = [
            (dot(h[5], h[3], 1, 1), dot(h[6], h[4], 1, 1), dot(h[7], h[8], 1, 1), dot(h[10], h[9], 1, 1))
            for h in heads
        ]
        prob = [(probs(s[0], *masks[0]), probs(s[1], *masks[1])) for s in scores]
        low = [(p[0].astype(BF16), p[1].astype(BF16)) for p in prob]
        slope = [(slopes(p[0], s[2]), slopes(p[1], s[3])) for p, s in zip(prob, scores)]
        for h, p, d in zip(heads, low, slope):
            q_cols, k_cols, v_cols, query, query_b, key, key_b, value, grad, grad_b, _ = h
            attended[:, q_cols] = dot(p[0], value, 0, 0).astype(BF16)
            grads[:frames, q_cols] = dot(d[0], key, 0, 0).astype(BF16)
            grads[frames:, q_cols] = dot(d[1][:, :EDGE], key_b, 0, 0).astype(BF16)
            grads[:, k_cols] = gather(d[0], d[1], query, query_b)
            grads[:, v_cols] = gather(p[0], p[1], grad, grad_b)
    if sends is None:
        return
    for k in range(4):
        slot = chip ^ k
        for i in range(4):
            block = 6 * i + k + (k + 1) // 2
            sends[slot, :, i * HEAD : (i + 1) * HEAD] = grads[:frames, pl.ds(block * HEAD, HEAD)]
        side = (k % 2) * (HEAD // 2)
        for pair in range(2):
            halves = []
            for i in (2 * pair, 2 * pair + 1):
                start = (6 * i + 1 + 3 * (k // 2)) * HEAD + side
                halves.append(grads[:frames, start : start + HEAD // 2])
            at = (4 + pair) * HEAD
            sends[slot, :, at : at + HEAD] = jnp.concatenate(halves, axis=1)


def attend_alone(place, qkv, both, next_cot, attended, grads, later):
    attend_kernel(place, qkv, both, next_cot, attended, grads, None, later)


def input_grad_kernel(place, grads, w, conv, both, *refs):
    grad_in, done, slopes = refs[-3:]
    frames, width = grad_in.shape
    taps = parts_of(both, frames)[2]
    begin, count = place[0], place[1]
    done[...] = jnp.zeros(done.shape, F32)
    live = begin + lax.broadcasted_iota(jnp.int32, (frames, 256), 0) < count
    for col in range(0, width, 256):
        cols = pl.ds(col, 256)
        grad_hidden = dot(grads[...], w[cols, :], 1, 1)
        value = conv[:, cols]
        logistic = 1.0 / (1.0 + jnp.exp(-value))
        slopes[:, cols] = grad_hidden * (logistic * (1.0 + value * (1.0 - logistic)))
        total = grad_hidden[:frames]
        for tap in range(KERNEL):
            low = KERNEL - 1 - tap
            total = total + taps[tap : tap + 1, cols] * slopes[low : low + frames, cols]
        grad_in[:, cols] = jnp.where(live, total, 0.0).astype(BF16)


def weight_kernel(mine, ys, place, own, peers, b, b1, b2, b3, out):
    parity = place[3] if mine else 1 - place[3]
    left = jnp.concatenate([b[0], b1[...], b2[...], b3[...]], axis=0)
    chips = [2 * y + x for y in ys for x in range(2)]
    right = jnp.concatenate(
        [jnp.concatenate([a[:, block(2 * k + parity)] for k in chips], axis=1) for a in (own, peers)],
        axis=0,
    )
    out[...] = dot(left, right, 0, 0).astype(out.dtype)


def block(index):
    return pl.ds(pl.multiple_of(index * HEAD, HEAD), HEAD)


def halves(place, value, same, other):
    bit = place[2] % 2
    for out, x in ((other, 1 - bit), (same, bit)):
        for y in range(2):
            out[:, y * HEAD : (y + 1) * HEAD] = value(y, x).astype(out.dtype)


def shard_rows(place, mask):
    i = place[4] ^ mask
    for at, size, base in ((0, HEAD, 0), (HEAD, HEAD // 2, 4 * HEAD)):
        rows = pl.ds(pl.multiple_of(base + i * size, size), size)
        yield rows, slice(at, at + size)


def core_sum_kernel(place, keep, got0, got1, *outs):
    for i, mask in enumerate((2, 3, 1, 0)):
        for rows, at in shard_rows(place, mask):

            def value(y, x, rows=rows):
                return keep[rows, block(2 * y + x)] + (got0, got1)[y][rows, block(x)].astype(F32)

            halves(place, value, outs[2 * i].at[at], outs[2 * i + 1].at[at])


def forward_kernel(place, ahead, got, out):
    out[...] = (ahead[...] + got[...].astype(F32)).astype(BF16)


def mid_sum_kernel(same, place, moved, kept, cross, sums, *refs):
    keep, send = refs[-2:]
    own = kept if same else moved
    bit = place[2] // 2
    for out, y in ((send, 1 - bit), (keep, bit)):
        cols = block(y)
        a, b, c = (ref[:, cols].astype(F32) for ref in (own, cross, sums))
        out[...] = (a + b + c).astype(out.dtype)


def place_kernel(scale, place, k0, k1, g0, g1, out):
    for slot, ref in enumerate((k0, k1, g0, g1)):
        value = ref[...].astype(F32) * scale
        k = place[2] ^ slot
        out[k + (k + 1) // 2] = value[:HEAD]
        start = pl.multiple_of((k % 2) * (HEAD // 2), HEAD // 2)
        out[1 + 3 * (k // 2), pl.ds(start, HEAD // 2)] = value[HEAD:]


def call(
    kernel, name, outs, place, operands, scratch=(), mib=16, flops=1000000, moved=1000000,
    remote=(), after=()
):
    def placed(*refs):
        begin, left, *rest = (ref[0] for ref in refs[: len(place)])
        kernel((begin, begin + left, *rest), *refs[len(place) :])

    return pl.pallas_call(
        placed,
        name=name,
        out_shape=[jax.ShapeDtypeStruct(shape, dtype) for shape, dtype in outs],
        in_specs=[pl.BlockSpec(memory_space=pltpu.SMEM)] * len(place)
        + vmem(len(operands))
        + [pl.BlockSpec(memory_space=pltpu.HBM)] * len(remote)
        + [pl.BlockSpec(memory_space=pl.ANY)] * len(after),
        out_specs=vmem(len(outs)),
        scratch_shapes=[pltpu.VMEM(*x) if isinstance(x, tuple) else x for x in scratch],
        compiler_params=params(mib),
        cost_estimate=cost(flops, moved),
    )(*place, *operands, *remote, *after)


def swap(value, axis, mask):
    return lax.ppermute(value, axis, [(i, i ^ mask) for i in range(lax.axis_size(axis))])


def swap_both(value, dp_mask, tm_mask):
    recs = lax.axis_size("dp")
    count = lax.axis_size("tm") * recs
    pairs = [(i, (i // recs ^ tm_mask) * recs + (i % recs ^ dp_mask)) for i in range(count)]
    return lax.ppermute(value, ("tm", "dp"), pairs)


def on_device(frames_in, valid_frames, kernel, w_qkv, cotangent):
    record, cot = frames_in[0], cotangent[0]
    frames, width = record.shape
    span = frames + HALO
    parts, recs = lax.axis_size("tm"), lax.axis_size("dp")
    me = lax.axis_index("tm")
    begin = me * frames
    place = [
        jnp.reshape(x, (1,)).astype(jnp.int32)
        for x in (begin, valid_frames[0] - begin, me // 2, me % 2, lax.axis_index("dp"))
    ]
    split = parts == 8 and recs == 4
    both = lax.optimization_barrier(
        jnp.concatenate([record.astype(F32), cot.astype(F32), kernel], axis=0)
    )
    own = both[:frames].astype(BF16)
    last, first = own[frames - HALO :], own[:HALO]
    first_cot = both[frames : frames + HALO].astype(BF16)
    low_core = me % 2 == 0
    edge = jnp.where(low_core, last, first)
    near = swap(edge, "tm", 1)
    far = lax.ppermute(
        jnp.where(low_core, first, last),
        "tm",
        [(i, (i + 1 if i % 2 else i - 1) % parts) for i in range(parts)],
    )
    next_cot = lax.ppermute(first_cot, "tm", [(i, (i - 1) % parts) for i in range(parts)])
    if split:
        peers = [swap(own, "tm", mask) for mask in (2, 4, 6)]
    rows = frames + 2 * HALO
    hidden, conv, qkv, w_near = call(
        project_kernel,
        "project",
        [
            ((frames, width), BF16),
            ((frames + EDGE, width), F32),
            ((HALO + 2 * frames, 3 * width), BF16),
            (w_qkv.shape, BF16),
        ],
        place,
        [near, far, both],
        [
            ((rows + KERNEL - 1, width), F32),
            ((rows, width), BF16),
            pltpu.SemaphoreType.DMA((3,)),
        ],
        flops=rows * width * 3 * width * 2,
        moved=9000000,
        remote=[w_qkv],
        after=[next_cot],
        mib=OWN,
    )
    outs = [((frames, width), BF16), ((frames + EDGE, 3 * width), BF16)]
    attended, grads, *sends = call(
        attend_kernel if split else attend_alone,
        "attend",
        outs + [((4, frames, 3 * width // 4), BF16)] * split,
        place,
        [qkv, both, next_cot],
        [((frames, width), BF16)],
        mib=16,
        flops=8 * 12 * span * 128 * 128 * 2 * 8,
        moved=5000000,
    )
    if split:
        sends = sends[0]
        got = [swap(sends[slot], "tm", 2 * slot) for slot in (1, 2, 3)]
    scale = float(recs * parts * frames) ** (-0.5)
    if split:
        cols = 3 * width // 4
        shard = cols // 4
        (ends,) = call(
            ends_kernel, "ends", [((4 * EDGE, width), BF16)], place, [both, *peers], after=[grads]
        )
        (peers_hidden,) = call(
            peers_kernel,
            "peer_hidden",
            [((3 * frames, width), BF16)],
            place,
            [*peers, swap(ends, "tm", 1), both],
            [((frames + EDGE, width), F32)],
            flops=3 * frames * width * 40,
            moved=2000000,
        )
        operands = [hidden, peers_hidden, sends, *got]
        whole, half = (shard, width // 2), (shard, 2 * HEAD)
        send0, send1, keep = (
            call(
                functools.partial(weight_kernel, mine, ys),
                "weight_" + name,
                [((cols, len(ys) * 2 * HEAD), F32 if mine else BF16)],
                place,
                operands,
                mib=20,
                flops=cols * width * frames * 4,
                moved=6000000,
            )[0]
            for name, mine, ys in (("send0", False, (0,)), ("send1", False, (1,)), ("keep", True, (0, 1)))
        )
        low, high = (half, BF16), (half, F32)
        near_same, near_other, *ahead, cross_same, cross_other, own_same, own_other = call(
            core_sum_kernel,
            "core_sum",
            [low, low, high, high, low, low, high, low],
            place,
            [keep, swap(send0, "tm", 1), swap(send1, "tm", 1)],
        )
        late = [near_same]
        grad_in, done = call(
            input_grad_kernel,
            "input_grad",
            [((frames, width), BF16), ((8, 128), F32)],
            place,
            [grads, w_near, conv, both],
            [((frames + EDGE, width), F32)],
            mib=20,
            flops=(frames + EDGE) * width * 3 * width * 2,
            moved=9000000,
            after=late,
        )
        got_near = swap(near_same, "dp", 1), swap(near_other, "dp", 1)
        got_cross = swap(cross_same, "dp", 1), swap_both(cross_other, 1, 2)
        got_own = swap(own_other, "tm", 2)
        same, other = (
            call(forward_kernel, "forward_" + name, [low], place, [part, got])[0]
            for name, part, got in zip(("same", "other"), ahead, got_near)
        )
        got_sums = swap(same, "dp", 3), swap_both(other, 3, 2)
        kept, moved = [], []
        early = [got_cross[1], done]
        for i, name in enumerate(("same", "other")):
            keep, send = call(
                functools.partial(mid_sum_kernel, i == 0),
                "mid_" + name,
                [((shard, HEAD), F32), ((shard, HEAD), BF16)],
                place,
                [got_own, own_same, got_cross[i], got_sums[i]],
                after=early,
            )
            kept.append(keep)
            moved.append(swap(send, "tm", 4))
        (qkv_grad,) = call(
            functools.partial(place_kernel, scale),
            "place",
            [((3 * HEADS // 4, HEAD, HEAD), F32)],
            place,
            [*kept, *moved],
        )
    else:
        late = []
        grad_in, done = call(
            input_grad_kernel,
            "input_grad",
            [((frames, width), BF16), ((8, 128), F32)],
            place,
            [grads, w_near, conv, both],
            [((frames + EDGE, width), F32)],
            mib=20,
            flops=(frames + EDGE) * width * 3 * width * 2,
            moved=9000000,
            after=late,
        )
        partial = dot(hidden, grads[:frames], 0, 0).astype(BF16)
        by_time = lax.psum_scatter(partial, "tm", scatter_dimension=0, tiled=True)
        summed = lax.psum_scatter(by_time, "dp", scatter_dimension=1, tiled=True).astype(F32)
        qkv_grad = summed.reshape(summed.shape[0], -1, HEAD).transpose(1, 2, 0) * scale
    return (attended[None], grad_in[None], qkv_grad)


def solution(mesh):
    return jax.shard_map(
        on_device,
        mesh=mesh,
        in_specs=(P("dp", "tm", None), P("dp"), P(), P(), P("dp", "tm", None)),
        out_specs=(P("dp", "tm", None), P("dp", "tm", None), P("dp", None, "tm")),
        check_vma=False,
    )
```
